32 devices in a mesh: dp: 8 (over z, y), tensor: 4 (over x, core).
Axes of the slice: x: 2, y: 2, z: 4, core: 2. Of those that a mesh axis runs over, the one named last changes fastest.
Arguments:
- tokens: bfloat16 [32768, 384], P('dp'), may hold values from -6 to 6
- crop_ids: int32 [32768], P('dp'), may hold values from 0 to 5, as said below
- cotangent: bfloat16 [32768, 384], P('dp'), may hold values from -18 to 18
- key_tokens: bfloat16 [32768, 384], P('dp'), may hold values from -6 to 6
- entry_weight: float32 [384, 3, 384], P('dp', None, 'tensor'), may hold values from -0.15625 to 0.15625
- exit_weight: float32 [384, 384], P('tensor', 'dp'), may hold values from -2.5 to 2.5
- up_weight: float32 [384, 1536], P('dp', 'tensor'), may hold values from -0.3125 to 0.3125
- down_weight: float32 [1536, 384], P('tensor', 'dp'), may hold values from -0.15625 to 0.15625
- small_params: float32 [6, 384], P(None, 'dp'), may hold values from -1.5 to 7
- hidden_bias: float32 [1536], P(('tensor', 'dp')), may hold values from -2.5 to 2.5
- entry_first: float32 [384, 3, 384], P('dp', None, 'tensor'), may hold values from -0.00048828125 to 0.00048828125
- exit_first: float32 [384, 384], P('tensor', 'dp'), may hold values from -0.00012207031 to 0.00012207031
- up_first: float32 [384, 1536], P('dp', 'tensor'), may hold values from -0.00048828125 to 0.00048828125
- down_first: float32 [1536, 384], P('tensor', 'dp'), may hold values from -0.00048828125 to 0.00048828125
- small_first: float32 [6, 384], P(None, 'dp'), may hold values from -0.0008544922 to 0.0008544922
- hidden_first: float32 [1536], P(('tensor', 'dp')), may hold values from -0.00010681152 to 0.00010681152
- entry_second: float32 [384, 3, 384], P('dp', None, 'tensor'), may hold values from 5.639166e-10 to 2.2556663e-09
- exit_second: float32 [384, 384], P('tensor', 'dp'), may hold values from 3.3834994e-11 to 1.3533998e-10
- up_second: float32 [384, 1536], P('dp', 'tensor'), may hold values from 5.639166e-10 to 2.2556663e-09
- down_second: float32 [1536, 384], P('tensor', 'dp'), may hold values from 5.639166e-10 to 2.2556663e-09
- small_second: float32 [6, 384], P(None, 'dp'), may hold values from 1.6917496e-09 to 6.7669985e-09
- hidden_second: float32 [1536], P(('tensor', 'dp')), may hold values from 2.2556663e-11 to 9.022665e-11
- key_entry: bfloat16 [384, 3, 384], P(None, None, 'tensor'), may hold values from -0.15625 to 0.15625
- key_exit: bfloat16 [384, 384], P('tensor'), may hold values from -2.5 to 2.5
- key_up: bfloat16 [384, 1536], P(None, 'tensor'), may hold values from -0.3125 to 0.3125
- key_down: bfloat16 [1536, 384], P('tensor'), may hold values from -0.15625 to 0.15625
- key_small: bfloat16 [6, 384], replicated, may hold values from -1.5 to 7
- key_hidden: bfloat16 [1536], P('tensor'), may hold values from -2.5 to 2.5
Outputs:
- block_output: bfloat16 [32768, 384], P('dp')
- key_output: bfloat16 [32768, 384], P('dp')
- input_grad: bfloat16 [32768, 384], P('dp')
- grad_norm: float32 [], replicated
- entry_moment: float32 [384, 3, 384], P('dp', None, 'tensor')
- entry_square: float32 [384, 3, 384], P('dp', None, 'tensor')
- entry_master: float32 [384, 3, 384], P('dp', None, 'tensor')
- exit_moment: float32 [384, 384], P('tensor', 'dp')
- exit_square: float32 [384, 384], P('tensor', 'dp')
- exit_master: float32 [384, 384], P('tensor', 'dp')
- up_moment: float32 [384, 1536], P('dp', 'tensor')
- up_square: float32 [384, 1536], P('dp', 'tensor')
- up_master: float32 [384, 1536], P('dp', 'tensor')
- down_moment: float32 [1536, 384], P('tensor', 'dp')
- down_square: float32 [1536, 384], P('tensor', 'dp')
- down_master: float32 [1536, 384], P('tensor', 'dp')
- small_moment: float32 [6, 384], P(None, 'dp')
- small_square: float32 [6, 384], P(None, 'dp')
- small_master: float32 [6, 384], P(None, 'dp')
- hidden_moment: float32 [1536], P(('tensor', 'dp'))
- hidden_square: float32 [1536], P(('tensor', 'dp'))
- hidden_master: float32 [1536], P(('tensor', 'dp'))
The draws below stay inside these ranges and needn't reach their ends.
Inputs may be any that keep to these rules, and one draw needn't show every extreme that they name: `crop_ids`: each aligned block of 512 rows holds whole crops of 197 or 101 rows from its first row on, numbered 0, 1, 2 and so on in order; the rows after them carry 5 and are padding.
All inputs are finite; a program needn't handle non-finite values.
Results may differ from the reference program's by a relative error of at most 0.017.
The reference program's roundings to bfloat16 on the way count: a program that leaves them out, or rounds other values in their place, can miss the bound.
Values may be sent and summed in bfloat16 or wider, within the bound.
A program may use at most 192 MiB of HBM per device.

```python
import math
import jax
import jax.numpy as jnp
from jax import lax

D = 384
FF = 1536
HEADS = 12
HEAD_DIM = 32
PACK = 512
LONG = 197
SHORT = 101
CROPS = 5
STEP = 10
TOKENS = 32768
PARAMS = 1773312


def small_table(steep, gain_noise, bias_noise):
    ramp = jnp.linspace(0.0, 1.0, D)
    gains = (1.0 + steep * ramp)[None, :] * gain_noise
    return jnp.stack([gains[0], bias_noise[0], gains[1], bias_noise[1], bias_noise[2], bias_noise[3]])


def bias_line(slope, noise):
    ramp = jnp.linspace(0.0, 1.0, FF)
    return -1.0 + slope * ramp + noise


def draw_crop_ids(key, part):
    key = jax.random.fold_in(key, 1)
    packs = TOKENS // PACK
    pattern = jax.random.randint(key, (packs,), 0, 5)
    table = jnp.array([[LONG, LONG, SHORT, 0, 0], [SHORT, SHORT, SHORT, SHORT, SHORT], [LONG, SHORT, 0, 0, 0], [LONG, LONG, 0, 0, 0], [SHORT, SHORT, SHORT, 0, 0]], jnp.int32)
    ends = jnp.cumsum(table[pattern], axis=1)
    place = jnp.arange(PACK, dtype=jnp.int32)
    numbers = jnp.sum((place[None, :, None] >= ends[:, None, :]).astype(jnp.int32), axis=2)
    return numbers.reshape(TOKENS).astype(jnp.int32)


def draw_cotangent(key, part):
    key = jax.random.fold_in(key, 2)
    ramp = jnp.linspace(0.0, 1.0, D)
    noise = jnp.clip(jax.random.normal(key, (TOKENS, D), jnp.float32), -6.0, 6.0)
    slope = 2.0
    return (noise * (1.0 + slope * ramp)[None, :]).astype(jnp.bfloat16)


def draw_small_params(key, part):
    key = jax.random.fold_in(key, 3)
    gain_key, bias_key = jax.random.split(key)
    table = small_table(2.0, jax.random.uniform(gain_key, (2, D), jnp.float32, 0.8, 1.25), 0.3 * jnp.clip(jax.random.normal(bias_key, (4, D), jnp.float32), -5.0, 5.0))
    return table.astype(jnp.float32)


def draw_key_small(key, part):
    key = jax.random.fold_in(key, 5)
    gain_key, bias_key = jax.random.split(key)
    table = small_table(2.0, jax.random.uniform(gain_key, (2, D), jnp.float32, 0.8, 1.25), 0.3 * jnp.clip(jax.random.normal(bias_key, (4, D), jnp.float32), -5.0, 5.0))
    return table.astype(jnp.bfloat16)


def draw_hidden_bias(key, part):
    key = jax.random.fold_in(key, 4)
    line = bias_line(2.0, 0.3 * jnp.clip(jax.random.normal(key, (FF,), jnp.float32), -5.0, 5.0))
    return line.astype(jnp.float32)


def draw_key_hidden(key, part):
    key = jax.random.fold_in(key, 6)
    line = bias_line(2.0, 0.3 * jnp.clip(jax.random.normal(key, (FF,), jnp.float32), -5.0, 5.0))
    return line.astype(jnp.bfloat16)


def shard_levels(own_key, dims, cuts, least, top_value):
    def one(dim, shards_of):
        heights = jax.random.uniform(jax.random.fold_in(jax.random.fold_in(own_key, 6), dim), (shards_of,), jnp.float32, least / len(cuts), top_value / len(cuts))
        return jnp.repeat(jnp.exp(heights), dims[dim] // shards_of).reshape((-1,) + (1,) * (len(dims) - dim - 1))

    factor_of = one(*cuts[0])
    for cut in cuts[1:]:
        factor_of = factor_of * one(*cut)
    return factor_of


def normal_values(stream_key, dims, width, most, pieces=(), kind=jnp.bfloat16):
    entries = jax.random.normal(stream_key, dims, jnp.float32) * width
    if len(pieces) > 0:
        entries = shard_levels(stream_key, dims, pieces, -0.22, 0.18) * entries
    return jnp.clip(entries, min=-most, max=most).astype(kind)


def setup_inputs(seed: int = 0) -> dict:
    key_list = jax.random.split(jax.random.key(seed), 29)
    return {
        "tokens": normal_values(key_list[0], (TOKENS, D), 1.0, 6.0, ((0, 8),)),
        "crop_ids": draw_crop_ids(jax.random.fold_in(key_list[28], 71), 0),
        "cotangent": draw_cotangent(jax.random.fold_in(key_list[28], 71), 0),
        "key_tokens": normal_values(key_list[3], (TOKENS, D), 1.0, 6.0, ((0, 8),)),
        "entry_weight": normal_values(key_list[4], (D, 3, D), (4 * D) ** -0.5, 0.15625, ((0, 8), (2, 4)), jnp.float32),
        "exit_weight": normal_values(key_list[5], (D, D), (max(D // 64, 1)) ** -0.5, 2.5, ((0, 4), (1, 8)), jnp.float32),
        "up_weight": normal_values(key_list[6], (D, FF), D ** -0.5, 0.3125, ((0, 8), (1, 4)), jnp.float32),
        "down_weight": normal_values(key_list[7], (FF, D), FF ** -0.5, 0.15625, ((0, 4), (1, 8)), jnp.float32),
        "small_params": draw_small_params(jax.random.fold_in(key_list[28], 71), 0),
        "hidden_bias": draw_hidden_bias(jax.random.fold_in(key_list[28], 71), 0),
        "entry_first": normal_values(key_list[10], (D, 3, D), (0.11 / PARAMS ** 0.5), 0.00048828125, ((0, 8), (2, 4)), jnp.float32),
        "exit_first": normal_values(key_list[11], (D, D), (0.03 / PARAMS ** 0.5), 0.00012207031, ((0, 4), (1, 8)), jnp.float32),
        "up_first": normal_values(key_list[12], (D, FF), (0.11 / PARAMS ** 0.5), 0.00048828125, ((0, 8), (1, 4)), jnp.float32),
        "down_first": normal_values(key_list[13], (FF, D), (0.11 / PARAMS ** 0.5), 0.00048828125, ((0, 4), (1, 8)), jnp.float32),
        "small_first": normal_values(key_list[14], (6, D), (0.2 / PARAMS ** 0.5), 0.0008544922, ((1, 8),), jnp.float32),
        "hidden_first": normal_values(key_list[15], (FF,), (0.022 / PARAMS ** 0.5), 0.00010681152, ((0, 32),), jnp.float32),
        "entry_second": jnp.clip(jnp.exp(math.log(2.2556663203943117e-09) - 1.3862944 * jax.random.uniform(key_list[16], (D, 3, D), jnp.float32) ** shard_levels(key_list[16], (D, 3, D), ((0, 8), (2, 4)), -0.2, 0.2)), 5.639165800985779e-10, 2.2556663203943117e-09),
        "exit_second": jnp.clip(jnp.exp(math.log(1.3533997533787812e-10) - 1.3862944 * jax.random.uniform(key_list[17], (D, D), jnp.float32) ** shard_levels(key_list[17], (D, D), ((0, 4), (1, 8)), -0.2, 0.2)), 3.383499383446953e-11, 1.3533997533787812e-10),
        "up_second": jnp.clip(jnp.exp(math.log(2.2556663203943117e-09) - 1.3862944 * jax.random.uniform(key_list[18], (D, FF), jnp.float32) ** shard_levels(key_list[18], (D, FF), ((0, 8), (1, 4)), -0.2, 0.2)), 5.639165800985779e-10, 2.2556663203943117e-09),
        "down_second": jnp.clip(jnp.exp(math.log(2.2556663203943117e-09) - 1.3862944 * jax.random.uniform(key_list[19], (FF, D), jnp.float32) ** shard_levels(key_list[19], (FF, D), ((0, 4), (1, 8)), -0.2, 0.2)), 5.639165800985779e-10, 2.2556663203943117e-09),
        "small_second": jnp.clip(jnp.exp(math.log(6.766998517093725e-09) - 1.3862944 * jax.random.uniform(key_list[20], (6, D), jnp.float32) ** shard_levels(key_list[20], (6, D), ((1, 8),), -0.2, 0.2)), 1.6917496292734313e-09, 6.766998517093725e-09),
        "hidden_second": jnp.clip(jnp.exp(math.log(9.022665253821671e-11) - 1.3862944 * jax.random.uniform(key_list[21], (FF,), jnp.float32) ** shard_levels(key_list[21], (FF,), ((0, 32),), -0.2, 0.2)), 2.2556663134554178e-11, 9.022665253821671e-11),
        "key_entry": normal_values(key_list[22], (D, 3, D), (4 * D) ** -0.5, 0.15625, ((2, 4),)),
        "key_exit": normal_values(key_list[23], (D, D), (max(D // 64, 1)) ** -0.5, 2.5, ((0, 4),)),
        "key_up": normal_values(key_list[24], (D, FF), D ** -0.5, 0.3125, ((1, 4),)),
        "key_down": normal_values(key_list[25], (FF, D), FF ** -0.5, 0.15625, ((0, 4),)),
        "key_small": draw_key_small(jax.random.fold_in(key_list[28], 71), 0),
        "key_hidden": draw_key_hidden(jax.random.fold_in(key_list[28], 71), 0),
    }


LN_EPS = 1e-06
CLIP = 1.0
RATE_MATRIX = 0.03
RATE_EXIT = 0.2
RATE_SMALL = 0.5
RATE_BIAS = 0.3
BETA_ONE = 0.9
BETA_TWO = 0.999
ADAM_EPS = 1e-08
DECAY = 0.05
MASKED = -1e+30

@jax.custom_vjp
def low(v):
    return lax.optimization_barrier(v.astype(jnp.bfloat16)).astype(jnp.float32)

@jax.custom_vjp
def low_back(v):
    return v

def low_keep(v):
    return (low(v), None)

def low_pass(kept, grad):
    return (grad,)

def back_keep(v):
    return (v, None)

def back_low(kept, grad):
    return (low(grad),)
low.defvjp(low_keep, low_pass)
low_back.defvjp(back_keep, back_low)

def matmul(left, right):
    return jnp.dot(left, right, precision=lax.Precision.HIGHEST, preferred_element_type=jnp.float32)

def normalize(values, gain, shift):
    mean = lax.optimization_barrier(jnp.mean(values, axis=1, keepdims=True))
    centred = values - mean
    spread = lax.optimization_barrier(jnp.mean(centred * centred, axis=1, keepdims=True))
    return centred * lax.rsqrt(spread + LN_EPS) * gain + shift

def attend(item):
    packed, segment = item
    query = packed[:, 0]
    keys = packed[:, 1]
    values = packed[:, 2]
    scores = jnp.einsum('qhd,khd->hqk', query, keys, precision=lax.Precision.HIGHEST) * HEAD_DIM ** (-0.5)
    scores = low_back(scores)
    same = segment[:, None] == segment[None, :]
    scores = jnp.where(same[None], scores, MASKED)
    probs = low(jax.nn.softmax(scores, axis=-1))
    return jnp.einsum('hqk,khd->qhd', probs, values, precision=lax.Precision.HIGHEST)

def block(inputs, segments, entry_master, exit_master, upper_master, lower_master, small_master, bias_master):
    entry_work = low(entry_master)
    exit_work = low(exit_master)
    upper_work = low(upper_master)
    lower_work = low(lower_master)
    small_work = low(small_master)
    bias_work = low(bias_master)
    first_norm = low(normalize(inputs, small_work[0], small_work[1]))
    packed = low_back(low(matmul(first_norm, entry_work.reshape(D, 3 * D))))
    packed = packed.reshape(-1, PACK, 3, HEADS, HEAD_DIM)
    attended = lax.map(jax.checkpoint(attend), (packed, segments.reshape(-1, PACK)))
    attended = low_back(low(attended.reshape(-1, D)))
    middle = inputs + low_back(matmul(attended, exit_work)) + small_work[4]
    second_norm = low(normalize(middle, small_work[2], small_work[3]))
    preact = low_back(matmul(second_norm, upper_work) + bias_work)
    activated = low(jax.nn.gelu(preact, approximate=False))
    return middle + low_back(matmul(activated, lower_work)) + small_work[5]

def adamw(grad, first, second, master, decay, rate):
    moment = BETA_ONE * first + (1.0 - BETA_ONE) * grad
    square = BETA_TWO * second + (1.0 - BETA_TWO) * grad * grad
    ahead = moment / (1.0 - BETA_ONE ** STEP)
    spread = square / (1.0 - BETA_TWO ** STEP)
    return (moment, square, master - rate * (ahead / (jnp.sqrt(spread) + ADAM_EPS) + decay * master))

def reference(tokens, crop_ids, cotangent, key_tokens, entry_weight, exit_weight, up_weight, down_weight, small_params, hidden_bias, entry_first, exit_first, up_first, down_first, small_first, hidden_first, entry_second, exit_second, up_second, down_second, small_second, hidden_second, key_entry, key_exit, key_up, key_down, key_small, key_hidden):
    valid = (crop_ids < CROPS).astype(jnp.float32)[:, None]
    inputs = tokens.astype(jnp.float32)
    masters = (entry_weight, exit_weight, up_weight, down_weight, small_params, hidden_bias)

    def run(values, params):
        return block(values, crop_ids, params[0], params[1], params[2], params[3], params[4], params[5])
    output, pull = jax.vjp(run, inputs, masters)
    grad_inputs, grads = pull(cotangent.astype(jnp.float32) * valid)
    key_result = block(key_tokens.astype(jnp.float32), crop_ids, key_entry.astype(jnp.float32), key_exit.astype(jnp.float32), key_up.astype(jnp.float32), key_down.astype(jnp.float32), key_small.astype(jnp.float32), key_hidden.astype(jnp.float32))
    squares = jnp.sum(grads[0] * grads[0])
    for grad in (grads[1], grads[2], grads[3], grads[4], grads[5]):
        squares = squares + jnp.sum(grad * grad)
    norm_value = jnp.sqrt(squares)
    factor = CLIP / jnp.maximum(norm_value, CLIP)
    entry_new = adamw(grads[0] * factor, entry_first, entry_second, entry_weight, DECAY, RATE_MATRIX)
    exit_new = adamw(grads[1] * factor, exit_first, exit_second, exit_weight, DECAY, RATE_EXIT)
    upper_new = adamw(grads[2] * factor, up_first, up_second, up_weight, DECAY, RATE_MATRIX)
    lower_new = adamw(grads[3] * factor, down_first, down_second, down_weight, DECAY, RATE_MATRIX)
    small_new = adamw(grads[4] * factor, small_first, small_second, small_params, 0.0, RATE_SMALL)
    bias_new = adamw(grads[5] * factor, hidden_first, hidden_second, hidden_bias, 0.0, RATE_BIAS)
    return (output.astype(jnp.bfloat16), key_result.astype(jnp.bfloat16), grad_inputs.astype(jnp.bfloat16), norm_value, entry_new[0], entry_new[1], entry_new[2], exit_new[0], exit_new[1], exit_new[2], upper_new[0], upper_new[1], upper_new[2], lower_new[0], lower_new[1], lower_new[2], small_new[0], small_new[1], small_new[2], bias_new[0], bias_new[1], bias_new[2])
```

```python
import math
from functools import partial

import jax
import jax.numpy as jnp
from jax import lax
from jax.experimental import pallas as pl
from jax.experimental.pallas import tpu as pltpu
from jax.sharding import PartitionSpec as P

HEAD_DIM = 32
PACK = 512
CROPS = 5
STEP = 10
LN_EPS = 1e-06
CLIP = 1.0
RATE_MATRIX = 0.03
RATE_EXIT = 0.2
RATE_SMALL = 0.5
RATE_BIAS = 0.3
BETA_ONE = 0.9
BETA_TWO = 0.999
ADAM_EPS = 1e-08
DECAY = 0.05
MASKED = -1e30

SCALE = HEAD_DIM ** (-0.5)
EXP_SCALE = SCALE * math.log2(math.e)
LANES = 128
HEADS_HERE = 3
USED = HEADS_HERE * HEAD_DIM
ONES = USED + CROPS + 1
ATT = 4 * LANES
SMALL_AT = USED
HIDDEN_AT = USED + 6
MESH = pl.DeviceIdType.MESH
BF = jnp.bfloat16
F32 = jnp.float32
VMEM = pltpu.VMEM
NT = (((1,), (1,)), ((), ()))
TN = (((0,), (0,)), ((), ()))

TAIL_AT = 0.305
TAIL = (
    0.12163973599672318,
    0.12246678024530411,
    0.10342107713222504,
    0.12102094292640686,
    -0.03797539696097374,
    0.18571528792381287,
    -0.15298734605312347,
    0.036698948591947556,
)


def mm(left, right):
    return jnp.dot(left, right, preferred_element_type=F32)


def mm_nt(left, right):
    return lax.dot_general(left, right, NT, preferred_element_type=F32)


def norm_parts(values):
    mean = jnp.mean(values, axis=1, keepdims=True)
    centred = values - mean
    spread = jnp.mean(centred * centred, axis=1, keepdims=True)
    scale = lax.rsqrt(spread + LN_EPS)
    return (centred * scale, scale)


def norm_back(grad, unit, scale, gain):
    scaled = grad * gain
    first = jnp.mean(scaled, axis=1, keepdims=True)
    second = jnp.mean(scaled * unit, axis=1, keepdims=True)
    return scale * (scaled - first - unit * second)


def tail_parts(pre):
    size = jnp.abs(pre)
    base = 1.0 + TAIL_AT * size
    part = pl.reciprocal(base, approx=True)
    part = part * (2.0 - base * part)
    poly = TAIL[7]
    for k in range(6, -1, -1):
        poly = poly * part + TAIL[k]
    bell = jnp.exp(-0.5 * pre * pre)
    tail = poly * part * bell
    return (jnp.where(pre < 0.0, tail, 1.0 - tail), bell)


def small_rows(w_ref):
    rows = w_ref[0, :, 0:LANES].astype(F32).T
    return rows[SMALL_AT : SMALL_AT + 6]


def hidden_row(w_ref, t):
    return w_ref[t, :, 0:LANES].astype(F32).T[HIDDEN_AT : HIDDEN_AT + 1]


def id_lanes(ids):
    place = lax.broadcasted_iota(jnp.int32, (LANES, PACK), 0)
    match = (place - USED) == ids
    ones = (place >= ONES) & (place < ONES + 3)
    key_side = jnp.where(match | ones, 1.0, 0.0).T
    crop = (place >= USED) & (place < ONES)
    query_side = jnp.where(crop & jnp.logical_not(match), MASKED, 0.0).astype(BF)
    return (key_side, query_side)


def attention(qkv_ref, a_ref, lse_ref, base, query_side, groups):
    place = lax.broadcasted_iota(jnp.int32, (LANES, PACK), 0) // HEAD_DIM
    ones = jnp.ones((16, PACK), BF)
    blank = jnp.zeros((LANES - USED, PACK), F32)
    rows = pl.ds(base, PACK)
    for g in range(groups):
        at = g * 3 * LANES
        query = qkv_ref[rows, at : at + LANES].T
        keys = qkv_ref[rows, at + LANES : at + 2 * LANES]
        values = qkv_ref[rows, at + 2 * LANES : at + 3 * LANES].T
        outs = []
        for h in range(HEADS_HERE):
            scores = mm(keys, jnp.where(place == h, query, query_side))
            top = jnp.max(scores, axis=0, keepdims=True)
            probs = jnp.exp2((scores - top) * EXP_SCALE).astype(BF)
            mix = jnp.concatenate([values[h * HEAD_DIM : (h + 1) * HEAD_DIM], ones], axis=0)
            mixed = mm(mix, probs)
            total = mixed[HEAD_DIM : HEAD_DIM + 1]
            outs.append(mixed[:HEAD_DIM] * (1.0 / total))
            if lse_ref is not None:
                line = g * HEADS_HERE + h
                lse_ref[line : line + 1, rows] = top + jnp.log(total) * (1.0 / SCALE)
        a_ref[rows, g * LANES : (g + 1) * LANES] = (
            jnp.concatenate(outs + [blank], axis=0).T.astype(BF)
        )


def forward_front(x_ref, ids_ref, w_ref, small, qkv_ref, a_ref, h1_ref, x1_ref, lse_ref, base, pack):
    groups = w_ref.shape[0]
    rows = pl.ds(base, PACK)
    values = x_ref[rows, :].astype(F32)
    unit, _ = norm_parts(values)
    first = (unit * small[0:1] + small[1:2]).astype(BF)
    if h1_ref is not None:
        h1_ref[rows, :] = first
    key_side, query_side = id_lanes(ids_ref[pack])
    for g in range(groups):
        at = g * 3 * LANES
        qkv_ref[rows, at : at + LANES] = mm(first, w_ref[g, :, 0:LANES]).astype(BF)
        packed = mm(first, w_ref[g, :, LANES : 3 * LANES])
        qkv_ref[rows, at + LANES : at + 2 * LANES] = (packed[:, :LANES] + key_side).astype(BF)
        qkv_ref[rows, at + 2 * LANES : at + 3 * LANES] = (packed[:, LANES:] + key_side).astype(BF)
    attention(qkv_ref, a_ref, lse_ref, base, query_side, groups)
    branch = mm_nt(a_ref[rows, 0:LANES], w_ref[0, :, 3 * LANES : 4 * LANES])
    for g in range(1, groups):
        branch += mm_nt(
            a_ref[rows, g * LANES : (g + 1) * LANES], w_ref[g, :, 3 * LANES : 4 * LANES]
        )
    x1_ref[rows, :] = x_ref[rows, :].astype(F32) + branch + small[4:5]


def ffn_tile(w_ref, j):
    depth = w_ref.shape[1]
    per = depth // LANES
    up, down = [], []
    for b in (2 * j, 2 * j + 1):
        t, o = b // per, (b % per) * LANES
        up.append(w_ref[t, :, ATT + o : ATT + o + LANES])
        down.append(w_ref[t, :, ATT + depth + o : ATT + depth + o + LANES])
    return (jnp.concatenate(up, axis=1), jnp.concatenate(down, axis=1))


def key_kernel(place_ref, x_ref, ids_ref, w_ref, out_ref, qkv_ref, a_ref, x1_ref, h2_ref, bias_ref):
    rows_here, depth = x_ref.shape
    small = small_rows(w_ref)
    for t in range(w_ref.shape[0]):
        bias_ref[:, t * depth : (t + 1) * depth] = hidden_row(w_ref, t)

    @pl.loop(0, rows_here // PACK)
    def _(pack):
        base = pl.multiple_of(pack * PACK, PACK)
        forward_front(x_ref, ids_ref, w_ref, small, qkv_ref, a_ref, None, x1_ref, None, base, pack)
        rows = pl.ds(base, PACK)
        unit, _ = norm_parts(x1_ref[rows, :])
        h2_ref[rows, :] = (unit * small[2:3] + small[3:4]).astype(BF)

    tiles = w_ref.shape[0] * depth // (2 * LANES)
    step = 256

    @pl.loop(0, rows_here // step)
    def _(r):
        rows = pl.ds(pl.multiple_of(r * step, step), step)
        second = h2_ref[rows, :]
        total = x1_ref[rows, :] + small[5:6]
        for j in range(tiles):
            up, down = ffn_tile(w_ref, j)
            pre = mm(second, up) + bias_ref[:, j * 256 : (j + 1) * 256]
            acts = []
            for i in range(0, step, 64):
                piece = pre[i : i + 64]
                phi, _ = tail_parts(piece)
                acts.append((piece * phi).astype(BF))
            total += mm_nt(jnp.concatenate(acts, axis=0), down)
        out_ref[rows, :] = total.astype(BF)


def query_kernel(
    place_ref,
    x_ref,
    cot_ref,
    ids_ref,
    w_ref,
    out_ref,
    qkv_ref,
    a_ref,
    lse_ref,
    h1_ref,
    dx1_ref,
    grad_ref,
    line_ref,
    hidden_ref,
    x1_ref,
    h2_ref,
    h2t_ref,
    eb_ref,
    ebt_ref,
    act_ref,
    dpre_ref,
    dh2_ref,
    bias_ref,
):
    rows_here, depth = x_ref.shape
    groups = w_ref.shape[0]
    small = small_rows(w_ref)
    for t in range(groups):
        bias_ref[:, t * depth : (t + 1) * depth] = hidden_row(w_ref, t)

    lse_ref[...] = jnp.zeros_like(lse_ref)
    h2t_ref[depth:, :] = jnp.ones((h2t_ref.shape[0] - depth, rows_here), BF)

    @pl.loop(0, rows_here // PACK)
    def _(pack):
        base = pl.multiple_of(pack * PACK, PACK)
        forward_front(
            x_ref, ids_ref, w_ref, small, qkv_ref, a_ref, h1_ref, x1_ref, lse_ref, base, pack
        )
        rows = pl.ds(base, PACK)
        unit, _ = norm_parts(x1_ref[rows, :])
        second = (unit * small[2:3] + small[3:4]).astype(BF)
        h2_ref[rows, :] = second
        h2t_ref[0:depth, rows] = second.T
        valid = jnp.where(ids_ref[pack] < CROPS, 1.0, 0.0)
        valid = jnp.broadcast_to(valid, (LANES, PACK)).T[:, 0:1]
        low = (cot_ref[rows, :].astype(F32) * valid).astype(BF)
        eb_ref[rows, :] = low
        ebt_ref[:, rows] = low.T

    tiles = groups * depth // (2 * LANES)
    step = 256
    chunks = rows_here // step
    per = depth // LANES
    for j in range(tiles):
        up, down = ffn_tile(w_ref, j)
        bias = bias_ref[:, j * 256 : (j + 1) * 256]
        for r in range(chunks):
            rows = slice(r * step, (r + 1) * step)
            pre = mm(h2_ref[rows, :], up) + bias
            da = mm(eb_ref[rows, :], down)
            acts, dps = [], []
            for i in range(0, step, 64):
                piece = pre[i : i + 64]
                phi, bell = tail_parts(piece)
                acts.append((piece * phi).astype(BF))
                slope = phi + piece * (bell * (1.0 / math.sqrt(2.0 * math.pi)))
                dps.append((da[i : i + 64] * slope).astype(BF))
            act = jnp.concatenate(acts, axis=0)
            dpre = jnp.concatenate(dps, axis=0)
            act_ref[rows, :] = act
            dpre_ref[rows, :] = dpre
            if j == 0:
                x1_now = x1_ref[rows, :] + small[5:6]
                qsum = x1_now + mm_nt(act, down)
                dsum = mm_nt(dpre, up)
            else:
                qsum = dh2_ref[0, rows, :] + mm_nt(act, down)
                dsum = dh2_ref[1, rows, :] + mm_nt(dpre, up)
            dh2_ref[0, rows, :] = qsum
            dh2_ref[1, rows, :] = dsum
        gup = mm(h2t_ref[...], dpre_ref[...])
        gdown = mm(ebt_ref[...], act_ref[...])
        for k, b in enumerate((2 * j, 2 * j + 1)):
            t, o = b // per, (b % per) * LANES
            grad_ref[t, :, o : o + LANES] = gup[:depth, k * LANES : (k + 1) * LANES].astype(BF)
            grad_ref[t, :, depth + o : depth + o + LANES] = gdown[
                :, k * LANES : (k + 1) * LANES
            ].astype(BF)
            hidden_ref[t : t + 1, o : o + LANES] = gup[
                depth : depth + 1, k * LANES : (k + 1) * LANES
            ]

    out_ref[...] = dh2_ref[0].astype(BF)

    line_ref[...] = jnp.zeros_like(line_ref)

    @pl.loop(0, rows_here // PACK)
    def _(pack):
        rows = pl.ds(pl.multiple_of(pack * PACK, PACK), PACK)
        unit, scale = norm_parts(x1_ref[rows, :])
        grad = dh2_ref[1, rows, :]
        valid = jnp.where(ids_ref[pack] < CROPS, 1.0, 0.0)
        valid = jnp.broadcast_to(valid, (LANES, PACK)).T[:, 0:1]
        wide = cot_ref[rows, :].astype(F32) * valid
        dx1 = wide + norm_back(grad, unit, scale, small[2:3])
        dx1_ref[rows, :] = dx1
        line_ref[2:3, :] += jnp.sum(grad * unit, axis=0, keepdims=True)
        line_ref[3:4, :] += jnp.sum(grad, axis=0, keepdims=True)
        line_ref[4:5, :] += jnp.sum(dx1, axis=0, keepdims=True)
        line_ref[5:6, :] += jnp.sum(wide, axis=0, keepdims=True)


def attention_back(qkv_ref, a_ref, lse_ref, da_ref, dqkv_ref, base, query_side, groups):
    place = lax.broadcasted_iota(jnp.int32, (LANES, PACK), 0)
    head_of = place // HEAD_DIM
    lane = lax.broadcasted_iota(jnp.int32, (PACK, LANES), 1) // HEAD_DIM
    rows = pl.ds(base, PACK)
    none = jnp.zeros((PACK, LANES), BF)

    def split(line):
        high = line.astype(BF).astype(F32)
        rest = line - high
        middle = rest.astype(BF).astype(F32)
        low = rest - middle
        block = jnp.where(
            place == ONES,
            high,
            jnp.where(place == ONES + 1, middle, jnp.where(place == ONES + 2, low, 0.0)),
        )
        return block.astype(BF)

    for g in range(groups):
        at = g * 3 * LANES
        query = qkv_ref[rows, at : at + LANES]
        keys = qkv_ref[rows, at + LANES : at + 2 * LANES]
        values = qkv_ref[rows, at + 2 * LANES : at + 3 * LANES]
        grad = da_ref[rows, g * LANES : (g + 1) * LANES]
        query_t, keys_t, grad_t = query.T, keys.T, grad.T
        both = a_ref[rows, g * LANES : (g + 1) * LANES].T.astype(F32) * grad_t.astype(F32)
        dq, dk, dv = [], None, None
        for h in range(HEADS_HERE):
            part = slice(h * HEAD_DIM, (h + 1) * HEAD_DIM)
            line = g * HEADS_HERE + h
            lse = lse_ref[line : line + 1, rows]
            side = jnp.where(place < ONES, query_side, split(-lse))
            scores = mm(keys, jnp.where(head_of == h, query_t, side))
            probs = jnp.exp2(scores * EXP_SCALE)
            inner = jnp.sum(both[part], axis=0, keepdims=True)
            pull = mm(values, jnp.where(head_of == h, grad_t, split(-inner)))
            low = probs.astype(BF)
            dscores = (probs * pull).astype(BF)
            dv_h = mm(low, jnp.where(lane == h, grad, none))
            dk_h = mm(dscores, jnp.where(lane == h, query, none))
            dv = dv_h if dv is None else dv + dv_h
            dk = dk_h if dk is None else dk + dk_h
            dq.append(mm(keys_t[part], dscores))
        dq.append(jnp.zeros((LANES - USED, PACK), F32))
        dqkv_ref[rows, at : at + LANES] = (jnp.concatenate(dq, axis=0).T * SCALE).astype(BF)
        dqkv_ref[rows, at + LANES : at + 2 * LANES] = (dk * SCALE).astype(BF)
        dqkv_ref[rows, at + 2 * LANES : at + 3 * LANES] = dv.astype(BF)


def back_kernel(
    place_ref,
    x_ref,
    ids_ref,
    w_ref,
    qkv_ref,
    a_ref,
    lse_ref,
    h1_ref,
    dx1_ref,
    line_ref,
    hidden_ref,
    out_ref,
    grad_ref,
    da_ref,
    dqkv_ref,
    h1t_ref,
    dybt_ref,
    sums_ref,
):
    rows_here, depth = x_ref.shape
    groups = w_ref.shape[0]
    small = small_rows(w_ref)
    sums_ref[...] = jnp.zeros_like(sums_ref)
    sums_ref[SMALL_AT : SMALL_AT + 8, :] = line_ref[...]

    @pl.loop(0, rows_here // PACK)
    def _(pack):
        base = pl.multiple_of(pack * PACK, PACK)
        rows = pl.ds(base, PACK)
        _, query_side = id_lanes(ids_ref[pack])
        low = dx1_ref[rows, :].astype(BF)
        dybt_ref[:, rows] = low.T
        h1t_ref[:, rows] = h1_ref[rows, :].T
        for g in range(groups):
            da_ref[rows, g * LANES : (g + 1) * LANES] = mm(
                low, w_ref[g, :, 3 * LANES : 4 * LANES]
            ).astype(BF)
        attention_back(qkv_ref, a_ref, lse_ref, da_ref, dqkv_ref, base, query_side, groups)
        width = 3 * LANES
        grad = mm_nt(dqkv_ref[rows, 0:width], w_ref[0, :, 0:width])
        for g in range(1, groups):
            grad += mm_nt(dqkv_ref[rows, g * width : (g + 1) * width], w_ref[g, :, 0:width])
        unit, scale = norm_parts(x_ref[rows, :].astype(F32))
        back = norm_back(grad, unit, scale, small[0:1])
        out_ref[rows, :] = (dx1_ref[rows, :] + back).astype(BF)
        sums_ref[SMALL_AT : SMALL_AT + 1, :] += jnp.sum(grad * unit, axis=0, keepdims=True)
        sums_ref[SMALL_AT + 1 : SMALL_AT + 2, :] += jnp.sum(grad, axis=0, keepdims=True)

    lane = lax.broadcasted_iota(jnp.int32, (depth, LANES), 1)
    for g in range(groups):
        width = 3 * LANES
        sums_ref[HIDDEN_AT : HIDDEN_AT + 1, :] = hidden_ref[g : g + 1, :]
        extra = sums_ref[...].T
        entry = mm(h1t_ref[...], dqkv_ref[:, g * width : (g + 1) * width])
        grad_ref[g, :, 0:LANES] = jnp.where(lane < USED, entry[:, :LANES], extra).astype(BF)
        grad_ref[g, :, LANES:width] = entry[:, LANES:].astype(BF)
        grad_ref[g, :, width : width + LANES] = mm(
            dybt_ref[...], a_ref[:, g * LANES : (g + 1) * LANES]
        ).astype(BF)


def params():
    return pltpu.CompilerParams(vmem_limit_bytes=60 * 2**20)


def whole(shape):
    return pl.BlockSpec(shape, lambda i, place: (0,) * len(shape))


def own_rows(rows, depth):
    return pl.BlockSpec((rows, depth), lambda i, place: (place[0], 0))


def own_ids(packs):
    return pl.BlockSpec((packs, 1, PACK), lambda i, place: (place[0], 0, 0))


def run_key(place, tokens, ids, weights, rows):
    depth = tokens.shape[1]
    groups, _, width = weights.shape
    return pl.pallas_call(
        key_kernel,
        grid_spec=pltpu.PrefetchScalarGridSpec(
            num_scalar_prefetch=1,
            grid=(1,),
            in_specs=[own_rows(rows, depth), own_ids(rows // PACK), whole(weights.shape)],
            out_specs=whole((rows, depth)),
            scratch_shapes=[
                VMEM((rows, groups * 3 * LANES), BF),
                VMEM((rows, groups * LANES), BF),
                VMEM((rows, depth), F32),
                VMEM((rows, depth), BF),
                VMEM((1, groups * depth), F32),
            ],
        ),
        out_shape=jax.ShapeDtypeStruct((rows, depth), BF),
        compiler_params=params(),
        name="key_block",
    )(place, tokens, ids, weights)


def run_query(place, tokens, cotangent, ids, weights, rows):
    depth = tokens.shape[1]
    groups = weights.shape[0]
    outs = [
        ((rows, depth), BF),
        ((rows, groups * 3 * LANES), BF),
        ((rows, groups * LANES), BF),
        ((16, rows), F32),
        ((rows, depth), BF),
        ((rows, depth), F32),
        ((groups, depth, 2 * depth), BF),
        ((8, depth), F32),
        ((groups, depth), F32),
    ]
    return pl.pallas_call(
        query_kernel,
        grid_spec=pltpu.PrefetchScalarGridSpec(
            num_scalar_prefetch=1,
            grid=(1,),
            in_specs=[
                own_rows(rows, depth),
                own_rows(rows, depth),
                own_ids(rows // PACK),
                whole(weights.shape),
            ],
            out_specs=[whole(shape) for shape, _ in outs],
            scratch_shapes=[
                VMEM((rows, depth), F32),
                VMEM((rows, depth), BF),
                VMEM((depth + 16, rows), BF),
                VMEM((rows, depth), BF),
                VMEM((depth, rows), BF),
                VMEM((rows, 2 * LANES), BF),
                VMEM((rows, 2 * LANES), BF),
                VMEM((2, rows, depth), F32),
                VMEM((1, groups * depth), F32),
            ],
        ),
        out_shape=[jax.ShapeDtypeStruct(shape, kind) for shape, kind in outs],
        compiler_params=params(),
        name="query_block",
    )(place, tokens, cotangent, ids, weights)


def run_back(place, tokens, ids, weights, kept, rows):
    depth = tokens.shape[1]
    groups = weights.shape[0]
    return pl.pallas_call(
        back_kernel,
        grid_spec=pltpu.PrefetchScalarGridSpec(
            num_scalar_prefetch=1,
            grid=(1,),
            in_specs=[own_rows(rows, depth), own_ids(rows // PACK), whole((groups, depth, ATT))]
            + [whole(item.shape) for item in kept],
            out_specs=[whole((rows, depth)), whole((groups, depth, ATT))],
            scratch_shapes=[
                VMEM((rows, groups * LANES), BF),
                VMEM((rows, groups * 3 * LANES), BF),
                VMEM((depth, rows), BF),
                VMEM((depth, rows), BF),
                VMEM((LANES, depth), F32),
            ],
        ),
        out_shape=[
            jax.ShapeDtypeStruct((rows, depth), BF),
            jax.ShapeDtypeStruct((groups, depth, ATT), BF),
        ],
        compiler_params=params(),
        name="back_block",
    )(place, tokens, ids, weights, *kept)


def pack_piece(entry, leave, up, down, small, hidden):
    def fill(block, *extra):
        block = jnp.concatenate([block] + [item.astype(block.dtype) for item in extra], axis=1)
        return jnp.pad(block, ((0, 0), (0, LANES - block.shape[1])))

    parts = [
        fill(entry[:, 0], small.T, hidden[:, None]),
        fill(entry[:, 1]),
        fill(entry[:, 2]),
        fill(leave.T),
        up,
        down.T,
    ]
    return jnp.concatenate([part.astype(BF) for part in parts], axis=1)


def unpack_piece(piece, depth):
    entry = jnp.stack([piece[:, k * LANES : k * LANES + USED] for k in range(3)], axis=1)
    leave = piece[:, 3 * LANES : 3 * LANES + USED].T
    up = piece[:, ATT : ATT + depth]
    down = piece[:, ATT + depth :].T
    small = piece[:, SMALL_AT : SMALL_AT + 6].T
    return (entry, leave, up, down, small, piece[:, HIDDEN_AT])


def adamw(grad, first, second, master, decay, rate):
    moment = BETA_ONE * first + (1.0 - BETA_ONE) * grad
    square = BETA_TWO * second + (1.0 - BETA_TWO) * grad * grad
    ahead = moment / (1.0 - BETA_ONE**STEP)
    spread = square / (1.0 - BETA_TWO**STEP)
    return (
        moment,
        square,
        master - rate * (ahead / (jnp.sqrt(spread) + ADAM_EPS) + decay * master),
    )


DECAYS = (DECAY, DECAY, DECAY, DECAY, 0.0, 0.0)
RATES = (RATE_MATRIX, RATE_EXIT, RATE_MATRIX, RATE_MATRIX, RATE_SMALL, RATE_BIAS)


def finish_plain(grad_att, grad_ffn, masters, firsts, seconds):
    depth = grad_att.shape[1]
    grads = jnp.concatenate([grad_att, grad_ffn], axis=2).astype(F32)
    own = lax.psum_scatter(grads, "tensor", scatter_dimension=0, tiled=False)
    own = lax.psum_scatter(own, "dp", scatter_dimension=0, tiled=True)
    shares = unpack_piece(own, depth)
    copies = float(lax.axis_size("tensor"))
    total = jnp.sum(shares[4] * shares[4]) / copies
    for k in (0, 1, 2, 3, 5):
        total = total + jnp.sum(shares[k] * shares[k])
    norm_value = jnp.sqrt(lax.psum(total, ("dp", "tensor")))
    factor = CLIP / jnp.maximum(norm_value, CLIP)
    outs = []
    for k in range(6):
        outs.extend(
            adamw(shares[k] * factor, firsts[k], seconds[k], masters[k], DECAYS[k], RATES[k])
        )
    return (norm_value, outs)


def on_device(*args):
    tokens, crop_ids, cotangent, key_tokens = args[:4]
    masters, firsts, seconds, keys = args[4:10], args[10:16], args[16:22], args[22:28]
    rows = tokens.shape[0] // lax.axis_size("tensor")
    place = lax.axis_index("tensor").astype(jnp.int32)[None]
    ids = crop_ids.reshape(-1, 1, PACK)
    key_weights = lax.all_gather(pack_piece(*keys), "tensor", axis=0)
    piece = pack_piece(*masters)
    weights = lax.all_gather(lax.all_gather(piece, "dp", axis=0, tiled=True), "tensor", axis=0)
    key_rows = run_key(place, key_tokens, ids, key_weights, rows)
    key_out = lax.all_gather(key_rows, "tensor", axis=0, tiled=True)
    forward = run_query(place, tokens, cotangent, ids, weights, rows)
    block_out = lax.all_gather(forward[0], "tensor", axis=0, tiled=True)
    qkv, a, lse, h1, dx1, grad_ffn, lines, hidden = forward[1:]
    grad_rows, grad_att = run_back(
        place, tokens, ids, weights, (qkv, a, lse, h1, dx1, lines, hidden), rows
    )
    input_grad = lax.all_gather(grad_rows, "tensor", axis=0, tiled=True)
    norm_value, outs = finish_plain(grad_att, grad_ffn, masters, firsts, seconds)
    return (block_out, key_out, input_grad, norm_value, *outs)


def solution(mesh):
    rows, line = P("dp", None), P("dp")
    entry, leave, up, down = P("dp", None, "tensor"), P("tensor", "dp"), P("dp", "tensor"), P("tensor", "dp")
    state = (entry, leave, up, down, P(None, "dp"), P(("tensor", "dp")))
    keys = (P(None, None, "tensor"), P("tensor", None), P(None, "tensor"), P("tensor", None), P(), P("tensor"))
    outs = tuple(spec for spec in state for _ in range(3))
    return jax.shard_map(
        on_device,
        mesh=mesh,
        in_specs=(rows, line, rows, rows) + state * 3 + keys,
        out_specs=(rows, rows, rows, P()) + outs,
        check_vma=False,
    )
```

```python
import math
from functools import partial

import jax
import jax.numpy as jnp
from jax import lax
from jax.experimental import pallas as pl
from jax.experimental.pallas import tpu as pltpu
from jax.sharding import PartitionSpec as P

HEAD_DIM = 32
PACK = 512
CROPS = 5
STEP = 10
LN_EPS = 1e-06
CLIP = 1.0
RATE_MATRIX = 0.03
RATE_EXIT = 0.2
RATE_SMALL = 0.5
RATE_BIAS = 0.3
BETA_ONE = 0.9
BETA_TWO = 0.999
ADAM_EPS = 1e-08
DECAY = 0.05
MASKED = -1e30

SCALE = HEAD_DIM ** (-0.5)
EXP_SCALE = SCALE * math.log2(math.e)
LANES = 128
HEADS_HERE = 3
USED = HEADS_HERE * HEAD_DIM
ONES = USED + CROPS + 1
ATT = 4 * LANES
SMALL_AT = USED
HIDDEN_AT = USED + 6
MESH = pl.DeviceIdType.MESH
BF = jnp.bfloat16
F32 = jnp.float32
VMEM = pltpu.VMEM
NT = (((1,), (1,)), ((), ()))
TN = (((0,), (0,)), ((), ()))

TAIL_AT = 0.305
TAIL = (
    0.12163973599672318,
    0.12246678024530411,
    0.10342107713222504,
    0.12102094292640686,
    -0.03797539696097374,
    0.18571528792381287,
    -0.15298734605312347,
    0.036698948591947556,
)


def mm(left, right):
    return jnp.dot(left, right, preferred_element_type=F32)


def mm_nt(left, right):
    return lax.dot_general(left, right, NT, preferred_element_type=F32)


def norm_parts(values):
    mean = jnp.mean(values, axis=1, keepdims=True)
    centred = values - mean
    spread = jnp.mean(centred * centred, axis=1, keepdims=True)
    scale = lax.rsqrt(spread + LN_EPS)
    return (centred * scale, scale)


def norm_back(grad, unit, scale, gain):
    scaled = grad * gain
    first = jnp.mean(scaled, axis=1, keepdims=True)
    second = jnp.mean(scaled * unit, axis=1, keepdims=True)
    return scale * (scaled - first - unit * second)


def tail_parts(pre):
    size = jnp.abs(pre)
    base = 1.0 + TAIL_AT * size
    part = pl.reciprocal(base, approx=True)
    part = part * (2.0 - base * part)
    poly = TAIL[7]
    for k in range(6, -1, -1):
        poly = poly * part + TAIL[k]
    bell = jnp.exp(-0.5 * pre * pre)
    tail = poly * part * bell
    return (jnp.where(pre < 0.0, tail, 1.0 - tail), bell)


def small_rows(w_ref):
    rows = w_ref[0, :, 0:LANES].astype(F32).T
    return rows[SMALL_AT : SMALL_AT + 6]


def hidden_row(w_ref, t):
    return w_ref[t, :, 0:LANES].astype(F32).T[HIDDEN_AT : HIDDEN_AT + 1]


def id_lanes(ids):
    place = lax.broadcasted_iota(jnp.int32, (LANES, PACK), 0)
    match = (place - USED) == ids
    ones = (place >= ONES) & (place < ONES + 3)
    key_side = jnp.where(match | ones, 1.0, 0.0).T
    crop = (place >= USED) & (place < ONES)
    query_side = jnp.where(crop & jnp.logical_not(match), MASKED, 0.0).astype(BF)
    return (key_side, query_side)


def attention(qkv_ref, a_ref, lse_ref, base, query_side, groups):
    place = lax.broadcasted_iota(jnp.int32, (LANES, PACK), 0) // HEAD_DIM
    ones = jnp.ones((16, PACK), BF)
    blank = jnp.zeros((LANES - USED, PACK), F32)
    rows = pl.ds(base, PACK)
    for g in range(groups):
        at = g * 3 * LANES
        query = qkv_ref[rows, at : at + LANES].T
        keys = qkv_ref[rows, at + LANES : at + 2 * LANES]
        values = qkv_ref[rows, at + 2 * LANES : at + 3 * LANES].T
        outs = []
        for h in range(HEADS_HERE):
            scores = mm(keys, jnp.where(place == h, query, query_side))
            top = jnp.max(scores, axis=0, keepdims=True)
            probs = jnp.exp2((scores - top) * EXP_SCALE).astype(BF)
            mix = jnp.concatenate([values[h * HEAD_DIM : (h + 1) * HEAD_DIM], ones], axis=0)
            mixed = mm(mix, probs)
            total = mixed[HEAD_DIM : HEAD_DIM + 1]
            outs.append(mixed[:HEAD_DIM] * (1.0 / total))
            if lse_ref is not None:
                line = g * HEADS_HERE + h
                lse_ref[line : line + 1, rows] = top + jnp.log(total) * (1.0 / SCALE)
        a_ref[rows, g * LANES : (g + 1) * LANES] = (
            jnp.concatenate(outs + [blank], axis=0).T.astype(BF)
        )


def forward_front(x_ref, ids_ref, w_ref, small, qkv_ref, a_ref, h1_ref, x1_ref, lse_ref, base, pack):
    groups = w_ref.shape[0]
    rows = pl.ds(base, PACK)
    values = x_ref[rows, :].astype(F32)
    unit, _ = norm_parts(values)
    first = (unit * small[0:1] + small[1:2]).astype(BF)
    if h1_ref is not None:
        h1_ref[rows, :] = first
    key_side, query_side = id_lanes(ids_ref[pack])
    for g in range(groups):
        at = g * 3 * LANES
        qkv_ref[rows, at : at + LANES] = mm(first, w_ref[g, :, 0:LANES]).astype(BF)
        packed = mm(first, w_ref[g, :, LANES : 3 * LANES])
        qkv_ref[rows, at + LANES : at + 2 * LANES] = (packed[:, :LANES] + key_side).astype(BF)
        qkv_ref[rows, at + 2 * LANES : at + 3 * LANES] = (packed[:, LANES:] + key_side).astype(BF)
    attention(qkv_ref, a_ref, lse_ref, base, query_side, groups)
    branch = mm_nt(a_ref[rows, 0:LANES], w_ref[0, :, 3 * LANES : 4 * LANES])
    for g in range(1, groups):
        branch += mm_nt(
            a_ref[rows, g * LANES : (g + 1) * LANES], w_ref[g, :, 3 * LANES : 4 * LANES]
        )
    x1_ref[rows, :] = x_ref[rows, :].astype(F32) + branch + small[4:5]


def ffn_tile(w_ref, j):
    depth = w_ref.shape[1]
    per = depth // LANES
    up, down = [], []
    for b in (2 * j, 2 * j + 1):
        t, o = b // per, (b % per) * LANES
        up.append(w_ref[t, :, ATT + o : ATT + o + LANES])
        down.append(w_ref[t, :, ATT + depth + o : ATT + depth + o + LANES])
    return (jnp.concatenate(up, axis=1), jnp.concatenate(down, axis=1))


def key_kernel(place_ref, x_ref, ids_ref, w_ref, out_ref, qkv_ref, a_ref, x1_ref, h2_ref, bias_ref):
    rows_here, depth = x_ref.shape
    small = small_rows(w_ref)
    for t in range(w_ref.shape[0]):
        bias_ref[:, t * depth : (t + 1) * depth] = hidden_row(w_ref, t)

    @pl.loop(0, rows_here // PACK)
    def _(pack):
        base = pl.multiple_of(pack * PACK, PACK)
        forward_front(x_ref, ids_ref, w_ref, small, qkv_ref, a_ref, None, x1_ref, None, base, pack)
        rows = pl.ds(base, PACK)
        unit, _ = norm_parts(x1_ref[rows, :])
        h2_ref[rows, :] = (unit * small[2:3] + small[3:4]).astype(BF)

    tiles = w_ref.shape[0] * depth // (2 * LANES)
    step = 256

    @pl.loop(0, rows_here // step)
    def _(r):
        rows = pl.ds(pl.multiple_of(r * step, step), step)
        second = h2_ref[rows, :]
        total = x1_ref[rows, :] + small[5:6]
        for j in range(tiles):
            up, down = ffn_tile(w_ref, j)
            pre = mm(second, up) + bias_ref[:, j * 256 : (j + 1) * 256]
            acts = []
            for i in range(0, step, 64):
                piece = pre[i : i + 64]
                phi, _ = tail_parts(piece)
                acts.append((piece * phi).astype(BF))
            total += mm_nt(jnp.concatenate(acts, axis=0), down)
        out_ref[rows, :] = total.astype(BF)


def query_kernel(
    place_ref,
    x_ref,
    cot_ref,
    ids_ref,
    w_ref,
    out_ref,
    qkv_ref,
    a_ref,
    lse_ref,
    h1_ref,
    dx1_ref,
    grad_ref,
    line_ref,
    hidden_ref,
    x1_ref,
    h2_ref,
    h2t_ref,
    eb_ref,
    ebt_ref,
    act_ref,
    dpre_ref,
    dh2_ref,
    bias_ref,
):
    rows_here, depth = x_ref.shape
    groups = w_ref.shape[0]
    small = small_rows(w_ref)
    for t in range(groups):
        bias_ref[:, t * depth : (t + 1) * depth] = hidden_row(w_ref, t)

    lse_ref[...] = jnp.zeros_like(lse_ref)
    h2t_ref[depth:, :] = jnp.ones((h2t_ref.shape[0] - depth, rows_here), BF)

    @pl.loop(0, rows_here // PACK)
    def _(pack):
        base = pl.multiple_of(pack * PACK, PACK)
        forward_front(
            x_ref, ids_ref, w_ref, small, qkv_ref, a_ref, h1_ref, x1_ref, lse_ref, base, pack
        )
        rows = pl.ds(base, PACK)
        unit, _ = norm_parts(x1_ref[rows, :])
        second = (unit * small[2:3] + small[3:4]).astype(BF)
        h2_ref[rows, :] = second
        h2t_ref[0:depth, rows] = second.T
        valid = jnp.where(ids_ref[pack] < CROPS, 1.0, 0.0)
        valid = jnp.broadcast_to(valid, (LANES, PACK)).T[:, 0:1]
        low = (cot_ref[rows, :].astype(F32) * valid).astype(BF)
        eb_ref[rows, :] = low
        ebt_ref[:, rows] = low.T

    tiles = groups * depth // (2 * LANES)
    step = 256
    chunks = rows_here // step
    per = depth // LANES
    for j in range(tiles):
        up, down = ffn_tile(w_ref, j)
        bias = bias_ref[:, j * 256 : (j + 1) * 256]
        for r in range(chunks):
            rows = slice(r * step, (r + 1) * step)
            pre = mm(h2_ref[rows, :], up) + bias
            da = mm(eb_ref[rows, :], down)
            acts, dps = [], []
            for i in range(0, step, 64):
                piece = pre[i : i + 64]
                phi, bell = tail_parts(piece)
                acts.append((piece * phi).astype(BF))
                slope = phi + piece * (bell * (1.0 / math.sqrt(2.0 * math.pi)))
                dps.append((da[i : i + 64] * slope).astype(BF))
            act = jnp.concatenate(acts, axis=0)
            dpre = jnp.concatenate(dps, axis=0)
            act_ref[rows, :] = act
            dpre_ref[rows, :] = dpre
            if j == 0:
                x1_now = x1_ref[rows, :] + small[5:6]
                qsum = x1_now + mm_nt(act, down)
                dsum = mm_nt(dpre, up)
            else:
                qsum = dh2_ref[0, rows, :] + mm_nt(act, down)
                dsum = dh2_ref[1, rows, :] + mm_nt(dpre, up)
            dh2_ref[0, rows, :] = qsum
            dh2_ref[1, rows, :] = dsum
        gup = mm(h2t_ref[...], dpre_ref[...])
        gdown = mm(ebt_ref[...], act_ref[...])
        for k, b in enumerate((2 * j, 2 * j + 1)):
            t, o = b // per, (b % per) * LANES
            grad_ref[t, :, o : o + LANES] = gup[:depth, k * LANES : (k + 1) * LANES].astype(BF)
            grad_ref[t, :, depth + o : depth + o + LANES] = gdown[
                :, k * LANES : (k + 1) * LANES
            ].astype(BF)
            hidden_ref[t : t + 1, o : o + LANES] = gup[
                depth : depth + 1, k * LANES : (k + 1) * LANES
            ]

    out_ref[...] = dh2_ref[0].astype(BF)

    line_ref[...] = jnp.zeros_like(line_ref)

    @pl.loop(0, rows_here // PACK)
    def _(pack):
        rows = pl.ds(pl.multiple_of(pack * PACK, PACK), PACK)
        unit, scale = norm_parts(x1_ref[rows, :])
        grad = dh2_ref[1, rows, :]
        valid = jnp.where(ids_ref[pack] < CROPS, 1.0, 0.0)
        valid = jnp.broadcast_to(valid, (LANES, PACK)).T[:, 0:1]
        wide = cot_ref[rows, :].astype(F32) * valid
        dx1 = wide + norm_back(grad, unit, scale, small[2:3])
        dx1_ref[rows, :] = dx1
        line_ref[2:3, :] += jnp.sum(grad * unit, axis=0, keepdims=True)
        line_ref[3:4, :] += jnp.sum(grad, axis=0, keepdims=True)
        line_ref[4:5, :] += jnp.sum(dx1, axis=0, keepdims=True)
        line_ref[5:6, :] += jnp.sum(wide, axis=0, keepdims=True)


def attention_back(qkv_ref, a_ref, lse_ref, da_ref, dqkv_ref, base, query_side, groups):
    place = lax.broadcasted_iota(jnp.int32, (LANES, PACK), 0)
    head_of = place // HEAD_DIM
    lane = lax.broadcasted_iota(jnp.int32, (PACK, LANES), 1) // HEAD_DIM
    rows = pl.ds(base, PACK)
    none = jnp.zeros((PACK, LANES), BF)

    def split(line):
        high = line.astype(BF).astype(F32)
        rest = line - high
        middle = rest.astype(BF).astype(F32)
        low = rest - middle
        block = jnp.where(
            place == ONES,
            high,
            jnp.where(place == ONES + 1, middle, jnp.where(place == ONES + 2, low, 0.0)),
        )
        return block.astype(BF)

    for g in range(groups):
        at = g * 3 * LANES
        query = qkv_ref[rows, at : at + LANES]
        keys = qkv_ref[rows, at + LANES : at + 2 * LANES]
        values = qkv_ref[rows, at + 2 * LANES : at + 3 * LANES]
        grad = da_ref[rows, g * LANES : (g + 1) * LANES]
        query_t, keys_t, grad_t = query.T, keys.T, grad.T
        both = a_ref[rows, g * LANES : (g + 1) * LANES].T.astype(F32) * grad_t.astype(F32)
        dq, dk, dv = [], None, None
        for h in range(HEADS_HERE):
            part = slice(h * HEAD_DIM, (h + 1) * HEAD_DIM)
            line = g * HEADS_HERE + h
            lse = lse_ref[line : line + 1, rows]
            side = jnp.where(place < ONES, query_side, split(-lse))
            scores = mm(keys, jnp.where(head_of == h, query_t, side))
            probs = jnp.exp2(scores * EXP_SCALE)
            inner = jnp.sum(both[part], axis=0, keepdims=True)
            pull = mm(values, jnp.where(head_of == h, grad_t, split(-inner)))
            low = probs.astype(BF)
            dscores = (probs * pull).astype(BF)
            dv_h = mm(low, jnp.where(lane == h, grad, none))
            dk_h = mm(dscores, jnp.where(lane == h, query, none))
            dv = dv_h if dv is None else dv + dv_h
            dk = dk_h if dk is None else dk + dk_h
            dq.append(mm(keys_t[part], dscores))
        dq.append(jnp.zeros((LANES - USED, PACK), F32))
        dqkv_ref[rows, at : at + LANES] = (jnp.concatenate(dq, axis=0).T * SCALE).astype(BF)
        dqkv_ref[rows, at + LANES : at + 2 * LANES] = (dk * SCALE).astype(BF)
        dqkv_ref[rows, at + 2 * LANES : at + 3 * LANES] = dv.astype(BF)


def back_kernel(
    place_ref,
    x_ref,
    ids_ref,
    w_ref,
    qkv_ref,
    a_ref,
    lse_ref,
    h1_ref,
    dx1_ref,
    line_ref,
    hidden_ref,
    out_ref,
    grad_ref,
    da_ref,
    dqkv_ref,
    h1t_ref,
    dybt_ref,
    sums_ref,
):
    rows_here, depth = x_ref.shape
    groups = w_ref.shape[0]
    small = small_rows(w_ref)
    sums_ref[...] = jnp.zeros_like(sums_ref)
    sums_ref[SMALL_AT : SMALL_AT + 8, :] = line_ref[...]

    @pl.loop(0, rows_here // PACK)
    def _(pack):
        base = pl.multiple_of(pack * PACK, PACK)
        rows = pl.ds(base, PACK)
        _, query_side = id_lanes(ids_ref[pack])
        low = dx1_ref[rows, :].astype(BF)
        dybt_ref[:, rows] = low.T
        h1t_ref[:, rows] = h1_ref[rows, :].T
        for g in range(groups):
            da_ref[rows, g * LANES : (g + 1) * LANES] = mm(
                low, w_ref[g, :, 3 * LANES : 4 * LANES]
            ).astype(BF)
        attention_back(qkv_ref, a_ref, lse_ref, da_ref, dqkv_ref, base, query_side, groups)
        width = 3 * LANES
        grad = mm_nt(dqkv_ref[rows, 0:width], w_ref[0, :, 0:width])
        for g in range(1, groups):
            grad += mm_nt(dqkv_ref[rows, g * width : (g + 1) * width], w_ref[g, :, 0:width])
        unit, scale = norm_parts(x_ref[rows, :].astype(F32))
        back = norm_back(grad, unit, scale, small[0:1])
        out_ref[rows, :] = (dx1_ref[rows, :] + back).astype(BF)
        sums_ref[SMALL_AT : SMALL_AT + 1, :] += jnp.sum(grad * unit, axis=0, keepdims=True)
        sums_ref[SMALL_AT + 1 : SMALL_AT + 2, :] += jnp.sum(grad, axis=0, keepdims=True)

    lane = lax.broadcasted_iota(jnp.int32, (depth, LANES), 1)
    for g in range(groups):
        width = 3 * LANES
        sums_ref[HIDDEN_AT : HIDDEN_AT + 1, :] = hidden_ref[g : g + 1, :]
        extra = sums_ref[...].T
        entry = mm(h1t_ref[...], dqkv_ref[:, g * width : (g + 1) * width])
        grad_ref[g, :, 0:LANES] = jnp.where(lane < USED, entry[:, :LANES], extra).astype(BF)
        grad_ref[g, :, LANES:width] = entry[:, LANES:].astype(BF)
        grad_ref[g, :, width : width + LANES] = mm(
            dybt_ref[...], a_ref[:, g * LANES : (g + 1) * LANES]
        ).astype(BF)


def params():
    return pltpu.CompilerParams(vmem_limit_bytes=60 * 2**20)


def whole(shape):
    return pl.BlockSpec(shape, lambda i, place: (0,) * len(shape))


def own_rows(rows, depth):
    return pl.BlockSpec((rows, depth), lambda i, place: (place[0], 0))


def own_ids(packs):
    return pl.BlockSpec((packs, 1, PACK), lambda i, place: (place[0], 0, 0))


def run_key(place, tokens, ids, weights, rows):
    depth = tokens.shape[1]
    groups, _, width = weights.shape
    return pl.pallas_call(
        key_kernel,
        grid_spec=pltpu.PrefetchScalarGridSpec(
            num_scalar_prefetch=1,
            grid=(1,),
            in_specs=[own_rows(rows, depth), own_ids(rows // PACK), whole(weights.shape)],
            out_specs=whole((rows, depth)),
            scratch_shapes=[
                VMEM((rows, groups * 3 * LANES), BF),
                VMEM((rows, groups * LANES), BF),
                VMEM((rows, depth), F32),
                VMEM((rows, depth), BF),
                VMEM((1, groups * depth), F32),
            ],
        ),
        out_shape=jax.ShapeDtypeStruct((rows, depth), BF),
        compiler_params=params(),
        name="key_block",
    )(place, tokens, ids, weights)


def run_query(place, tokens, cotangent, ids, weights, rows):
    depth = tokens.shape[1]
    groups = weights.shape[0]
    outs = [
        ((rows, depth), BF),
        ((rows, groups * 3 * LANES), BF),
        ((rows, groups * LANES), BF),
        ((16, rows), F32),
        ((rows, depth), BF),
        ((rows, depth), F32),
        ((groups, depth, 2 * depth), BF),
        ((8, depth), F32),
        ((groups, depth), F32),
    ]
    return pl.pallas_call(
        query_kernel,
        grid_spec=pltpu.PrefetchScalarGridSpec(
            num_scalar_prefetch=1,
            grid=(1,),
            in_specs=[
                own_rows(rows, depth),
                own_rows(rows, depth),
                own_ids(rows // PACK),
                whole(weights.shape),
            ],
            out_specs=[whole(shape) for shape, _ in outs],
            scratch_shapes=[
                VMEM((rows, depth), F32),
                VMEM((rows, depth), BF),
                VMEM((depth + 16, rows), BF),
                VMEM((rows, depth), BF),
                VMEM((depth, rows), BF),
                VMEM((rows, 2 * LANES), BF),
                VMEM((rows, 2 * LANES), BF),
                VMEM((2, rows, depth), F32),
                VMEM((1, groups * depth), F32),
            ],
        ),
        out_shape=[jax.ShapeDtypeStruct(shape, kind) for shape, kind in outs],
        compiler_params=params(),
        name="query_block",
    )(place, tokens, cotangent, ids, weights)


def run_back(place, tokens, ids, weights, kept, rows):
    depth = tokens.shape[1]
    groups = weights.shape[0]
    return pl.pallas_call(
        back_kernel,
        grid_spec=pltpu.PrefetchScalarGridSpec(
            num_scalar_prefetch=1,
            grid=(1,),
            in_specs=[own_rows(rows, depth), own_ids(rows // PACK), whole((groups, depth, ATT))]
            + [whole(item.shape) for item in kept],
            out_specs=[whole((rows, depth)), whole((groups, depth, ATT))],
            scratch_shapes=[
                VMEM((rows, groups * LANES), BF),
                VMEM((rows, groups * 3 * LANES), BF),
                VMEM((depth, rows), BF),
                VMEM((depth, rows), BF),
                VMEM((LANES, depth), F32),
            ],
        ),
        out_shape=[
            jax.ShapeDtypeStruct((rows, depth), BF),
            jax.ShapeDtypeStruct((groups, depth, ATT), BF),
        ],
        compiler_params=params(),
        name="back_block",
    )(place, tokens, ids, weights, *kept)


def pack_piece(entry, leave, up, down, small, hidden):
    def fill(block, *extra):
        block = jnp.concatenate([block] + [item.astype(block.dtype) for item in extra], axis=1)
        return jnp.pad(block, ((0, 0), (0, LANES - block.shape[1])))

    parts = [
        fill(entry[:, 0], small.T, hidden[:, None]),
        fill(entry[:, 1]),
        fill(entry[:, 2]),
        fill(leave.T),
        up,
        down.T,
    ]
    return jnp.concatenate([part.astype(BF) for part in parts], axis=1)


def unpack_piece(piece, depth):
    entry = jnp.stack([piece[:, k * LANES : k * LANES + USED] for k in range(3)], axis=1)
    leave = piece[:, 3 * LANES : 3 * LANES + USED].T
    up = piece[:, ATT : ATT + depth]
    down = piece[:, ATT + depth :].T
    small = piece[:, SMALL_AT : SMALL_AT + 6].T
    return (entry, leave, up, down, small, piece[:, HIDDEN_AT])


def adamw(grad, first, second, master, decay, rate):
    moment = BETA_ONE * first + (1.0 - BETA_ONE) * grad
    square = BETA_TWO * second + (1.0 - BETA_TWO) * grad * grad
    ahead = moment / (1.0 - BETA_ONE**STEP)
    spread = square / (1.0 - BETA_TWO**STEP)
    return (
        moment,
        square,
        master - rate * (ahead / (jnp.sqrt(spread) + ADAM_EPS) + decay * master),
    )


DECAYS = (DECAY, DECAY, DECAY, DECAY, 0.0, 0.0)
RATES = (RATE_MATRIX, RATE_EXIT, RATE_MATRIX, RATE_MATRIX, RATE_SMALL, RATE_BIAS)


def finish_plain(grad_att, grad_ffn, masters, firsts, seconds):
    depth = grad_att.shape[1]
    grads = jnp.concatenate([grad_att, grad_ffn], axis=2).astype(F32)
    own = lax.psum_scatter(grads, "tensor", scatter_dimension=0, tiled=False)
    own = lax.psum_scatter(own, "dp", scatter_dimension=0, tiled=True)
    shares = unpack_piece(own, depth)
    copies = float(lax.axis_size("tensor"))
    total = jnp.sum(shares[4] * shares[4]) / copies
    for k in (0, 1, 2, 3, 5):
        total = total + jnp.sum(shares[k] * shares[k])
    norm_value = jnp.sqrt(lax.psum(total, ("dp", "tensor")))
    factor = CLIP / jnp.maximum(norm_value, CLIP)
    outs = []
    for k in range(6):
        outs.extend(
            adamw(shares[k] * factor, firsts[k], seconds[k], masters[k], DECAYS[k], RATES[k])
        )
    return (norm_value, outs)


def spot():
    dp, t = lax.axis_index("dp"), lax.axis_index("tensor")
    return (dp, t)


def flip(value, bits):
    for bit in (1, 2, 4):
        if bits & bit:
            value = value + bit - 2 * bit * ((value // bit) % 2)
    return value


def greet(peers):
    barrier = pltpu.get_barrier_semaphore()
    for peer in peers:
        pl.semaphore_signal(barrier, inc=1, device_id=peer, device_id_type=MESH)
    pl.semaphore_wait(barrier, len(peers))


KEY_CHUNKS = 4
GATHER_SENDS = 6 + KEY_CHUNKS + 1 + 5 + 12 + 8 + KEY_CHUNKS


def gather_kernel(*refs):
    entry_ref, leave_ref, up_ref, down_ref, small_ref, hidden_ref = refs[:6]
    key_refs = refs[6:12]
    all_ref, keys_ref, piece_ref, key_ref, send_sem, recv_sem, local_sem = refs[12:]
    dp, t = spot()
    core, across = (dp, flip(t, 1)), (dp, flip(t, 2))
    side = (flip(dp, 1), t)
    line = [(flip(dp, 2 * j), t) for j in range(4)]
    count = [0]
    sent = []

    def send(src, dst, peer):
        k = count[0]
        count[0] += 1
        copy = pltpu.make_async_remote_copy(
            src_ref=src,
            dst_ref=dst,
            send_sem=send_sem.at[k],
            recv_sem=recv_sem.at[k],
            device_id=peer,
            device_id_type=MESH,
        )
        copy.start()
        sent.append(copy)
        return copy

    rows = up_ref.shape[0]
    depth = up_ref.shape[1]
    wide = LANES - USED
    extra = [small_ref[...], hidden_ref[...], jnp.zeros((wide - 7, rows), F32)]
    extra = jnp.concatenate(extra, axis=0).T
    blank = jnp.zeros((rows, wide), F32)
    blocks = [entry_ref[0], entry_ref[1], entry_ref[2], leave_ref[...]]
    for k, block in enumerate(blocks):
        block = jnp.concatenate([block, blank if k else extra], axis=1)
        piece_ref[:, k * LANES : (k + 1) * LANES] = block.astype(BF)
    piece_ref[:, ATT : ATT + depth] = up_ref[...].astype(BF)
    piece_ref[:, ATT + depth :] = down_ref[...].astype(BF)
    greet([core, across, side] + line[1:])
    far = flip(t, 2)
    part = depth // KEY_CHUNKS
    to_across = send(piece_ref, all_ref.at[t, dp], across)
    to_line = [[send(piece_ref, all_ref.at[t, dp], line[j])] for j in range(1, 4)]
    to_side = [[send(piece_ref, all_ref.at[t, dp], side)]]
    entry_ref, leave_ref, up_ref, down_ref, small_ref, hidden_ref = key_refs
    blank = jnp.zeros((wide, depth), BF)
    extra = [small_ref[...], hidden_ref[...], jnp.zeros((wide - 7, depth), BF)]
    blocks = [entry_ref[0], entry_ref[1], entry_ref[2], leave_ref[...]]
    for k, block in enumerate(blocks):
        block = jnp.concatenate([block] + ([blank] if k else extra), axis=0)
        key_ref[:, k * LANES : (k + 1) * LANES] = block.T
    key_ref[:, ATT : ATT + depth] = up_ref[...]
    key_ref[:, ATT + depth :] = down_ref[...].T
    own = [
        pltpu.make_async_copy(piece_ref, all_ref.at[t, dp], local_sem.at[0]),
        pltpu.make_async_copy(key_ref, keys_ref.at[t], local_sem.at[1]),
    ]
    for copy in own:
        copy.start()
    key_across = []
    for k in range(KEY_CHUNKS):
        rows = pl.ds(k * part, part)
        key_across.append(send(key_ref.at[rows], keys_ref.at[t, rows], across))
    rest = [send(key_ref, keys_ref.at[t], core), send(piece_ref, all_ref.at[t, dp], core)]
    to_across.wait_recv()
    piece = all_ref.at[far, dp]
    for j in range(1, 4):
        to_line[j - 1].append(send(piece, piece, line[j]))
    to_side[0].append(send(piece, piece, side))
    rest.append(send(piece, piece, core))
    for j in range(1, 4):
        other = line[j][0]
        pair = []
        for k, group in enumerate((t, far)):
            to_line[j - 1][k].wait_recv()
            piece = all_ref.at[group, other]
            pair.append(send(piece, piece, side))
            rest.append(send(piece, piece, core))
        to_side.append(pair)
    for j in range(4):
        other = flip(line[j][0], 1)
        for k, group in enumerate((t, far)):
            to_side[j][k].wait_recv()
            piece = all_ref.at[group, other]
            rest.append(send(piece, piece, core))
    for k in range(KEY_CHUNKS):
        rows = pl.ds(k * part, part)
        key_across[k].wait_recv()
        rest.append(send(keys_ref.at[far, rows], keys_ref.at[far, rows], core))
    for copy in rest:
        copy.wait_recv()
    for copy in sent:
        copy.wait_send()
    for copy in own:
        copy.wait()


def lay(entry, leave, up, down, small, hidden):
    return [entry.transpose(1, 0, 2), leave.T, up, down.T, small, hidden.reshape(1, -1)]


def run_gather(masters, keys, dp, tensor):
    key_entry, key_leave, key_up, key_down, key_small, key_hidden = keys
    rows, depth = masters[2].shape
    width = ATT + 2 * depth
    anywhere = pl.BlockSpec(memory_space=pl.ANY)
    args = lay(*masters)
    args += [key_entry.transpose(1, 2, 0), key_leave, key_up, key_down, key_small]
    args.append(key_hidden.reshape(1, -1))
    return pl.pallas_call(
        gather_kernel,
        in_specs=[pl.BlockSpec(memory_space=VMEM)] * 12,
        out_specs=[anywhere] * 2,
        out_shape=[
            jax.ShapeDtypeStruct((tensor, dp, rows, width), BF),
            jax.ShapeDtypeStruct((tensor, depth, width), BF),
        ],
        scratch_shapes=[
            VMEM((rows, width), BF),
            VMEM((depth, width), BF),
            pltpu.SemaphoreType.DMA((GATHER_SENDS,)),
            pltpu.SemaphoreType.DMA((GATHER_SENDS,)),
            pltpu.SemaphoreType.DMA((2,)),
        ],
        compiler_params=pltpu.CompilerParams(
            collective_id=1, has_side_effects=True, vmem_limit_bytes=32 * 2**20
        ),
        name="gather_weights",
    )(*args)


FINISH_SENDS = (2 + 1 + 4 + 3) + (2 + 8 + 1 + 3) + 3 + 7


def finish_kernel(*refs):
    ga_ref, gb_ref, norm_ref, own_a, own_b = refs[:5]
    rc_a, s0_a, r1_a, s1_a, r2_a, s2_a, r3_a = refs[5:12]
    rc_b, s0_b, r1_b, s1_b, r2_b, s2_b, r3_b = refs[12:19]
    near_ref, far_ref, send_sem, recv_sem = refs[19:]
    dp, t = spot()
    x, c = t // 2, t % 2
    z, y = dp // 2, dp % 2
    core, across = (dp, flip(t, 1)), (dp, flip(t, 2))
    side = (flip(dp, 1), t)
    line = [(flip(dp, 2 * j), t) for j in range(4)]
    greet([(dp, flip(t, k)) for k in (1, 2, 3)] + [(flip(dp, k), t) for k in range(1, 8)])
    count = [0]
    sent = []

    def send(src, dst, peer):
        k = count[0]
        count[0] += 1
        copy = pltpu.make_async_remote_copy(
            src_ref=src,
            dst_ref=dst,
            send_sem=send_sem.at[k],
            recv_sem=recv_sem.at[k],
            device_id=peer,
            device_id_type=MESH,
        )
        copy.start()
        sent.append(copy)
        return copy

    def arrived(copies):
        for copy in copies:
            copy.wait_recv()

    def add(dst, left, right):
        dst[...] = (left[...].astype(F32) + right[...].astype(F32)).astype(BF)

    core_b = [send(gb_ref.at[2 * k + 1 - c], rc_b.at[k], core) for k in range(2)]
    core_a = [send(ga_ref.at[2 * k + 1 - c], rc_a.at[k], core) for k in range(2)]
    arrived(core_b)

    @pl.loop(0, 8)
    def _(d):
        for k in range(2):
            add(s0_b.at[k, d], gb_ref.at[2 * k + c, d], rc_b.at[k, d])

    side_b = [
        send(s0_b.at[k, 2 * w + 1 - y], r1_b.at[k, w], side) for k in range(2) for w in range(4)
    ]
    arrived(core_a)

    @pl.loop(0, 8)
    def _(d):
        for k in range(2):
            add(s0_a.at[k, d], ga_ref.at[2 * k + c, d], rc_a.at[k, d])

    across_a = [send(s0_a.at[1 - x], r1_a, across)]
    arrived(side_b)

    @pl.loop(0, 4)
    def _(w):
        for k in range(2):
            add(s1_b.at[k, w], s0_b.at[k, 2 * w + y], r1_b.at[k, w])

    across_b = [send(s1_b.at[1 - x], r2_b, across)]
    arrived(across_a)

    @pl.loop(0, 8)
    def _(d):
        add(s1_a.at[d], s0_a.at[x, d], r1_a.at[d])

    side_a = [send(s1_a.at[2 * w + 1 - y], r2_a.at[w], side) for w in range(4)]
    arrived(across_b)

    @pl.loop(0, 4)
    def _(w):
        add(s2_b.at[w], s1_b.at[x, w], r2_b.at[w])

    line_b = [send(s2_b.at[line[j][0] // 2], r3_b.at[j - 1], line[j]) for j in range(1, 4)]
    arrived(side_a)

    @pl.loop(0, 4)
    def _(w):
        add(s2_a.at[w], s1_a.at[2 * w + y], r2_a.at[w])

    line_a = [send(s2_a.at[line[j][0] // 2], r3_a.at[j - 1], line[j]) for j in range(1, 4)]
    arrived(line_b)
    grad_b = s2_b[z].astype(F32)
    for j in range(3):
        grad_b = grad_b + r3_b[j].astype(F32)
    arrived(line_a)
    grad_a = s2_a[z].astype(F32)
    for j in range(3):
        grad_a = grad_a + r3_a[j].astype(F32)

    rows, width = grad_a.shape
    depth = grad_b.shape[1] // 2
    lane = lax.broadcasted_iota(jnp.int32, (rows, LANES), 1)
    total = jnp.zeros((8, LANES), F32)

    def fold(block):
        out = block[0:8]
        for k in range(8, rows, 8):
            out = out + block[k : k + 8]
        return out

    once = jnp.where(t == 0, 1.0, 0.0)
    small_share = jnp.where(lane < HIDDEN_AT, once, jnp.where(lane == HIDDEN_AT, 1.0, 0.0))
    for k in range(4):
        block = grad_a[:, k * LANES : (k + 1) * LANES]
        share = jnp.where(lane < USED, 1.0, small_share if k == 0 else 0.0)
        total = total + fold(block * block * share)
    for k in range(2 * depth // LANES):
        block = grad_b[:, k * LANES : (k + 1) * LANES]
        total = total + fold(block * block)
    near_ref[t] = total
    near = [send(near_ref.at[t], near_ref.at[t], (dp, flip(t, k))) for k in (1, 2, 3)]
    arrived(near)
    far_ref[dp] = (near_ref[0] + near_ref[1]) + (near_ref[2] + near_ref[3])
    far = [send(far_ref.at[dp], far_ref.at[dp], (flip(dp, k), t)) for k in range(1, 8)]
    arrived(far)
    total = far_ref[0]
    for k in range(1, 8):
        total = total + far_ref[k]
    total = jnp.sum(total, axis=0, keepdims=True)
    norm_value = jnp.sqrt(jnp.sum(total, axis=1, keepdims=True))
    norm_ref[...] = jnp.broadcast_to(norm_value, norm_ref.shape)
    own_a[...] = grad_a
    own_b[...] = grad_b
    for copy in sent:
        copy.wait_send()


def run_finish(grad_att, grad_ffn):
    groups, dp, rows, wide_a = grad_att.shape
    wide_b = grad_ffn.shape[3]
    shapes = [
        jax.ShapeDtypeStruct((8, LANES), F32),
        jax.ShapeDtypeStruct((rows, wide_a), F32),
        jax.ShapeDtypeStruct((rows, wide_b), F32),
    ]
    scratch = []
    for wide, first in ((wide_a, (8,)), (wide_b, (2, 4))):
        scratch.append(VMEM((2, 8, rows, wide), BF))
        scratch.append(VMEM((2, 8, rows, wide), BF))
        scratch.append(VMEM(first + (rows, wide), BF))
        scratch.append(VMEM(first + (rows, wide), BF))
        scratch.append(VMEM((4, rows, wide), BF))
        scratch.append(VMEM((4, rows, wide), BF))
        scratch.append(VMEM((3, rows, wide), BF))
    scratch.append(VMEM((4, 8, LANES), F32))
    scratch.append(VMEM((8, 8, LANES), F32))
    scratch.append(pltpu.SemaphoreType.DMA((FINISH_SENDS,)))
    scratch.append(pltpu.SemaphoreType.DMA((FINISH_SENDS,)))
    spec = pl.BlockSpec(memory_space=VMEM)
    return pl.pallas_call(
        finish_kernel,
        in_specs=[spec] * 2,
        out_specs=[spec] * 3,
        out_shape=shapes,
        scratch_shapes=scratch,
        compiler_params=pltpu.CompilerParams(
            collective_id=2, has_side_effects=True, vmem_limit_bytes=60 * 2**20
        ),
        name="finish",
    )(grad_att, grad_ffn)


def step_kernel(norm_ref, ga_ref, gb_ref, *refs):
    masters, firsts, seconds = refs[0:6], refs[6:12], refs[12:18]
    value_ref, outs = refs[18], refs[19:]
    norm_value = norm_ref[0:1, 0:1]
    value_ref[...] = norm_value
    factor = CLIP / jnp.maximum(norm_value, CLIP)
    grad_a = ga_ref[...] * factor
    grad_b = gb_ref[...] * factor
    depth = grad_b.shape[1] // 2

    def update(k, at, grad):
        new = adamw(grad, firsts[k][at], seconds[k][at], masters[k][at], DECAYS[k], RATES[k])
        for j in range(3):
            outs[3 * k + j][at] = new[j]

    for j in range(3):
        update(0, j, grad_a[:, j * LANES : j * LANES + USED])
    update(1, slice(None), grad_a[:, 3 * LANES : 3 * LANES + USED])
    update(2, slice(None), grad_b[:, :depth])
    update(3, slice(None), grad_b[:, depth:])
    lines = grad_a[:, :LANES].T
    update(4, slice(None), lines[SMALL_AT : SMALL_AT + 6])
    update(5, slice(None), lines[HIDDEN_AT : HIDDEN_AT + 1])


def run_step(norm_tile, grad_a, grad_b, masters, firsts, seconds):
    state = lay(*masters) + lay(*firsts) + lay(*seconds)
    shapes = [jax.ShapeDtypeStruct((1, 1), F32)]
    for item in state[:6]:
        shapes.extend([jax.ShapeDtypeStruct(item.shape, F32)] * 3)
    spec = pl.BlockSpec(memory_space=VMEM)
    result = pl.pallas_call(
        step_kernel,
        in_specs=[spec] * 21,
        out_specs=[spec] * 19,
        out_shape=shapes,
        name="optimizer_step",
    )(norm_tile, grad_a, grad_b, *state)
    outs = list(result[1:])
    for k in range(3):
        outs[k] = outs[k].transpose(1, 0, 2)
        outs[3 + k] = outs[3 + k].T
        outs[9 + k] = outs[9 + k].T
        outs[15 + k] = outs[15 + k].reshape(-1)
    return (result[0].reshape(()), outs)


def join_kernel(place_ref, own_ref, core_ref, far_ref, both_ref, out_ref):
    for k, ref in enumerate((own_ref, core_ref, far_ref, both_ref)):

        @pl.when(pl.program_id(0) == k)
        def _():
            out_ref[...] = ref[...]


def spread_rows(place, own):
    def swap(item, bits):
        return lax.ppermute(item, "tensor", [(i, i ^ bits) for i in range(4)])

    far = swap(own, 2)
    near = swap(own, 1)
    both = swap(far, 1)
    rows, depth = own.shape

    def spot_of(i, place):
        return (place[0] + i - 2 * (i % 2) * (place[0] % 2) - 4 * (i // 2) * (place[0] // 2), 0)

    return pl.pallas_call(
        join_kernel,
        grid_spec=pltpu.PrefetchScalarGridSpec(
            num_scalar_prefetch=1,
            grid=(4,),
            in_specs=[pl.BlockSpec((rows, depth), lambda i, place: (0, 0))] * 4,
            out_specs=pl.BlockSpec((rows, depth), spot_of),
        ),
        out_shape=jax.ShapeDtypeStruct((4 * rows, depth), BF),
        compiler_params=pltpu.CompilerParams(vmem_limit_bytes=32 * 2**20),
        name="join_rows",
    )(place, own, near, far, both)


def on_device(*args):
    tokens, crop_ids, cotangent, key_tokens = args[:4]
    masters, firsts, seconds, keys = args[4:10], args[10:16], args[16:22], args[22:28]
    count, groups = lax.axis_size("dp"), lax.axis_size("tensor")
    direct = count == 8 and groups == 4
    rows, depth = tokens.shape[0] // groups, tokens.shape[1]
    place = lax.axis_index("tensor").astype(jnp.int32)[None]
    ids = crop_ids.reshape(-1, 1, PACK)
    if direct:
        weights, key_weights = run_gather(masters, keys, count, groups)
        weights = weights.reshape(groups, depth, -1)
    else:
        key_weights = lax.all_gather(pack_piece(*keys), "tensor", axis=0)
        weights = lax.all_gather(pack_piece(*masters), "dp", axis=0, tiled=True)
        weights = lax.all_gather(weights, "tensor", axis=0)

    def spread(own):
        if direct:
            return spread_rows(place, own)
        return lax.all_gather(own, "tensor", axis=0, tiled=True)

    key_out = spread(run_key(place, key_tokens, ids, key_weights, rows))
    forward = run_query(place, tokens, cotangent, ids, weights, rows)
    block_out = spread(forward[0])
    qkv, a, lse, h1, dx1, grad_ffn, lines, hidden = forward[1:]
    grad_rows, grad_att = run_back(
        place, tokens, ids, weights, (qkv, a, lse, h1, dx1, lines, hidden), rows
    )
    input_grad = spread(grad_rows)
    if direct:
        grads = run_finish(
            grad_att.reshape(groups, count, depth // count, -1),
            grad_ffn.reshape(groups, count, depth // count, -1),
        )
        norm_value, outs = run_step(*grads, masters, firsts, seconds)
    else:
        norm_value, outs = finish_plain(grad_att, grad_ffn, masters, firsts, seconds)
    return (block_out, key_out, input_grad, norm_value, *outs)


def solution(mesh):
    rows, line = P("dp", None), P("dp")
    entry, leave, up, down = P("dp", None, "tensor"), P("tensor", "dp"), P("dp", "tensor"), P("tensor", "dp")
    state = (entry, leave, up, down, P(None, "dp"), P(("tensor", "dp")))
    keys = (P(None, None, "tensor"), P("tensor", None), P(None, "tensor"), P("tensor", None), P(), P("tensor"))
    outs = tuple(spec for spec in state for _ in range(3))
    return jax.shard_map(
        on_device,
        mesh=mesh,
        in_specs=(rows, line, rows, rows) + state * 3 + keys,
        out_specs=(rows, rows, rows, P()) + outs,
        check_vma=False,
    )
```

```python
import math
from functools import partial

import jax
import jax.numpy as jnp
from jax import lax
from jax.experimental import pallas as pl
from jax.experimental.pallas import tpu as pltpu
from jax.sharding import PartitionSpec as P

HEAD_DIM = 32
PACK = 512
CROPS = 5
STEP = 10
LN_EPS = 1e-06
CLIP = 1.0
RATE_MATRIX = 0.03
RATE_EXIT = 0.2
RATE_SMALL = 0.5
RATE_BIAS = 0.3
BETA_ONE = 0.9
BETA_TWO = 0.999
ADAM_EPS = 1e-08
DECAY = 0.05
MASKED = -1e30

SCALE = HEAD_DIM ** (-0.5)
EXP_SCALE = SCALE * math.log2(math.e)
LOG_TWO = math.log(2.0)
LANES = 128
TILE = 2 * LANES
PIECE = 64
HEADS_HERE = 3
USED = HEADS_HERE * HEAD_DIM
ONES = USED + CROPS + 1
ATT = 4 * LANES
SMALL_AT = USED
HIDDEN_AT = USED + 6
MESH = pl.DeviceIdType.MESH
BF = jnp.bfloat16
F32 = jnp.float32
VMEM = pltpu.VMEM
NT = (((1,), (1,)), ((), ()))
TN = (((0,), (0,)), ((), ()))

def mm(left, right):
    return jnp.dot(left, right, preferred_element_type=F32)


def mm_nt(left, right):
    return lax.dot_general(left, right, NT, preferred_element_type=F32)


def norm_parts(values):
    mean = jnp.mean(values, axis=1, keepdims=True)
    centred = values - mean
    spread = jnp.mean(centred * centred, axis=1, keepdims=True)
    scale = lax.rsqrt(spread + LN_EPS)
    return (centred * scale, scale)


def norm_back(grad, unit, scale, gain):
    scaled = grad * gain
    first = jnp.mean(scaled, axis=1, keepdims=True)
    second = jnp.mean(scaled * unit, axis=1, keepdims=True)
    return scale * (scaled - first - unit * second)


def below(pre):
    return 0.5 + 0.5 * lax.erf(pre * math.sqrt(0.5))


def below_and_slope(pre):
    phi = below(pre)
    bell = jnp.exp2((pre * (-0.5 * math.log2(math.e))) * pre)
    return (phi, phi + (pre * (1.0 / math.sqrt(2.0 * math.pi))) * bell)


def small_rows_of(weight):
    return weight.astype(F32).T[SMALL_AT : SMALL_AT + 6]


def hidden_line(weight):
    return weight.astype(F32).T[HIDDEN_AT : HIDDEN_AT + 1]


def small_rows(w_ref):
    return small_rows_of(w_ref[0, :, 0:LANES])


def hidden_row(w_ref, t):
    return hidden_line(w_ref[t, :, 0:LANES])


def id_lanes(ids):
    place = lax.broadcasted_iota(jnp.int32, (LANES, PACK), 0)
    match = (place - USED) == ids
    ones = (place >= ONES) & (place < ONES + 3)
    key_side = jnp.where(match | ones, 1.0, 0.0).T
    crop = (place >= USED) & (place < ONES)
    query_side = jnp.where(crop & jnp.logical_not(match), MASKED, 0.0).astype(BF)
    return (key_side, query_side)


def attention(qkv_ref, a_ref, lse_ref, places, sides):
    place = lax.broadcasted_iota(jnp.int32, (LANES, PACK), 0) // HEAD_DIM
    ones = jnp.ones((16, PACK), BF)
    blank = jnp.zeros((LANES - USED, PACK), F32)
    heads = [(k, h) for k in range(len(places)) for h in range(HEADS_HERE)]
    held, outs = {}, {}

    def scores_of(k, h):
        if k not in held:
            slot, base = places[k]
            rows, at = pl.ds(base, PACK), slot * 3 * LANES
            query = qkv_ref[rows, at : at + LANES].T
            keys = qkv_ref[rows, at + LANES : at + 2 * LANES]
            values = qkv_ref[rows, at + 2 * LANES : at + 3 * LANES].T
            held[k] = (query, keys, values)
        query, keys, _ = held[k]
        return mm(keys, jnp.where(place == h, query, sides[k]))

    def mix(k, h, top, probs):
        slot, base = places[k]
        rows = pl.ds(base, PACK)
        values = held[k][2][h * HEAD_DIM : (h + 1) * HEAD_DIM]
        mixed = mm(jnp.concatenate([values, ones], axis=0), probs)
        total = mixed[HEAD_DIM : HEAD_DIM + 1]
        outs[(k, h)] = mixed[:HEAD_DIM] * (1.0 / total)
        if lse_ref is not None:
            line = slot * HEADS_HERE + h
            lse_ref[line : line + 1, rows] = top + jnp.log2(total)
        if h == HEADS_HERE - 1:
            parts = [outs[(k, n)] for n in range(HEADS_HERE)] + [blank]
            a_ref[rows, slot * LANES : (slot + 1) * LANES] = (
                jnp.concatenate(parts, axis=0).T.astype(BF)
            )

    scores = scores_of(*heads[0])
    waiting = None
    for n, head in enumerate(heads):
        later = scores_of(*heads[n + 1]) if n + 1 < len(heads) else None
        if waiting is not None:
            mix(*waiting)
        top = jnp.max(scores, axis=0, keepdims=True)
        waiting = head + (top, jnp.exp2(scores - top).astype(BF))
        scores = later
    mix(*waiting)


def enter(x_ref, ids_ref, small, h1_ref, base, pack):
    rows = pl.ds(base, PACK)
    values = x_ref[rows, :].astype(F32)
    unit, _ = norm_parts(values)
    first = (unit * small[0:1] + small[1:2]).astype(BF)
    h1_ref[rows, :] = first
    return id_lanes(ids_ref[pack])


def project(first, weight, qkv_ref, key_side, base, slot):
    rows, at = pl.ds(base, PACK), slot * 3 * LANES
    packed = mm(first, weight)
    qkv_ref[rows, at : at + LANES] = (packed[:, :LANES] * EXP_SCALE).astype(BF)
    for k in (1, 2):
        part = packed[:, k * LANES : (k + 1) * LANES] + key_side
        qkv_ref[rows, at + k * LANES : at + (k + 1) * LANES] = part.astype(BF)


def project_all(first, w_ref, qkv_ref, key_side, base):
    for g in range(w_ref.shape[0]):
        project(first, w_ref[g, :, 0 : 3 * LANES], qkv_ref, key_side, base, g)


def leaving(w_ref):
    return gathered(w_ref, 3 * LANES, LANES)


def leave(x_ref, weight, small, a_ref, x1_ref, base):
    rows = pl.ds(base, PACK)
    branch = mm_nt(a_ref[rows, :], weight)
    x1 = x_ref[rows, :].astype(F32) + branch + small[4:5]
    x1_ref[rows, :] = x1
    unit, _ = norm_parts(x1)
    return (unit * small[2:3] + small[3:4]).astype(BF)


def gathered(w_ref, at, width):
    parts = [w_ref[t, :, at : at + width] for t in range(w_ref.shape[0])]
    return jnp.concatenate(parts, axis=1)


def tile_of(w_ref, j, first):
    depth = w_ref.shape[1]
    per = depth // LANES
    parts = []
    for b in range(j * TILE // LANES, (j + 1) * TILE // LANES):
        at = first + (b % per) * LANES
        parts.append(w_ref[b // per, :, at : at + LANES])
    return jnp.concatenate(parts, axis=1)


def up_tile(w_ref, j):
    return tile_of(w_ref, j, ATT)


def down_tile(w_ref, j):
    return tile_of(w_ref, j, ATT + w_ref.shape[1])


def key_kernel(
    place_ref, x_ref, ids_ref, w_ref, out_ref, qkv_ref, a_ref, x1_ref, h1_ref, act_ref, bias_ref
):
    rows_here, depth = x_ref.shape
    groups = w_ref.shape[0]
    small = small_rows(w_ref)
    for t in range(groups):
        bias_ref[:, t * depth : (t + 1) * depth] = hidden_row(w_ref, t)

    @pl.loop(0, rows_here // PACK)
    def _(pack):
        base = pl.multiple_of(pack * PACK, PACK)
        rows = pl.ds(base, PACK)
        key_side, query_side = enter(x_ref, ids_ref, small, h1_ref, base, pack)
        project_all(h1_ref[rows, :], w_ref, qkv_ref, key_side, base)
        attention(qkv_ref, a_ref, None, [(g, base) for g in range(groups)], [query_side] * groups)
        second = leave(x_ref, leaving(w_ref), small, a_ref, x1_ref, base)
        feed(second, w_ref, bias_ref, act_ref)
        product = mm_nt(act_ref[...], gathered(w_ref, ATT + depth, depth))
        out_ref[rows, :] = (x1_ref[rows, :] + product + small[5:6]).astype(BF)


def feed(second, w_ref, bias_ref, act_ref):
    tiles = act_ref.shape[1] // TILE
    pre = mm(second, up_tile(w_ref, 0))
    for j in range(tiles):
        later = mm(second, up_tile(w_ref, j + 1)) if j + 1 < tiles else None
        cols = slice(j * TILE, (j + 1) * TILE)
        bias = bias_ref[:, cols]
        for i in range(0, pre.shape[0], PIECE):
            piece = pre[i : i + PIECE] + bias
            act_ref[i : i + PIECE, cols] = (piece * below(piece)).astype(BF)
        pre = later


def query_kernel(
    place_ref,
    x_ref,
    cot_ref,
    ids_ref,
    w_ref,
    out_ref,
    qkv_ref,
    a_ref,
    lse_ref,
    h1_ref,
    dx1_ref,
    grad_ref,
    line_ref,
    hidden_ref,
    x1_ref,
    h2_ref,
    h2t_ref,
    eb_ref,
    ebt_ref,
    act_ref,
    dpre_ref,
    bias_ref,
):
    rows_here, depth = x_ref.shape
    groups = w_ref.shape[0]
    small = small_rows(w_ref)
    for t in range(groups):
        bias_ref[:, t * depth : (t + 1) * depth] = hidden_row(w_ref, t)

    lse_ref[...] = jnp.zeros_like(lse_ref)
    line_ref[...] = jnp.zeros_like(line_ref)
    h2t_ref[depth:, :] = jnp.ones((h2t_ref.shape[0] - depth, rows_here), BF)

    @pl.loop(0, rows_here // PACK)
    def _(pack):
        base = pl.multiple_of(pack * PACK, PACK)
        rows = pl.ds(base, PACK)
        key_side, query_side = enter(x_ref, ids_ref, small, h1_ref, base, pack)
        project_all(h1_ref[rows, :], w_ref, qkv_ref, key_side, base)
        attention(
            qkv_ref, a_ref, lse_ref, [(g, base) for g in range(groups)], [query_side] * groups
        )
        second = leave(x_ref, leaving(w_ref), small, a_ref, x1_ref, base)
        h2_ref[rows, :] = second
        h2t_ref[0:depth, rows] = second.T
        low = masked_cot(cot_ref, ids_ref, pack, rows).astype(BF)
        eb_ref[rows, :] = low
        ebt_ref[:, rows] = low.T

    tiles = groups * depth // TILE
    per = depth // LANES
    step = PACK
    units = [(j, r) for j in range(tiles) for r in range(rows_here // step)]

    def start(unit):
        j, r = unit
        rows = slice(r * step, (r + 1) * step)
        return (mm(h2_ref[rows, :], up_tile(w_ref, j)), mm(eb_ref[rows, :], down_tile(w_ref, j)))

    now = start(units[0])
    for k, (j, r) in enumerate(units):
        later = start(units[k + 1]) if k + 1 < len(units) else None
        cols = slice(j * TILE, (j + 1) * TILE)
        bias = bias_ref[:, cols]
        pre, da = now
        for i in range(0, step, PIECE):
            rows = slice(r * step + i, r * step + i + PIECE)
            piece = pre[i : i + PIECE] + bias
            phi, slope = below_and_slope(piece)
            act_ref[rows, cols] = (piece * phi).astype(BF)
            dpre_ref[rows, cols] = (da[i : i + PIECE] * slope).astype(BF)
        now = later
        if (r + 1) * step == rows_here:
            gup = mm(h2t_ref[...], dpre_ref[:, cols])
            gdown = mm(ebt_ref[...], act_ref[:, cols])
            for n, b in enumerate((2 * j, 2 * j + 1)):
                t, o = b // per, (b % per) * LANES
                part = slice(n * LANES, (n + 1) * LANES)
                grad_ref[t, :, o : o + LANES] = gup[:depth, part].astype(BF)
                grad_ref[t, :, depth + o : depth + o + LANES] = gdown[:, part].astype(BF)
                hidden_ref[t : t + 1, o : o + LANES] = gup[depth : depth + 1, part]

    @pl.loop(0, rows_here // PACK)
    def _(pack):
        rows = pl.ds(pl.multiple_of(pack * PACK, PACK), PACK)
        x1 = x1_ref[rows, :]
        product = mm_nt(act_ref[rows, :], gathered(w_ref, ATT + depth, depth))
        out_ref[rows, :] = (x1 + product + small[5:6]).astype(BF)
        grad = mm_nt(dpre_ref[rows, :], gathered(w_ref, ATT, depth))
        unit, scale = norm_parts(x1)
        wide = masked_cot(cot_ref, ids_ref, pack, rows)
        dx1 = wide + norm_back(grad, unit, scale, small[2:3])
        dx1_ref[rows, :] = dx1
        line_ref[2:3, :] += jnp.sum(grad * unit, axis=0, keepdims=True)
        line_ref[3:4, :] += jnp.sum(grad, axis=0, keepdims=True)
        line_ref[4:5, :] += jnp.sum(dx1, axis=0, keepdims=True)
        line_ref[5:6, :] += jnp.sum(wide, axis=0, keepdims=True)


def masked_cot(cot_ref, ids_ref, pack, rows):
    valid = jnp.where(ids_ref[pack] < CROPS, 1.0, 0.0)
    valid = jnp.broadcast_to(valid, (LANES, PACK)).T[:, 0:1]
    return cot_ref[rows, :].astype(F32) * valid


def attention_back(qkv_ref, a_ref, lse_ref, da_ref, dqkv_ref, base, query_side, groups):
    place = lax.broadcasted_iota(jnp.int32, (LANES, PACK), 0)
    head_of = place // HEAD_DIM
    lane = lax.broadcasted_iota(jnp.int32, (PACK, LANES), 1) // HEAD_DIM
    rows = pl.ds(base, PACK)
    none = jnp.zeros((PACK, LANES), BF)

    def split(line):
        high = line.astype(BF).astype(F32)
        rest = line - high
        middle = rest.astype(BF).astype(F32)
        low = rest - middle
        block = jnp.where(
            place == ONES,
            high,
            jnp.where(place == ONES + 1, middle, jnp.where(place == ONES + 2, low, 0.0)),
        )
        return block.astype(BF)

    held, made = {}, {}
    heads = [(g, h) for g in groups for h in range(HEADS_HERE)]

    def load(g):
        at = g * 3 * LANES
        query = qkv_ref[rows, at : at + LANES]
        keys = qkv_ref[rows, at + LANES : at + 2 * LANES]
        values = qkv_ref[rows, at + 2 * LANES : at + 3 * LANES]
        grad = da_ref[rows, g * LANES : (g + 1) * LANES]
        grad_t = grad.T
        both = a_ref[rows, g * LANES : (g + 1) * LANES].T.astype(F32) * grad_t.astype(F32)
        held[g] = (query, keys, values, grad, query.T, keys.T, grad_t, both)

    def scores_of(g, h):
        if g not in held:
            load(g)
        query, keys, values, grad, query_t, keys_t, grad_t, both = held[g]
        part = slice(h * HEAD_DIM, (h + 1) * HEAD_DIM)
        line = g * HEADS_HERE + h
        side = jnp.where(place < ONES, query_side, split(-lse_ref[line : line + 1, rows]))
        scores = mm(keys, jnp.where(head_of == h, query_t, side))
        inner = jnp.sum(both[part], axis=0, keepdims=True)
        pull = mm(values, jnp.where(head_of == h, grad_t, split(-inner)))
        return (scores, pull)

    def finish(g, h, low, dscores):
        query, keys, values, grad, query_t, keys_t, grad_t, both = held[g]
        part = slice(h * HEAD_DIM, (h + 1) * HEAD_DIM)
        dv = mm(low, jnp.where(lane == h, grad, none))
        dk = mm(dscores, jnp.where(lane == h, query, none))
        dq = mm(keys_t[part], dscores)
        if h:
            last = made[g]
            made[g] = (last[0] + [dq], last[1] + dk, last[2] + dv)
        else:
            made[g] = ([dq], dk, dv)
        if h == HEADS_HERE - 1:
            dqs, dk, dv = made[g]
            dqs = jnp.concatenate(dqs + [jnp.zeros((LANES - USED, PACK), F32)], axis=0)
            at = g * 3 * LANES
            dqkv_ref[rows, at : at + LANES] = (dqs.T * SCALE).astype(BF)
            dqkv_ref[rows, at + LANES : at + 2 * LANES] = (dk * LOG_TWO).astype(BF)
            dqkv_ref[rows, at + 2 * LANES : at + 3 * LANES] = dv.astype(BF)

    now = scores_of(*heads[0])
    waiting = None
    for k, head in enumerate(heads):
        later = scores_of(*heads[k + 1]) if k + 1 < len(heads) else None
        if waiting is not None:
            finish(*waiting)
        scores, pull = now
        probs = jnp.exp2(scores)
        waiting = head + (probs.astype(BF), (probs * pull).astype(BF))
        now = later
    finish(*waiting)


def back_kernel(
    place_ref,
    x_ref,
    ids_ref,
    w_ref,
    qkv_ref,
    a_ref,
    lse_ref,
    h1_ref,
    dx1_ref,
    line_ref,
    hidden_ref,
    out_ref,
    grad_ref,
    da_ref,
    dqkv_ref,
    h1t_ref,
    dybt_ref,
    sums_ref,
):
    rows_here, depth = x_ref.shape
    groups = w_ref.shape[0]
    small = small_rows(w_ref)
    sums_ref[...] = jnp.zeros_like(sums_ref)
    sums_ref[SMALL_AT : SMALL_AT + 8, :] = line_ref[...]

    @pl.loop(0, rows_here // PACK)
    def _(pack):
        base = pl.multiple_of(pack * PACK, PACK)
        rows = pl.ds(base, PACK)
        _, query_side = id_lanes(ids_ref[pack])
        low = dx1_ref[rows, :].astype(BF)
        dybt_ref[:, rows] = low.T
        h1t_ref[:, rows] = h1_ref[rows, :].T
        for g in range(groups):
            da_ref[rows, g * LANES : (g + 1) * LANES] = mm(
                low, w_ref[g, :, 3 * LANES : 4 * LANES]
            ).astype(BF)
        attention_back(
            qkv_ref, a_ref, lse_ref, da_ref, dqkv_ref, base, query_side, range(groups)
        )
        width = 3 * LANES
        grad = mm_nt(dqkv_ref[rows, 0:width], w_ref[0, :, 0:width])
        for g in range(1, groups):
            grad += mm_nt(dqkv_ref[rows, g * width : (g + 1) * width], w_ref[g, :, 0:width])
        unit, scale = norm_parts(x_ref[rows, :].astype(F32))
        back = norm_back(grad, unit, scale, small[0:1])
        out_ref[rows, :] = (dx1_ref[rows, :] + back).astype(BF)
        sums_ref[SMALL_AT : SMALL_AT + 1, :] += jnp.sum(grad * unit, axis=0, keepdims=True)
        sums_ref[SMALL_AT + 1 : SMALL_AT + 2, :] += jnp.sum(grad, axis=0, keepdims=True)

    lane = lax.broadcasted_iota(jnp.int32, (depth, LANES), 1)
    for g in range(groups):
        width = 3 * LANES
        sums_ref[HIDDEN_AT : HIDDEN_AT + 1, :] = hidden_ref[g : g + 1, :]
        extra = sums_ref[...].T
        entry = mm(h1t_ref[...], dqkv_ref[:, g * width : (g + 1) * width])
        grad_ref[g, :, 0:LANES] = jnp.where(lane < USED, entry[:, :LANES], extra).astype(BF)
        grad_ref[g, :, LANES:width] = entry[:, LANES:].astype(BF)
        grad_ref[g, :, width : width + LANES] = mm(
            dybt_ref[...], a_ref[:, g * LANES : (g + 1) * LANES]
        ).astype(BF)


def params():
    return pltpu.CompilerParams(vmem_limit_bytes=60 * 2**20)


def whole(shape):
    return pl.BlockSpec(shape, lambda i, place: (0,) * len(shape))


def own_rows(rows, depth):
    return pl.BlockSpec((rows, depth), lambda i, place: (place[0], 0))


def own_ids(packs):
    return pl.BlockSpec((packs, 1, PACK), lambda i, place: (place[0], 0, 0))


def run_key(place, tokens, ids, weights, rows):
    depth = tokens.shape[1]
    groups, _, width = weights.shape
    return pl.pallas_call(
        key_kernel,
        grid_spec=pltpu.PrefetchScalarGridSpec(
            num_scalar_prefetch=1,
            grid=(1,),
            in_specs=[own_rows(rows, depth), own_ids(rows // PACK), whole(weights.shape)],
            out_specs=whole((rows, depth)),
            scratch_shapes=[
                VMEM((rows, groups * 3 * LANES), BF),
                VMEM((rows, groups * LANES), BF),
                VMEM((rows, depth), F32),
                VMEM((rows, depth), BF),
                VMEM((PACK, groups * depth), BF),
                VMEM((1, groups * depth), F32),
            ],
        ),
        out_shape=jax.ShapeDtypeStruct((rows, depth), BF),
        compiler_params=params(),
        name="key_block",
    )(place, tokens, ids, weights)


def run_query(place, tokens, cotangent, ids, weights, rows):
    depth = tokens.shape[1]
    groups = weights.shape[0]
    outs = [
        ((rows, depth), BF),
        ((rows, groups * 3 * LANES), BF),
        ((rows, groups * LANES), BF),
        ((16, rows), F32),
        ((rows, depth), BF),
        ((rows, depth), F32),
        ((groups, depth, 2 * depth), BF),
        ((8, depth), F32),
        ((groups, depth), F32),
    ]
    return pl.pallas_call(
        query_kernel,
        grid_spec=pltpu.PrefetchScalarGridSpec(
            num_scalar_prefetch=1,
            grid=(1,),
            in_specs=[
                own_rows(rows, depth),
                own_rows(rows, depth),
                own_ids(rows // PACK),
                whole(weights.shape),
            ],
            out_specs=[whole(shape) for shape, _ in outs],
            scratch_shapes=[
                VMEM((rows, depth), F32),
                VMEM((rows, depth), BF),
                VMEM((depth + 16, rows), BF),
                VMEM((rows, depth), BF),
                VMEM((depth, rows), BF),
                VMEM((rows, groups * depth), BF),
                VMEM((rows, groups * depth), BF),
                VMEM((1, groups * depth), F32),
            ],
        ),
        out_shape=[jax.ShapeDtypeStruct(shape, kind) for shape, kind in outs],
        compiler_params=params(),
        name="query_block",
    )(place, tokens, cotangent, ids, weights)


def run_back(place, tokens, ids, weights, kept, rows):
    depth = tokens.shape[1]
    groups = weights.shape[0]
    return pl.pallas_call(
        back_kernel,
        grid_spec=pltpu.PrefetchScalarGridSpec(
            num_scalar_prefetch=1,
            grid=(1,),
            in_specs=[own_rows(rows, depth), own_ids(rows // PACK), whole((groups, depth, ATT))]
            + [whole(item.shape) for item in kept],
            out_specs=[whole((rows, depth)), whole((groups, depth, ATT))],
            scratch_shapes=[
                VMEM((rows, groups * LANES), BF),
                VMEM((rows, groups * 3 * LANES), BF),
                VMEM((depth, rows), BF),
                VMEM((depth, rows), BF),
                VMEM((LANES, depth), F32),
            ],
        ),
        out_shape=[
            jax.ShapeDtypeStruct((rows, depth), BF),
            jax.ShapeDtypeStruct((groups, depth, ATT), BF),
        ],
        compiler_params=params(),
        name="back_block",
    )(place, tokens, ids, weights, *kept)


def pack_piece(entry, leave, up, down, small, hidden):
    def fill(block, *extra):
        block = jnp.concatenate([block] + [item.astype(block.dtype) for item in extra], axis=1)
        return jnp.pad(block, ((0, 0), (0, LANES - block.shape[1])))

    parts = [
        fill(entry[:, 0], small.T, hidden[:, None]),
        fill(entry[:, 1]),
        fill(entry[:, 2]),
        fill(leave.T),
        up,
        down.T,
    ]
    return jnp.concatenate([part.astype(BF) for part in parts], axis=1)


def unpack_piece(piece, depth):
    entry = jnp.stack([piece[:, k * LANES : k * LANES + USED] for k in range(3)], axis=1)
    leave = piece[:, 3 * LANES : 3 * LANES + USED].T
    up = piece[:, ATT : ATT + depth]
    down = piece[:, ATT + depth :].T
    small = piece[:, SMALL_AT : SMALL_AT + 6].T
    return (entry, leave, up, down, small, piece[:, HIDDEN_AT])


def adamw(grad, first, second, master, decay, rate):
    moment = BETA_ONE * first + (1.0 - BETA_ONE) * grad
    square = BETA_TWO * second + (1.0 - BETA_TWO) * grad * grad
    ahead = moment / (1.0 - BETA_ONE**STEP)
    spread = square / (1.0 - BETA_TWO**STEP)
    return (
        moment,
        square,
        master - rate * (ahead / (jnp.sqrt(spread) + ADAM_EPS) + decay * master),
    )


DECAYS = (DECAY, DECAY, DECAY, DECAY, 0.0, 0.0)
RATES = (RATE_MATRIX, RATE_EXIT, RATE_MATRIX, RATE_MATRIX, RATE_SMALL, RATE_BIAS)


def finish_plain(grad_att, grad_ffn, masters, firsts, seconds):
    depth = grad_att.shape[1]
    grads = jnp.concatenate([grad_att, grad_ffn], axis=2).astype(F32)
    own = lax.psum_scatter(grads, "tensor", scatter_dimension=0, tiled=False)
    own = lax.psum_scatter(own, "dp", scatter_dimension=0, tiled=True)
    shares = unpack_piece(own, depth)
    copies = float(lax.axis_size("tensor"))
    total = jnp.sum(shares[4] * shares[4]) / copies
    for k in (0, 1, 2, 3, 5):
        total = total + jnp.sum(shares[k] * shares[k])
    norm_value = jnp.sqrt(lax.psum(total, ("dp", "tensor")))
    factor = CLIP / jnp.maximum(norm_value, CLIP)
    outs = []
    for k in range(6):
        outs.extend(
            adamw(shares[k] * factor, firsts[k], seconds[k], masters[k], DECAYS[k], RATES[k])
        )
    return (norm_value, outs)


def spot():
    dp, t = lax.axis_index("dp"), lax.axis_index("tensor")
    return (dp, t)


def flip(value, bits):
    for bit in (1, 2, 4):
        if bits & bit:
            value = value + bit - 2 * bit * ((value // bit) % 2)
    return value


def greet(peers):
    barrier = pltpu.get_barrier_semaphore()
    for peer in peers:
        pl.semaphore_signal(barrier, inc=1, device_id=peer, device_id_type=MESH)
    pl.semaphore_wait(barrier, len(peers))


KEY_PARTS = 3
GATHER_SENDS = 6 + 2 * KEY_PARTS + 5 + 12 + 8 + KEY_PARTS


class Mail:
    def __init__(self, send_sem, recv_sem):
        self.send_sem, self.recv_sem = send_sem, recv_sem
        self.count, self.sent = 0, []

    def send(self, src, dst, peer):
        copy = pltpu.make_async_remote_copy(
            src_ref=src,
            dst_ref=dst,
            send_sem=self.send_sem.at[self.count],
            recv_sem=self.recv_sem.at[self.count],
            device_id=peer,
            device_id_type=MESH,
        )
        copy.start()
        self.count += 1
        self.sent.append(copy)
        return copy

    def close(self):
        for copy in self.sent:
            copy.wait_send()


def arrived(copies):
    for copy in copies:
        copy.wait_recv()


def load_rows(src, dst, t, sem):
    count = dst.shape[0]
    copy = pltpu.make_async_copy(src.at[pl.ds(t * count, count)], dst, sem)
    copy.start()
    return copy


def front_kernel(*refs):
    entry_ref, leave_ref, up_ref, down_ref, small_ref, hidden_ref = refs[0:6]
    key_entry, key_leave, key_up, key_down, key_small, key_hidden = refs[6:12]
    tokens_ref, crops_ref, all_ref, out_ref = refs[12:16]
    x_ref, ids_ref, piece_ref, keys_ref, qkv_ref, a_ref, x1_ref, h1_ref, act_ref, bias_ref = refs[
        16:26
    ]
    send_sem, recv_sem, local_sem = refs[26:]
    dp, t = spot()
    loads = [load_rows(tokens_ref, x_ref, t, local_sem.at[1])]
    loads.append(load_rows(crops_ref, ids_ref, t, local_sem.at[2]))
    far = flip(t, 2)
    core, across = (dp, flip(t, 1)), (dp, far)
    side = (flip(dp, 1), t)
    line = [(flip(dp, 2 * j), t) for j in range(4)]
    mail = Mail(send_sem, recv_sem)
    send = mail.send

    rows, depth = up_ref.shape
    wide = LANES - USED
    extra = [small_ref[...], hidden_ref[...], jnp.zeros((wide - 7, rows), F32)]
    extra = jnp.concatenate(extra, axis=0).T
    blank = jnp.zeros((rows, wide), F32)
    for k, block in enumerate([entry_ref[0], entry_ref[1], entry_ref[2], leave_ref[...]]):
        block = jnp.concatenate([block, blank if k else extra], axis=1)
        piece_ref[:, k * LANES : (k + 1) * LANES] = block.astype(BF)
    piece_ref[:, ATT : ATT + depth] = up_ref[...].astype(BF)
    piece_ref[:, ATT + depth :] = down_ref[...].astype(BF)
    blank = jnp.zeros((wide, depth), BF)
    extra = [key_small[...], key_hidden[...], jnp.zeros((wide - 7, depth), BF)]
    for k, block in enumerate([key_entry[0], key_entry[1], key_entry[2], key_leave[...]]):
        block = jnp.concatenate([block] + ([blank] if k else extra), axis=0)
        keys_ref[t, :, k * LANES : (k + 1) * LANES] = block.T
    keys_ref[t, :, ATT : ATT + depth] = key_up[...]
    keys_ref[t, :, ATT + depth :] = key_down[...].T
    greet([core, across, side] + line[1:])

    own = pltpu.make_async_copy(piece_ref, all_ref.at[t, dp], local_sem.at[0])
    own.start()
    parts = [pl.ds(0, ATT), pl.ds(ATT, depth), pl.ds(ATT + depth, depth)]

    def key_part(group, k):
        return keys_ref.at[group, :, parts[k]]

    to_across = send(piece_ref, all_ref.at[t, dp], across)
    key_core = [send(key_part(t, k), key_part(t, k), core) for k in range(KEY_PARTS)]
    key_across = [send(key_part(t, k), key_part(t, k), across) for k in range(KEY_PARTS)]
    to_line = [[send(piece_ref, all_ref.at[t, dp], line[j])] for j in range(1, 4)]
    to_side = [[send(piece_ref, all_ref.at[t, dp], side)]]
    rest = [send(piece_ref, all_ref.at[t, dp], core)]

    small = small_rows_of(keys_ref[t, :, 0:LANES])
    for copy in loads:
        copy.wait()
    packs = x_ref.shape[0] // PACK
    bases = [pack * PACK for pack in range(packs)]
    masks = [enter(x_ref, ids_ref, small, h1_ref, base, pack) for pack, base in enumerate(bases)]

    def group_step(slot):
        weight = keys_ref[flip(t, slot), :, 0 : 3 * LANES]
        for base, (key_side, _) in zip(bases, masks):
            project(h1_ref[base : base + PACK, :], weight, qkv_ref, key_side, base, slot)
        places = [(slot, base) for base in bases]
        attention(qkv_ref, a_ref, None, places, [query_side for _, query_side in masks])

    group_step(0)
    to_across.wait_recv()
    piece = all_ref.at[far, dp]
    for j in range(1, 4):
        to_line[j - 1].append(send(piece, piece, line[j]))
    to_side[0].append(send(piece, piece, side))
    rest.append(send(piece, piece, core))
    arrived(key_core[:1])
    group_step(1)

    def pass_key(k):
        key_across[k].wait_recv()
        return send(key_part(far, k), key_part(far, k), core)

    key_far = [pass_key(0)]
    group_step(2)

    def pass_line(k):
        group = far if k else t
        for j in range(1, 4):
            other = line[j][0]
            to_line[j - 1][k].wait_recv()
            piece = all_ref.at[group, other]
            if k:
                to_side[j].append(send(piece, piece, side))
            else:
                to_side.append([send(piece, piece, side)])
            rest.append(send(piece, piece, core))

    arrived(key_far)
    group_step(3)
    pass_line(0)
    key_far.append(pass_key(1))
    weight = jnp.concatenate(
        [keys_ref[flip(t, k), :, 3 * LANES : 4 * LANES] for k in range(4)], axis=1
    )
    seconds = [leave(x_ref, weight, small, a_ref, x1_ref, base) for base in bases]
    for base, second in zip(bases, seconds):
        h1_ref[base : base + PACK, :] = second
    arrived(key_core[1:2] + key_far[1:2])
    for k in range(4):
        bias_ref[:, k * depth : (k + 1) * depth] = hidden_line(keys_ref[k, :, 0:LANES])
    for base in bases:
        feed(h1_ref[base : base + PACK, :], keys_ref, bias_ref, act_ref.at[base : base + PACK])
    key_far.append(pass_key(2))
    pass_line(1)
    arrived(key_core[2:] + key_far[2:])
    for base in bases:
        spots = slice(base, base + PACK)
        product = mm_nt(act_ref[spots, :], gathered(keys_ref, ATT + depth, depth))
        out_ref[spots, :] = (x1_ref[spots, :] + product + small[5:6]).astype(BF)
    for j in range(4):
        other = flip(line[j][0], 1)
        for k, group in enumerate((t, far)):
            to_side[j][k].wait_recv()
            piece = all_ref.at[group, other]
            rest.append(send(piece, piece, core))
    arrived(rest)
    mail.close()
    own.wait()


def lay(entry, leave, up, down, small, hidden):
    return [entry.transpose(1, 0, 2), leave.T, up, down.T, small, hidden.reshape(1, -1)]


def run_front(masters, keys, tokens, ids, dp, tensor):
    key_entry, key_leave, key_up, key_down, key_small, key_hidden = keys
    rows, depth = masters[2].shape
    count = tokens.shape[0] // tensor
    width = ATT + 2 * depth
    args = lay(*masters)
    args += [key_entry.transpose(1, 2, 0), key_leave, key_up, key_down, key_small]
    args.append(key_hidden.reshape(1, -1))

    def all_of(shape):
        return pl.BlockSpec(shape, lambda i: (0,) * len(shape))

    anywhere = pl.BlockSpec(memory_space=pl.ANY)
    return pl.pallas_call(
        front_kernel,
        grid=(1,),
        in_specs=[all_of(item.shape) for item in args] + [anywhere] * 2,
        out_specs=[anywhere, all_of((count, depth))],
        scratch_shapes=[
            VMEM((count, depth), BF),
            VMEM((count // PACK, 1, PACK), jnp.int32),
            VMEM((rows, width), BF),
            VMEM((tensor, depth, width), BF),
            VMEM((count, tensor * 3 * LANES), BF),
            VMEM((count, tensor * LANES), BF),
            VMEM((count, depth), F32),
            VMEM((count, depth), BF),
            VMEM((count, tensor * depth), BF),
            VMEM((1, tensor * depth), F32),
            pltpu.SemaphoreType.DMA((GATHER_SENDS,)),
            pltpu.SemaphoreType.DMA((GATHER_SENDS,)),
            pltpu.SemaphoreType.DMA((3,)),
        ],
        out_shape=[
            jax.ShapeDtypeStruct((tensor, dp, rows, width), BF),
            jax.ShapeDtypeStruct((count, depth), BF),
        ],
        compiler_params=pltpu.CompilerParams(
            collective_id=1, has_side_effects=True, vmem_limit_bytes=60 * 2**20
        ),
        name="key_block_and_gather",
    )(*args, tokens, ids)


FINISH_SENDS = (2 + 1 + 4 + 3) + (2 + 8 + 1 + 3) + 3 + 7


def finish_kernel(*refs):
    ga_ref, gb_ref, norm_ref, own_a, own_b = refs[:5]
    rc_a, s0_a, r1_a, s1_a, r2_a, s2_a, r3_a = refs[5:12]
    rc_b, s0_b, r1_b, s1_b, r2_b, s2_b, r3_b = refs[12:19]
    near_ref, far_ref, send_sem, recv_sem = refs[19:]
    dp, t = spot()
    x, c = t // 2, t % 2
    z, y = dp // 2, dp % 2
    core, across = (dp, flip(t, 1)), (dp, flip(t, 2))
    side = (flip(dp, 1), t)
    line = [(flip(dp, 2 * j), t) for j in range(4)]
    greet([(dp, flip(t, k)) for k in (1, 2, 3)] + [(flip(dp, k), t) for k in range(1, 8)])
    mail = Mail(send_sem, recv_sem)
    send = mail.send

    def add(dst, left, right):
        dst[...] = (left[...].astype(F32) + right[...].astype(F32)).astype(BF)

    core_b = [send(gb_ref.at[2 * k + 1 - c], rc_b.at[k], core) for k in range(2)]
    core_a = [send(ga_ref.at[2 * k + 1 - c], rc_a.at[k], core) for k in range(2)]
    arrived(core_b)

    @pl.loop(0, 8)
    def _(d):
        for k in range(2):
            add(s0_b.at[k, d], gb_ref.at[2 * k + c, d], rc_b.at[k, d])

    side_b = [
        send(s0_b.at[k, 2 * w + 1 - y], r1_b.at[k, w], side) for k in range(2) for w in range(4)
    ]
    arrived(core_a)

    @pl.loop(0, 8)
    def _(d):
        for k in range(2):
            add(s0_a.at[k, d], ga_ref.at[2 * k + c, d], rc_a.at[k, d])

    across_a = [send(s0_a.at[1 - x], r1_a, across)]
    arrived(side_b)

    @pl.loop(0, 4)
    def _(w):
        for k in range(2):
            add(s1_b.at[k, w], s0_b.at[k, 2 * w + y], r1_b.at[k, w])

    across_b = [send(s1_b.at[1 - x], r2_b, across)]
    arrived(across_a)

    @pl.loop(0, 8)
    def _(d):
        add(s1_a.at[d], s0_a.at[x, d], r1_a.at[d])

    side_a = [send(s1_a.at[2 * w + 1 - y], r2_a.at[w], side) for w in range(4)]
    arrived(across_b)

    @pl.loop(0, 4)
    def _(w):
        add(s2_b.at[w], s1_b.at[x, w], r2_b.at[w])

    line_b = [send(s2_b.at[line[j][0] // 2], r3_b.at[j - 1], line[j]) for j in range(1, 4)]
    arrived(side_a)

    @pl.loop(0, 4)
    def _(w):
        add(s2_a.at[w], s1_a.at[2 * w + y], r2_a.at[w])

    line_a = [send(s2_a.at[line[j][0] // 2], r3_a.at[j - 1], line[j]) for j in range(1, 4)]
    arrived(line_b)
    grad_b = s2_b[z].astype(F32)
    for j in range(3):
        grad_b = grad_b + r3_b[j].astype(F32)
    arrived(line_a)
    grad_a = s2_a[z].astype(F32)
    for j in range(3):
        grad_a = grad_a + r3_a[j].astype(F32)

    rows, width = grad_a.shape
    depth = grad_b.shape[1] // 2
    lane = lax.broadcasted_iota(jnp.int32, (rows, LANES), 1)
    total = jnp.zeros((8, LANES), F32)

    def fold(block):
        out = block[0:8]
        for k in range(8, rows, 8):
            out = out + block[k : k + 8]
        return out

    once = jnp.where(t == 0, 1.0, 0.0)
    small_share = jnp.where(lane < HIDDEN_AT, once, jnp.where(lane == HIDDEN_AT, 1.0, 0.0))
    for k in range(4):
        block = grad_a[:, k * LANES : (k + 1) * LANES]
        share = jnp.where(lane < USED, 1.0, small_share if k == 0 else 0.0)
        total = total + fold(block * block * share)
    for k in range(2 * depth // LANES):
        block = grad_b[:, k * LANES : (k + 1) * LANES]
        total = total + fold(block * block)
    near_ref[t] = total
    near = [send(near_ref.at[t], near_ref.at[t], (dp, flip(t, k))) for k in (1, 2, 3)]
    arrived(near)
    far_ref[dp] = (near_ref[0] + near_ref[1]) + (near_ref[2] + near_ref[3])
    far = [send(far_ref.at[dp], far_ref.at[dp], (flip(dp, k), t)) for k in range(1, 8)]
    arrived(far)
    total = far_ref[0]
    for k in range(1, 8):
        total = total + far_ref[k]
    total = jnp.sum(total, axis=0, keepdims=True)
    norm_value = jnp.sqrt(jnp.sum(total, axis=1, keepdims=True))
    norm_ref[...] = jnp.broadcast_to(norm_value, norm_ref.shape)
    own_a[...] = grad_a
    own_b[...] = grad_b
    mail.close()


def run_finish(grad_att, grad_ffn):
    groups, dp, rows, wide_a = grad_att.shape
    wide_b = grad_ffn.shape[3]
    shapes = [
        jax.ShapeDtypeStruct((8, LANES), F32),
        jax.ShapeDtypeStruct((rows, wide_a), F32),
        jax.ShapeDtypeStruct((rows, wide_b), F32),
    ]
    scratch = []
    for wide, first in ((wide_a, (8,)), (wide_b, (2, 4))):
        scratch.append(VMEM((2, 8, rows, wide), BF))
        scratch.append(VMEM((2, 8, rows, wide), BF))
        scratch.append(VMEM(first + (rows, wide), BF))
        scratch.append(VMEM(first + (rows, wide), BF))
        scratch.append(VMEM((4, rows, wide), BF))
        scratch.append(VMEM((4, rows, wide), BF))
        scratch.append(VMEM((3, rows, wide), BF))
    scratch.append(VMEM((4, 8, LANES), F32))
    scratch.append(VMEM((8, 8, LANES), F32))
    scratch.append(pltpu.SemaphoreType.DMA((FINISH_SENDS,)))
    scratch.append(pltpu.SemaphoreType.DMA((FINISH_SENDS,)))
    spec = pl.BlockSpec(memory_space=VMEM)
    return pl.pallas_call(
        finish_kernel,
        in_specs=[spec] * 2,
        out_specs=[spec] * 3,
        out_shape=shapes,
        scratch_shapes=scratch,
        compiler_params=pltpu.CompilerParams(
            collective_id=2, has_side_effects=True, vmem_limit_bytes=60 * 2**20
        ),
        name="finish",
    )(grad_att, grad_ffn)


def step_kernel(norm_ref, ga_ref, gb_ref, *refs):
    masters, firsts, seconds = refs[0:6], refs[6:12], refs[12:18]
    value_ref, outs = refs[18], refs[19:]
    norm_value = norm_ref[0:1, 0:1]
    value_ref[...] = norm_value
    factor = CLIP / jnp.maximum(norm_value, CLIP)
    grad_a = ga_ref[...] * factor
    grad_b = gb_ref[...] * factor
    depth = grad_b.shape[1] // 2

    def update(k, at, grad):
        new = adamw(grad, firsts[k][at], seconds[k][at], masters[k][at], DECAYS[k], RATES[k])
        for j in range(3):
            outs[3 * k + j][at] = new[j]

    for j in range(3):
        update(0, j, grad_a[:, j * LANES : j * LANES + USED])
    update(1, slice(None), grad_a[:, 3 * LANES : 3 * LANES + USED])
    update(2, slice(None), grad_b[:, :depth])
    update(3, slice(None), grad_b[:, depth:])
    lines = grad_a[:, :LANES].T
    update(4, slice(None), lines[SMALL_AT : SMALL_AT + 6])
    update(5, slice(None), lines[HIDDEN_AT : HIDDEN_AT + 1])


def run_step(norm_tile, grad_a, grad_b, masters, firsts, seconds):
    state = lay(*masters) + lay(*firsts) + lay(*seconds)
    shapes = [jax.ShapeDtypeStruct((1, 1), F32)]
    for item in state[:6]:
        shapes.extend([jax.ShapeDtypeStruct(item.shape, F32)] * 3)
    spec = pl.BlockSpec(memory_space=VMEM)
    result = pl.pallas_call(
        step_kernel,
        in_specs=[spec] * 21,
        out_specs=[spec] * 19,
        out_shape=shapes,
        name="optimizer_step",
    )(norm_tile, grad_a, grad_b, *state)
    outs = list(result[1:])
    for k in range(3):
        outs[k] = outs[k].transpose(1, 0, 2)
        outs[3 + k] = outs[3 + k].T
        outs[9 + k] = outs[9 + k].T
        outs[15 + k] = outs[15 + k].reshape(-1)
    return (result[0].reshape(()), outs)


def join_kernel(place_ref, own_ref, core_ref, far_ref, both_ref, out_ref):
    for k, ref in enumerate((own_ref, core_ref, far_ref, both_ref)):

        @pl.when(pl.program_id(0) == k)
        def _():
            out_ref[...] = ref[...]


def spread_rows(place, own):
    def swap(item, bits):
        return lax.ppermute(item, "tensor", [(i, i ^ bits) for i in range(4)])

    far = swap(own, 2)
    near = swap(own, 1)
    both = swap(far, 1)
    rows, depth = own.shape

    def spot_of(i, place):
        return (place[0] + i - 2 * (i % 2) * (place[0] % 2) - 4 * (i // 2) * (place[0] // 2), 0)

    return pl.pallas_call(
        join_kernel,
        grid_spec=pltpu.PrefetchScalarGridSpec(
            num_scalar_prefetch=1,
            grid=(4,),
            in_specs=[pl.BlockSpec((rows, depth), lambda i, place: (0, 0))] * 4,
            out_specs=pl.BlockSpec((rows, depth), spot_of),
        ),
        out_shape=jax.ShapeDtypeStruct((4 * rows, depth), BF),
        compiler_params=pltpu.CompilerParams(vmem_limit_bytes=32 * 2**20),
        name="join_rows",
    )(place, own, near, far, both)


def on_device(*args):
    tokens, crop_ids, cotangent, key_tokens = args[:4]
    masters, firsts, seconds, keys = args[4:10], args[10:16], args[16:22], args[22:28]
    count, groups = lax.axis_size("dp"), lax.axis_size("tensor")
    direct = count == 8 and groups == 4
    rows, depth = tokens.shape[0] // groups, tokens.shape[1]
    place = lax.axis_index("tensor").astype(jnp.int32)[None]
    ids = crop_ids.reshape(-1, 1, PACK)
    if direct:
        weights, key_rows = run_front(masters, keys, key_tokens, ids, count, groups)
        weights = weights.reshape(groups, depth, -1)
    else:
        key_weights = lax.all_gather(pack_piece(*keys), "tensor", axis=0)
        weights = lax.all_gather(pack_piece(*masters), "dp", axis=0, tiled=True)
        weights = lax.all_gather(weights, "tensor", axis=0)
        key_rows = run_key(place, key_tokens, ids, key_weights, rows)

    def spread(own):
        if direct:
            return spread_rows(place, own)
        return lax.all_gather(own, "tensor", axis=0, tiled=True)

    key_out = spread(key_rows)
    forward = run_query(place, tokens, cotangent, ids, weights, rows)
    block_out = spread(forward[0])
    qkv, a, lse, h1, dx1, grad_ffn, lines, hidden = forward[1:]
    grad_rows, grad_att = run_back(
        place, tokens, ids, weights, (qkv, a, lse, h1, dx1, lines, hidden), rows
    )
    input_grad = spread(grad_rows)
    if direct:
        grads = run_finish(
            grad_att.reshape(groups, count, depth // count, -1),
            grad_ffn.reshape(groups, count, depth // count, -1),
        )
        norm_value, outs = run_step(*grads, masters, firsts, seconds)
    else:
        norm_value, outs = finish_plain(grad_att, grad_ffn, masters, firsts, seconds)
    return (block_out, key_out, input_grad, norm_value, *outs)


def solution(mesh):
    rows, line = P("dp", None), P("dp")
    entry, leave, up, down = P("dp", None, "tensor"), P("tensor", "dp"), P("dp", "tensor"), P("tensor", "dp")
    state = (entry, leave, up, down, P(None, "dp"), P(("tensor", "dp")))
    keys = (P(None, None, "tensor"), P("tensor", None), P(None, "tensor"), P("tensor", None), P(), P("tensor"))
    outs = tuple(spec for spec in state for _ in range(3))
    return jax.shard_map(
        on_device,
        mesh=mesh,
        in_specs=(rows, line, rows, rows) + state * 3 + keys,
        out_specs=(rows, rows, rows, P()) + outs,
        check_vma=False,
    )
```

```python
import math
from functools import partial

import jax
import jax.numpy as jnp
from jax import lax
from jax.experimental import pallas as pl
from jax.experimental.pallas import tpu as pltpu
from jax.sharding import PartitionSpec as P

HEAD_DIM = 32
PACK = 512
CROPS = 5
STEP = 10
LN_EPS = 1e-06
CLIP = 1.0
RATE_MATRIX = 0.03
RATE_EXIT = 0.2
RATE_SMALL = 0.5
RATE_BIAS = 0.3
BETA_ONE = 0.9
BETA_TWO = 0.999
ADAM_EPS = 1e-08
DECAY = 0.05
MASKED = -1e30

SCALE = HEAD_DIM ** (-0.5)
EXP_SCALE = SCALE * math.log2(math.e)
LOG_TWO = math.log(2.0)
LANES = 128
TILE = 2 * LANES
PIECE = 64
HEADS_HERE = 3
USED = HEADS_HERE * HEAD_DIM
ONES = USED + CROPS + 1
ATT = 4 * LANES
SMALL_AT = USED
HIDDEN_AT = USED + 6
MESH = pl.DeviceIdType.MESH
BF = jnp.bfloat16
F32 = jnp.float32
VMEM = pltpu.VMEM
NT = (((1,), (1,)), ((), ()))
TN = (((0,), (0,)), ((), ()))

def mm(left, right):
    return jnp.dot(left, right, preferred_element_type=F32)


def mm_nt(left, right):
    return lax.dot_general(left, right, NT, preferred_element_type=F32)


def norm_parts(values):
    mean = jnp.mean(values, axis=1, keepdims=True)
    centred = values - mean
    spread = jnp.mean(centred * centred, axis=1, keepdims=True)
    scale = lax.rsqrt(spread + LN_EPS)
    return (centred * scale, scale)


def norm_back(grad, unit, scale, gain):
    scaled = grad * gain
    first = jnp.mean(scaled, axis=1, keepdims=True)
    second = jnp.mean(scaled * unit, axis=1, keepdims=True)
    return scale * (scaled - first - unit * second)


def below(pre):
    return 0.5 + 0.5 * lax.erf(pre * math.sqrt(0.5))


def below_and_slope(pre):
    phi = below(pre)
    bell = jnp.exp2((pre * (-0.5 * math.log2(math.e))) * pre)
    return (phi, phi + (pre * (1.0 / math.sqrt(2.0 * math.pi))) * bell)


def small_rows_of(weight):
    return weight.astype(F32).T[SMALL_AT : SMALL_AT + 6]


def hidden_line(weight):
    return weight.astype(F32).T[HIDDEN_AT : HIDDEN_AT + 1]


def small_rows(w_ref):
    return small_rows_of(w_ref[0, :, 0:LANES])


def hidden_row(w_ref, t):
    return hidden_line(w_ref[t, :, 0:LANES])


def id_lanes(ids):
    place = lax.broadcasted_iota(jnp.int32, (LANES, PACK), 0)
    match = (place - USED) == ids
    ones = (place >= ONES) & (place < ONES + 3)
    key_side = jnp.where(match | ones, 1.0, 0.0).T
    crop = (place >= USED) & (place < ONES)
    query_side = jnp.where(crop & jnp.logical_not(match), MASKED, 0.0).astype(BF)
    return (key_side, query_side)


def attention(qkv_ref, a_ref, lse_ref, places, sides):
    place = lax.broadcasted_iota(jnp.int32, (LANES, PACK), 0) // HEAD_DIM
    ones = jnp.ones((16, PACK), BF)
    blank = jnp.zeros((LANES - USED, PACK), F32)
    heads = [(k, h) for k in range(len(places)) for h in range(HEADS_HERE)]
    held, outs = {}, {}

    def scores_of(k, h):
        if k not in held:
            slot, base = places[k]
            rows, at = pl.ds(base, PACK), slot * 3 * LANES
            query = qkv_ref[rows, at : at + LANES].T
            keys = qkv_ref[rows, at + LANES : at + 2 * LANES]
            values = qkv_ref[rows, at + 2 * LANES : at + 3 * LANES].T
            held[k] = (query, keys, values)
        query, keys, _ = held[k]
        return mm(keys, jnp.where(place == h, query, sides[k]))

    def mix(k, h, top, probs):
        slot, base = places[k]
        rows = pl.ds(base, PACK)
        values = held[k][2][h * HEAD_DIM : (h + 1) * HEAD_DIM]
        mixed = mm(jnp.concatenate([values, ones], axis=0), probs)
        total = mixed[HEAD_DIM : HEAD_DIM + 1]
        outs[(k, h)] = mixed[:HEAD_DIM] * (1.0 / total)
        if lse_ref is not None:
            line = slot * HEADS_HERE + h
            lse_ref[line : line + 1, rows] = top + jnp.log2(total)
        if h == HEADS_HERE - 1:
            parts = [outs[(k, n)] for n in range(HEADS_HERE)] + [blank]
            a_ref[rows, slot * LANES : (slot + 1) * LANES] = (
                jnp.concatenate(parts, axis=0).T.astype(BF)
            )

    scores = scores_of(*heads[0])
    waiting = None
    for n, head in enumerate(heads):
        later = scores_of(*heads[n + 1]) if n + 1 < len(heads) else None
        if waiting is not None:
            mix(*waiting)
        top = jnp.max(scores, axis=0, keepdims=True)
        waiting = head + (top, jnp.exp2(scores - top).astype(BF))
        scores = later
    mix(*waiting)


def enter(x_ref, ids_ref, small, h1_ref, base, pack):
    rows = pl.ds(base, PACK)
    values = x_ref[rows, :].astype(F32)
    unit, _ = norm_parts(values)
    first = (unit * small[0:1] + small[1:2]).astype(BF)
    h1_ref[rows, :] = first
    return id_lanes(ids_ref[pack])


def project(first, weight, qkv_ref, key_side, base, slot):
    rows, at = pl.ds(base, PACK), slot * 3 * LANES
    packed = mm(first, weight)
    qkv_ref[rows, at : at + LANES] = (packed[:, :LANES] * EXP_SCALE).astype(BF)
    for k in (1, 2):
        part = packed[:, k * LANES : (k + 1) * LANES] + key_side
        qkv_ref[rows, at + k * LANES : at + (k + 1) * LANES] = part.astype(BF)


def project_all(first, w_ref, qkv_ref, key_side, base):
    for g in range(w_ref.shape[0]):
        project(first, w_ref[g, :, 0 : 3 * LANES], qkv_ref, key_side, base, g)


def leaving(w_ref):
    return gathered(w_ref, 3 * LANES, LANES)


def leave(x_ref, weight, small, a_ref, x1_ref, base):
    rows = pl.ds(base, PACK)
    branch = mm_nt(a_ref[rows, :], weight)
    x1 = x_ref[rows, :].astype(F32) + branch + small[4:5]
    x1_ref[rows, :] = x1
    unit, _ = norm_parts(x1)
    return (unit * small[2:3] + small[3:4]).astype(BF)


def gathered(w_ref, at, width):
    parts = [w_ref[t, :, at : at + width] for t in range(w_ref.shape[0])]
    return jnp.concatenate(parts, axis=1)


def tile_of(w_ref, j, first):
    depth = w_ref.shape[1]
    per = depth // LANES
    parts = []
    for b in range(j * TILE // LANES, (j + 1) * TILE // LANES):
        at = first + (b % per) * LANES
        parts.append(w_ref[b // per, :, at : at + LANES])
    return jnp.concatenate(parts, axis=1)


def key_kernel(
    place_ref, x_ref, ids_ref, w_ref, out_ref, qkv_ref, a_ref, x1_ref, h1_ref, act_ref, bias_ref
):
    rows_here, depth = x_ref.shape
    groups = w_ref.shape[0]
    small = small_rows(w_ref)
    for t in range(groups):
        bias_ref[:, t * depth : (t + 1) * depth] = hidden_row(w_ref, t)

    @pl.loop(0, rows_here // PACK)
    def _(pack):
        base = pl.multiple_of(pack * PACK, PACK)
        rows = pl.ds(base, PACK)
        key_side, query_side = enter(x_ref, ids_ref, small, h1_ref, base, pack)
        project_all(h1_ref[rows, :], w_ref, qkv_ref, key_side, base)
        attention(qkv_ref, a_ref, None, [(g, base) for g in range(groups)], [query_side] * groups)
        second = leave(x_ref, leaving(w_ref), small, a_ref, x1_ref, base)
        feed(second, w_ref, bias_ref, act_ref)
        product = mm_nt(act_ref[...], gathered(w_ref, ATT + depth, depth))
        out_ref[rows, :] = (x1_ref[rows, :] + product + small[5:6]).astype(BF)


def feed(second, w_ref, bias_ref, act_ref, first=ATT):
    tiles = act_ref.shape[1] // TILE
    pre = mm(second, tile_of(w_ref, 0, first))
    for j in range(tiles):
        later = mm(second, tile_of(w_ref, j + 1, first)) if j + 1 < tiles else None
        cols = slice(j * TILE, (j + 1) * TILE)
        bias = bias_ref[:, cols]
        for i in range(0, pre.shape[0], PIECE):
            piece = pre[i : i + PIECE] + bias
            act_ref[i : i + PIECE, cols] = (piece * below(piece)).astype(BF)
        pre = later


def query_kernel(
    place_ref,
    x_ref,
    cot_ref,
    ids_ref,
    w_ref,
    out_ref,
    qkv_ref,
    a_ref,
    lse_ref,
    h1_ref,
    dx1_ref,
    grad_ref,
    line_ref,
    hidden_ref,
    x1_ref,
    h2_ref,
    h2t_ref,
    eb_ref,
    ebt_ref,
    act_ref,
    dpre_ref,
    bias_ref,
):
    rows_here, depth = x_ref.shape
    groups = w_ref.shape[0]
    small = small_rows(w_ref)
    for t in range(groups):
        bias_ref[:, t * depth : (t + 1) * depth] = hidden_row(w_ref, t)

    lse_ref[...] = jnp.zeros_like(lse_ref)
    line_ref[...] = jnp.zeros_like(line_ref)
    h2t_ref[depth:, :] = jnp.ones((h2t_ref.shape[0] - depth, rows_here), BF)

    @pl.loop(0, rows_here // PACK)
    def _(pack):
        base = pl.multiple_of(pack * PACK, PACK)
        rows = pl.ds(base, PACK)
        key_side, query_side = enter(x_ref, ids_ref, small, h1_ref, base, pack)
        project_all(h1_ref[rows, :], w_ref, qkv_ref, key_side, base)
        attention(
            qkv_ref, a_ref, lse_ref, [(g, base) for g in range(groups)], [query_side] * groups
        )
        second = leave(x_ref, leaving(w_ref), small, a_ref, x1_ref, base)
        h2_ref[rows, :] = second
        h2t_ref[0:depth, rows] = second.T
        low = masked_cot(cot_ref, ids_ref, pack, rows).astype(BF)
        eb_ref[rows, :] = low
        ebt_ref[:, rows] = low.T

    feed_back(
        w_ref, ATT, h2_ref, h2t_ref, eb_ref, ebt_ref, bias_ref, act_ref, dpre_ref, grad_ref, hidden_ref
    )

    @pl.loop(0, rows_here // PACK)
    def _(pack):
        rows = pl.ds(pl.multiple_of(pack * PACK, PACK), PACK)
        x1 = x1_ref[rows, :]
        product = mm_nt(act_ref[rows, :], gathered(w_ref, ATT + depth, depth))
        out_ref[rows, :] = (x1 + product + small[5:6]).astype(BF)
        grad = mm_nt(dpre_ref[rows, :], gathered(w_ref, ATT, depth))
        unit, scale = norm_parts(x1)
        wide = masked_cot(cot_ref, ids_ref, pack, rows)
        dx1 = wide + norm_back(grad, unit, scale, small[2:3])
        dx1_ref[rows, :] = dx1
        line_ref[2:3, :] += jnp.sum(grad * unit, axis=0, keepdims=True)
        line_ref[3:4, :] += jnp.sum(grad, axis=0, keepdims=True)
        line_ref[4:5, :] += jnp.sum(dx1, axis=0, keepdims=True)
        line_ref[5:6, :] += jnp.sum(wide, axis=0, keepdims=True)


def feed_back(
    w_ref, first, h2_ref, h2t_ref, eb_ref, ebt_ref, bias_ref, act_ref, dpre_ref, grad_ref, hidden_ref
):
    rows_here, depth = h2_ref.shape
    tiles = act_ref.shape[1] // TILE
    per = depth // LANES
    step = PACK
    units = [(j, r) for j in range(tiles) for r in range(rows_here // step)]

    def start(unit):
        j, r = unit
        rows = slice(r * step, (r + 1) * step)
        pre = mm(h2_ref[rows, :], tile_of(w_ref, j, first))
        return (pre, mm(eb_ref[rows, :], tile_of(w_ref, j, first + depth)))

    now = start(units[0])
    for k, (j, r) in enumerate(units):
        later = start(units[k + 1]) if k + 1 < len(units) else None
        cols = slice(j * TILE, (j + 1) * TILE)
        bias = bias_ref[:, cols]
        pre, da = now
        for i in range(0, step, PIECE):
            rows = slice(r * step + i, r * step + i + PIECE)
            piece = pre[i : i + PIECE] + bias
            phi, slope = below_and_slope(piece)
            act_ref[rows, cols] = (piece * phi).astype(BF)
            dpre_ref[rows, cols] = (da[i : i + PIECE] * slope).astype(BF)
        now = later
        if (r + 1) * step == rows_here:
            gup = mm(h2t_ref[...], dpre_ref[:, cols])
            gdown = mm(ebt_ref[...], act_ref[:, cols])
            for n, b in enumerate((2 * j, 2 * j + 1)):
                t, o = b // per, (b % per) * LANES
                part = slice(n * LANES, (n + 1) * LANES)
                grad_ref[t, :, o : o + LANES] = gup[:depth, part].astype(BF)
                grad_ref[t, :, depth + o : depth + o + LANES] = gdown[:, part].astype(BF)
                hidden_ref[t : t + 1, o : o + LANES] = gup[depth : depth + 1, part]


def masked_cot(cot_ref, ids_ref, pack, rows):
    valid = jnp.where(ids_ref[pack] < CROPS, 1.0, 0.0)
    valid = jnp.broadcast_to(valid, (LANES, PACK)).T[:, 0:1]
    return cot_ref[rows, :].astype(F32) * valid


def attention_back(qkv_ref, a_ref, lse_ref, da_ref, dqkv_ref, places, sides):
    place = lax.broadcasted_iota(jnp.int32, (LANES, PACK), 0)
    head_of = place // HEAD_DIM
    lane = lax.broadcasted_iota(jnp.int32, (PACK, LANES), 1) // HEAD_DIM
    none = jnp.zeros((PACK, LANES), BF)

    def split(line):
        high = line.astype(BF).astype(F32)
        rest = line - high
        middle = rest.astype(BF).astype(F32)
        low = rest - middle
        block = jnp.where(
            place == ONES,
            high,
            jnp.where(place == ONES + 1, middle, jnp.where(place == ONES + 2, low, 0.0)),
        )
        return block.astype(BF)

    held, made = {}, {}
    heads = [(k, h) for k in range(len(places)) for h in range(HEADS_HERE)]

    def load(k):
        slot, base, da_at, _ = places[k]
        rows, at = pl.ds(base, PACK), slot * 3 * LANES
        query = qkv_ref[rows, at : at + LANES]
        keys = qkv_ref[rows, at + LANES : at + 2 * LANES]
        values = qkv_ref[rows, at + 2 * LANES : at + 3 * LANES]
        grad = da_ref[rows, da_at * LANES : (da_at + 1) * LANES]
        grad_t = grad.T
        mixed = a_ref[rows, slot * LANES : (slot + 1) * LANES].T
        both = mixed.astype(F32) * grad_t.astype(F32)
        held[k] = (query, keys, values, grad, query.T, keys.T, grad_t, both)

    def scores_of(k, h):
        if k not in held:
            load(k)
        slot, base, _, _ = places[k]
        query, keys, values, grad, query_t, keys_t, grad_t, both = held[k]
        part = slice(h * HEAD_DIM, (h + 1) * HEAD_DIM)
        line = slot * HEADS_HERE + h
        lse = lse_ref[line : line + 1, pl.ds(base, PACK)]
        side = jnp.where(place < ONES, sides[k], split(-lse))
        scores = mm(keys, jnp.where(head_of == h, query_t, side))
        inner = jnp.sum(both[part], axis=0, keepdims=True)
        pull = mm(values, jnp.where(head_of == h, grad_t, split(-inner)))
        return (scores, pull)

    def finish(k, h, low, dscores):
        query, keys, values, grad, query_t, keys_t, grad_t, both = held[k]
        part = slice(h * HEAD_DIM, (h + 1) * HEAD_DIM)
        dv = mm(low, jnp.where(lane == h, grad, none))
        dk = mm(dscores, jnp.where(lane == h, query, none))
        dq = mm(keys_t[part], dscores)
        if h:
            last = made[k]
            made[k] = (last[0] + [dq], last[1] + dk, last[2] + dv)
        else:
            made[k] = ([dq], dk, dv)
        if h == HEADS_HERE - 1:
            dqs, dk, dv = made[k]
            dqs = jnp.concatenate(dqs + [jnp.zeros((LANES - USED, PACK), F32)], axis=0)
            _, base, _, slot = places[k]
            rows, at = pl.ds(base, PACK), slot * 3 * LANES
            dqkv_ref[rows, at : at + LANES] = (dqs.T * SCALE).astype(BF)
            dqkv_ref[rows, at + LANES : at + 2 * LANES] = (dk * LOG_TWO).astype(BF)
            dqkv_ref[rows, at + 2 * LANES : at + 3 * LANES] = dv.astype(BF)

    now = scores_of(*heads[0])
    waiting = None
    for n, head in enumerate(heads):
        later = scores_of(*heads[n + 1]) if n + 1 < len(heads) else None
        if waiting is not None:
            finish(*waiting)
        scores, pull = now
        probs = jnp.exp2(scores)
        waiting = head + (probs.astype(BF), (probs * pull).astype(BF))
        now = later
    finish(*waiting)


def back_kernel(
    place_ref,
    x_ref,
    ids_ref,
    w_ref,
    qkv_ref,
    a_ref,
    lse_ref,
    h1_ref,
    dx1_ref,
    line_ref,
    hidden_ref,
    out_ref,
    grad_ref,
    da_ref,
    dqkv_ref,
    h1t_ref,
    dybt_ref,
    sums_ref,
):
    rows_here, depth = x_ref.shape
    groups = w_ref.shape[0]
    small = small_rows(w_ref)
    sums_ref[...] = jnp.zeros_like(sums_ref)
    sums_ref[SMALL_AT : SMALL_AT + 8, :] = line_ref[...]

    @pl.loop(0, rows_here // PACK)
    def _(pack):
        base = pl.multiple_of(pack * PACK, PACK)
        rows = pl.ds(base, PACK)
        _, query_side = id_lanes(ids_ref[pack])
        low = dx1_ref[rows, :].astype(BF)
        dybt_ref[:, rows] = low.T
        h1t_ref[:, rows] = h1_ref[rows, :].T
        for g in range(groups):
            da_ref[rows, g * LANES : (g + 1) * LANES] = mm(
                low, w_ref[g, :, 3 * LANES : 4 * LANES]
            ).astype(BF)
        places = [(g, base, g, g) for g in range(groups)]
        attention_back(qkv_ref, a_ref, lse_ref, da_ref, dqkv_ref, places, [query_side] * groups)
        width = 3 * LANES
        grad = mm_nt(dqkv_ref[rows, 0:width], w_ref[0, :, 0:width])
        for g in range(1, groups):
            grad += mm_nt(dqkv_ref[rows, g * width : (g + 1) * width], w_ref[g, :, 0:width])
        unit, scale = norm_parts(x_ref[rows, :].astype(F32))
        back = norm_back(grad, unit, scale, small[0:1])
        out_ref[rows, :] = (dx1_ref[rows, :] + back).astype(BF)
        sums_ref[SMALL_AT : SMALL_AT + 1, :] += jnp.sum(grad * unit, axis=0, keepdims=True)
        sums_ref[SMALL_AT + 1 : SMALL_AT + 2, :] += jnp.sum(grad, axis=0, keepdims=True)

    lane = lax.broadcasted_iota(jnp.int32, (depth, LANES), 1)
    for g in range(groups):
        width = 3 * LANES
        sums_ref[HIDDEN_AT : HIDDEN_AT + 1, :] = hidden_ref[g : g + 1, :]
        extra = sums_ref[...].T
        entry = mm(h1t_ref[...], dqkv_ref[:, g * width : (g + 1) * width])
        grad_ref[g, :, 0:LANES] = jnp.where(lane < USED, entry[:, :LANES], extra).astype(BF)
        grad_ref[g, :, LANES:width] = entry[:, LANES:].astype(BF)
        grad_ref[g, :, width : width + LANES] = mm(
            dybt_ref[...], a_ref[:, g * LANES : (g + 1) * LANES]
        ).astype(BF)


def params():
    return pltpu.CompilerParams(vmem_limit_bytes=60 * 2**20)


def whole(shape):
    return pl.BlockSpec(shape, lambda i, place: (0,) * len(shape))


def own_rows(rows, depth):
    return pl.BlockSpec((rows, depth), lambda i, place: (place[0], 0))


def own_ids(packs):
    return pl.BlockSpec((packs, 1, PACK), lambda i, place: (place[0], 0, 0))


def run_key(place, tokens, ids, weights, rows):
    depth = tokens.shape[1]
    groups, _, width = weights.shape
    return pl.pallas_call(
        key_kernel,
        grid_spec=pltpu.PrefetchScalarGridSpec(
            num_scalar_prefetch=1,
            grid=(1,),
            in_specs=[own_rows(rows, depth), own_ids(rows // PACK), whole(weights.shape)],
            out_specs=whole((rows, depth)),
            scratch_shapes=[
                VMEM((rows, groups * 3 * LANES), BF),
                VMEM((rows, groups * LANES), BF),
                VMEM((rows, depth), F32),
                VMEM((rows, depth), BF),
                VMEM((PACK, groups * depth), BF),
                VMEM((1, groups * depth), F32),
            ],
        ),
        out_shape=jax.ShapeDtypeStruct((rows, depth), BF),
        compiler_params=params(),
        name="key_block",
    )(place, tokens, ids, weights)


def run_query(place, tokens, cotangent, ids, weights, rows):
    depth = tokens.shape[1]
    groups = weights.shape[0]
    outs = [
        ((rows, depth), BF),
        ((rows, groups * 3 * LANES), BF),
        ((rows, groups * LANES), BF),
        ((16, rows), F32),
        ((rows, depth), BF),
        ((rows, depth), F32),
        ((groups, depth, 2 * depth), BF),
        ((8, depth), F32),
        ((groups, depth), F32),
    ]
    return pl.pallas_call(
        query_kernel,
        grid_spec=pltpu.PrefetchScalarGridSpec(
            num_scalar_prefetch=1,
            grid=(1,),
            in_specs=[
                own_rows(rows, depth),
                own_rows(rows, depth),
                own_ids(rows // PACK),
                whole(weights.shape),
            ],
            out_specs=[whole(shape) for shape, _ in outs],
            scratch_shapes=[
                VMEM((rows, depth), F32),
                VMEM((rows, depth), BF),
                VMEM((depth + 16, rows), BF),
                VMEM((rows, depth), BF),
                VMEM((depth, rows), BF),
                VMEM((rows, groups * depth), BF),
                VMEM((rows, groups * depth), BF),
                VMEM((1, groups * depth), F32),
            ],
        ),
        out_shape=[jax.ShapeDtypeStruct(shape, kind) for shape, kind in outs],
        compiler_params=params(),
        name="query_block",
    )(place, tokens, cotangent, ids, weights)


def run_back(place, tokens, ids, weights, kept, rows):
    depth = tokens.shape[1]
    groups = weights.shape[0]
    return pl.pallas_call(
        back_kernel,
        grid_spec=pltpu.PrefetchScalarGridSpec(
            num_scalar_prefetch=1,
            grid=(1,),
            in_specs=[own_rows(rows, depth), own_ids(rows // PACK), whole((groups, depth, ATT))]
            + [whole(item.shape) for item in kept],
            out_specs=[whole((rows, depth)), whole((groups, depth, ATT))],
            scratch_shapes=[
                VMEM((rows, groups * LANES), BF),
                VMEM((rows, groups * 3 * LANES), BF),
                VMEM((depth, rows), BF),
                VMEM((depth, rows), BF),
                VMEM((LANES, depth), F32),
            ],
        ),
        out_shape=[
            jax.ShapeDtypeStruct((rows, depth), BF),
            jax.ShapeDtypeStruct((groups, depth, ATT), BF),
        ],
        compiler_params=params(),
        name="back_block",
    )(place, tokens, ids, weights, *kept)


def pack_piece(entry, leave, up, down, small, hidden):
    def fill(block, *extra):
        block = jnp.concatenate([block] + [item.astype(block.dtype) for item in extra], axis=1)
        return jnp.pad(block, ((0, 0), (0, LANES - block.shape[1])))

    parts = [
        fill(entry[:, 0], small.T, hidden[:, None]),
        fill(entry[:, 1]),
        fill(entry[:, 2]),
        fill(leave.T),
        up,
        down.T,
    ]
    return jnp.concatenate([part.astype(BF) for part in parts], axis=1)


def unpack_piece(piece, depth):
    entry = jnp.stack([piece[:, k * LANES : k * LANES + USED] for k in range(3)], axis=1)
    leave = piece[:, 3 * LANES : 3 * LANES + USED].T
    up = piece[:, ATT : ATT + depth]
    down = piece[:, ATT + depth :].T
    small = piece[:, SMALL_AT : SMALL_AT + 6].T
    return (entry, leave, up, down, small, piece[:, HIDDEN_AT])


def adamw(grad, first, second, master, decay, rate):
    moment = BETA_ONE * first + (1.0 - BETA_ONE) * grad
    square = BETA_TWO * second + (1.0 - BETA_TWO) * grad * grad
    ahead = moment / (1.0 - BETA_ONE**STEP)
    spread = square / (1.0 - BETA_TWO**STEP)
    return (
        moment,
        square,
        master - rate * (ahead / (jnp.sqrt(spread) + ADAM_EPS) + decay * master),
    )


DECAYS = (DECAY, DECAY, DECAY, DECAY, 0.0, 0.0)
RATES = (RATE_MATRIX, RATE_EXIT, RATE_MATRIX, RATE_MATRIX, RATE_SMALL, RATE_BIAS)


def finish_plain(grad_att, grad_ffn, masters, firsts, seconds):
    depth = grad_att.shape[1]
    grads = jnp.concatenate([grad_att, grad_ffn], axis=2).astype(F32)
    own = lax.psum_scatter(grads, "tensor", scatter_dimension=0, tiled=False)
    own = lax.psum_scatter(own, "dp", scatter_dimension=0, tiled=True)
    shares = unpack_piece(own, depth)
    copies = float(lax.axis_size("tensor"))
    total = jnp.sum(shares[4] * shares[4]) / copies
    for k in (0, 1, 2, 3, 5):
        total = total + jnp.sum(shares[k] * shares[k])
    norm_value = jnp.sqrt(lax.psum(total, ("dp", "tensor")))
    factor = CLIP / jnp.maximum(norm_value, CLIP)
    outs = []
    for k in range(6):
        outs.extend(
            adamw(shares[k] * factor, firsts[k], seconds[k], masters[k], DECAYS[k], RATES[k])
        )
    return (norm_value, outs)


def spot():
    dp, t = lax.axis_index("dp"), lax.axis_index("tensor")
    return (dp, t)


def flip(value, bits):
    for bit in (1, 2, 4):
        if bits & bit:
            value = value + bit - 2 * bit * ((value // bit) % 2)
    return value


def greet(peers):
    barrier = pltpu.get_barrier_semaphore()
    for peer in peers:
        pl.semaphore_signal(barrier, inc=1, device_id=peer, device_id_type=MESH)
    pl.semaphore_wait(barrier, len(peers))


KEY_PARTS = 3
SENDS = 62 + 9 + 12 + 34 + 10


class Mail:
    def __init__(self, send_sem, recv_sem):
        self.send_sem, self.recv_sem = send_sem, recv_sem
        self.count, self.sent = 0, []

    def send(self, src, dst, peer):
        copy = pltpu.make_async_remote_copy(
            src_ref=src,
            dst_ref=dst,
            send_sem=self.send_sem.at[self.count],
            recv_sem=self.recv_sem.at[self.count],
            device_id=peer,
            device_id_type=MESH,
        )
        copy.start()
        self.count += 1
        self.sent.append(copy)
        return copy

    def close(self):
        for copy in self.sent:
            copy.wait_send()


def arrived(copies):
    for copy in copies:
        copy.wait_recv()


def load_rows(src, dst, t, sem):
    count = dst.shape[0]
    copy = pltpu.make_async_copy(src.at[pl.ds(t * count, count)], dst, sem)
    copy.start()
    return copy


def fold(block):
    out = block[0:8]
    for k in range(8, block.shape[0], 8):
        out = out + block[k : k + 8]
    return out


class Reduce:
    def __init__(self, mail, grad_ref, refs, where):
        self.mail, self.grad = mail, grad_ref
        self.rc, self.s0, self.r1, self.s1, self.r2, self.s2, self.r3 = refs
        self.where = where
        self.core = [None, None]
        self.side = [None, None]
        self.line = [None, None]
        self.across = None

    def slab(self, group, k):
        rows = self.s1.shape[2]
        return self.grad.at[group, pl.ds(pl.multiple_of(k * rows, 16), rows)]

    def to_core(self, q):
        dp, t, core, across, side, line = self.where
        self.core[q] = self.mail.send(self.grad.at[flip(t, 1 + 2 * q)], self.rc.at[q], core)

    def to_side(self, q):
        dp, t, core, across, side, line = self.where
        self.core[q].wait_recv()
        own = flip(t, 2 * q)
        y = dp % 2
        rows = self.s1.shape[2]

        @pl.loop(0, 8)
        def _(k):
            part = pl.ds(pl.multiple_of(k * rows, 16), rows)
            left = self.grad[own, part, :].astype(F32)
            self.s0[q, k] = (left + self.rc[q, part, :].astype(F32)).astype(BF)

        self.side[q] = [
            self.mail.send(self.s0.at[q, 2 * w + 1 - y], self.r1.at[q, w], side) for w in range(4)
        ]

    def to_line(self, q):
        dp, t, core, across, side, line = self.where
        arrived(self.side[q])
        y = dp % 2

        @pl.loop(0, 4)
        def _(w):
            left = self.s0[q, 2 * w + y].astype(F32)
            self.s1[q, w] = (left + self.r1[q, w].astype(F32)).astype(BF)

        self.line[q] = [
            self.mail.send(self.s1.at[q, line[j][0] // 2], self.r2.at[q, j - 1], line[j])
            for j in range(1, 4)
        ]

    def to_across(self, q):
        dp, t, core, across, side, line = self.where
        arrived(self.line[q])
        total = self.s1[q, dp // 2].astype(F32)
        for j in range(3):
            total = total + self.r2[q, j].astype(F32)
        self.s2[q] = total.astype(BF)
        if q:
            self.across = self.mail.send(self.s2.at[1], self.r3, across)

    def result(self):
        self.across.wait_recv()
        return self.s2[0].astype(F32) + self.r3[...].astype(F32)


class Spread:
    def __init__(self, mail, where, own_ref, out_ref, first, sem):
        dp, t, core, across, side, line = where
        self.mail, self.where, self.out = mail, where, out_ref
        self.count = own_ref.shape[0]
        self.first = first
        here = self.part(t)
        self.across = mail.send(own_ref, here, across)
        self.core = [mail.send(own_ref, here, core)]
        self.local = pltpu.make_async_copy(own_ref, here, sem)
        self.local.start()

    def part(self, t):
        at = t * self.first[1] + self.first[0]
        return self.out.at[pl.ds(pl.multiple_of(at, 16), self.count)]

    def forward(self):
        dp, t, core, across, side, line = self.where
        self.across.wait_recv()
        far = self.part(flip(t, 2))
        self.core.append(self.mail.send(far, far, core))

    def finish(self):
        arrived(self.core)
        self.local.wait()


class Gather:
    def __init__(self, mail, where, own_ref, all_ref, sem):
        self.mail, self.where, self.own, self.all = mail, where, own_ref, all_ref
        dp, t, core, across, side, line = where
        self.local = pltpu.make_async_copy(own_ref, self.piece(t, dp), sem)
        self.local.start()

    def piece(self, group, dp):
        rows = self.own.shape[0]
        return self.all.at[group, pl.ds(pl.multiple_of(dp * rows, 16), rows)]

    def start_across(self):
        dp, t, core, across, side, line = self.where
        self.across = self.mail.send(self.own, self.piece(t, dp), across)

    def start(self):
        dp, t, core, across, side, line = self.where
        send, here = self.mail.send, self.piece(t, dp)
        self.line = [[send(self.own, here, line[j])] for j in range(1, 4)]
        self.side = [[send(self.own, here, side)], [], [], []]
        self.core = [[send(self.own, here, core)], []]

    def pass_across(self):
        dp, t, core, across, side, line = self.where
        send, far = self.mail.send, self.piece(flip(t, 2), dp)
        self.across.wait_recv()
        for j in range(1, 4):
            self.line[j - 1].append(send(far, far, line[j]))
        self.side[0].append(send(far, far, side))
        self.core[1].append(send(far, far, core))

    def pass_line(self, k):
        dp, t, core, across, side, line = self.where
        for j in range(1, 4):
            self.line[j - 1][k].wait_recv()
            piece = self.piece(flip(t, 2 * k), line[j][0])
            self.side[j].append(self.mail.send(piece, piece, side))
            self.core[k].append(self.mail.send(piece, piece, core))

    def pass_side(self, k):
        dp, t, core, across, side, line = self.where
        for j in range(4):
            self.side[j][k].wait_recv()
            piece = self.piece(flip(t, 2 * k), flip(line[j][0], 1))
            self.core[k].append(self.mail.send(piece, piece, core))

    def finish(self, k):
        arrived(self.core[k])


def block_kernel(*refs):
    entry_ref, leave_ref, up_ref, down_ref, small_ref, hidden_ref = refs[0:6]
    key_entry, key_leave, key_up, key_down, key_small, key_hidden = refs[6:12]
    tokens_ref, cot_all_ref, key_tokens_ref, crops_ref = refs[12:16]
    block_out, key_out, input_grad, norm_ref, own_a, own_f, own_s = refs[16:23]
    (
        kx_ref, qx_ref, cot_ref, ids_ref, pa_ref, pf_ref, keys_ref, wa_ref, wf_ref,
        kqkv_ref, qqkv_ref, ka_ref, qa_ref, lse_ref, kh_ref, h1_ref, kx1_ref, x1_ref,
        act_ref, dpre_ref, h2_ref, h2t_ref, eb_ref, ebt_ref, bias_ref, hid_ref, line_ref,
        unit_ref, scale_ref, h1t_ref, dyb_ref, dybt_ref, dqkv_ref, ga_ref, gf_ref,
        key_rows, block_rows, grad_rows, near_ref, far_ref, turn_ref,
    ) = refs[23:64]
    red_a, red_f = refs[64:71], refs[71:78]
    send_sem, recv_sem, local_sem = refs[78:]
    dp, t = spot()
    far = flip(t, 2)
    core, across = (dp, flip(t, 1)), (dp, far)
    side = (flip(dp, 1), t)
    line = [(flip(dp, 2 * j), t) for j in range(4)]
    where = (dp, t, core, across, side, line)
    mail = Mail(send_sem, recv_sem)
    send = mail.send
    loads = [
        load_rows(src, dst, t, local_sem.at[k])
        for k, (src, dst) in enumerate(
            ((key_tokens_ref, kx_ref), (crops_ref, ids_ref), (tokens_ref, qx_ref), (cot_all_ref, cot_ref))
        )
    ]

    rows, depth = up_ref.shape
    wide = LANES - USED
    extra = [small_ref[...], hidden_ref[...], jnp.zeros((wide - 7, rows), F32)]
    extra = jnp.concatenate(extra, axis=0).T
    blank = jnp.zeros((rows, wide), F32)
    for k, block in enumerate([entry_ref[0], entry_ref[1], entry_ref[2], leave_ref[...]]):
        block = jnp.concatenate([block, blank if k else extra], axis=1)
        pa_ref[:, k * LANES : (k + 1) * LANES] = block.astype(BF)
    pf_ref[:, 0:depth] = up_ref[...].astype(BF)
    pf_ref[:, depth:] = down_ref[...].astype(BF)
    blank = jnp.zeros((wide, depth), BF)
    extra = [key_small[...], key_hidden[...], jnp.zeros((wide - 7, depth), BF)]
    for k, block in enumerate([key_entry[0], key_entry[1], key_entry[2], key_leave[...]]):
        block = jnp.concatenate([block] + ([blank] if k else extra), axis=0)
        keys_ref[t, :, k * LANES : (k + 1) * LANES] = block.T
    keys_ref[t, :, ATT : ATT + depth] = key_up[...]
    keys_ref[t, :, ATT + depth :] = key_down[...].T
    greet([(dp, flip(t, k)) for k in (1, 2, 3)] + [(flip(dp, k), t) for k in range(1, 8)])

    parts = [pl.ds(0, ATT), pl.ds(ATT, depth), pl.ds(ATT + depth, depth)]

    def key_part(group, k):
        return keys_ref.at[group, :, parts[k]]

    def key_send(k, peer):
        return send(key_part(t, k), key_part(t, k), peer)

    gather_a = Gather(mail, where, pa_ref, wa_ref, local_sem.at[4])
    gather_f = Gather(mail, where, pf_ref, wf_ref, local_sem.at[5])
    gather_a.start_across()
    key_core = [key_send(0, core)]
    key_across = [key_send(0, across)]
    gather_a.start()
    gather_f.start_across()
    key_core += [key_send(k, core) for k in (1, 2)]
    key_across += [key_send(k, across) for k in (1, 2)]
    gather_f.start()

    packs = kx_ref.shape[0] // PACK
    bases = [pack * PACK for pack in range(packs)]
    spots = [slice(base, base + PACK) for base in bases]
    loads[0].wait()
    loads[1].wait()
    key_norms = small_rows_of(keys_ref[t, :, 0:LANES])
    masks = [enter(kx_ref, ids_ref, key_norms, kh_ref, base, k) for k, base in enumerate(bases)]
    sides = [query_side for _, query_side in masks]

    def heads_of(slot, weight, first_ref, qkv_ref, a_ref, lse):
        for base, (key_side, _) in zip(bases, masks):
            project(first_ref[base : base + PACK, :], weight, qkv_ref, key_side, base, slot)
        attention(qkv_ref, a_ref, lse, [(slot, base) for base in bases], sides)

    def key_heads(slot):
        heads_of(slot, keys_ref[flip(t, slot), :, 0 : 3 * LANES], kh_ref, kqkv_ref, ka_ref, None)

    def query_heads(slot):
        heads_of(slot, wa_ref[flip(t, slot), :, 0 : 3 * LANES], h1_ref, qqkv_ref, qa_ref, lse_ref)

    def pass_key(k):
        key_across[k].wait_recv()
        return send(key_part(far, k), key_part(far, k), core)

    key_heads(0)
    gather_a.pass_across()
    arrived(key_core[:1])
    key_heads(1)
    gather_a.pass_line(0)
    gather_f.pass_across()
    loads[2].wait()
    loads[3].wait()
    for k, spot_rows in enumerate(spots):
        low = masked_cot(cot_ref, ids_ref, k, spot_rows).astype(BF)
        eb_ref[spot_rows, :] = low
        ebt_ref[:, spot_rows] = low.T
    gather_a.pass_line(1)
    gather_a.pass_side(0)
    gather_a.local.wait()
    norms = small_rows_of(wa_ref[t, :, 0:LANES])
    for spot_rows in spots:
        unit, scale = norm_parts(qx_ref[spot_rows, :].astype(F32))
        first = (unit * norms[0:1] + norms[1:2]).astype(BF)
        unit_ref[spot_rows, :] = unit
        scale_ref[spot_rows, :] = jnp.broadcast_to(scale, (PACK, LANES))
        h1_ref[spot_rows, :] = first
        h1t_ref[:, spot_rows] = first.T
    query_heads(0)
    key_far = [pass_key(0)]
    gather_a.pass_side(1)
    key_heads(2)
    gather_f.pass_line(0)
    arrived(key_far)
    key_heads(3)
    gather_a.finish(0)
    query_heads(1)
    gather_f.pass_line(1)
    query_heads(2)
    gather_f.pass_side(0)
    gather_a.finish(1)
    query_heads(3)
    key_far.append(pass_key(1))

    def leaving_of(w_ref):
        weights = [w_ref[flip(t, k), :, 3 * LANES : 4 * LANES] for k in range(4)]
        return jnp.concatenate(weights, axis=1)

    weight = leaving_of(keys_ref)
    for base in bases:
        second = leave(kx_ref, weight, key_norms, ka_ref, kx1_ref, base)
        kh_ref[base : base + PACK, :] = second
    gather_f.pass_side(1)
    arrived(key_core[1:2] + key_far[1:2])
    for k in range(4):
        bias_ref[:, k * depth : (k + 1) * depth] = hidden_line(keys_ref[k, :, 0:LANES])
    for base in bases:
        feed(kh_ref[base : base + PACK, :], keys_ref, bias_ref, act_ref.at[base : base + PACK])
    key_far.append(pass_key(2))
    weight = leaving_of(wa_ref)
    for base in bases:
        second = leave(qx_ref, weight, norms, qa_ref, x1_ref, base)
        h2_ref[base : base + PACK, :] = second
        h2t_ref[0:depth, base : base + PACK] = second.T
    h2t_ref[depth:, :] = jnp.ones((h2t_ref.shape[0] - depth, h2t_ref.shape[1]), BF)
    arrived(key_core[2:] + key_far[2:])
    weight = gathered(keys_ref, ATT + depth, depth)
    for spot_rows in spots:
        product = mm_nt(act_ref[spot_rows, :], weight)
        key_rows[spot_rows, :] = (kx1_ref[spot_rows, :] + product + key_norms[5:6]).astype(BF)
    count = key_rows.shape[0]
    spread_key = Spread(mail, where, key_rows, key_out, (0, count), local_sem.at[6])

    gather_f.finish(0)
    gather_f.finish(1)
    gather_f.local.wait()
    for k in range(4):
        bias_ref[:, k * depth : (k + 1) * depth] = hidden_line(wa_ref[k, :, 0:LANES])
    feed_back(
        wf_ref, 0, h2_ref, h2t_ref, eb_ref, ebt_ref, bias_ref, act_ref, dpre_ref, gf_ref, hid_ref
    )
    reduce_f = Reduce(mail, gf_ref, red_f, where)
    reduce_f.to_core(0)
    reduce_f.to_core(1)
    weight = gathered(wf_ref, depth, depth)
    for spot_rows in spots:
        product = mm_nt(act_ref[spot_rows, :], weight)
        block_rows[spot_rows, :] = (x1_ref[spot_rows, :] + product + norms[5:6]).astype(BF)
    spread_block = Spread(mail, where, block_rows, block_out, (0, count), local_sem.at[7])
    line_ref[...] = jnp.zeros_like(line_ref)
    weight = gathered(wf_ref, 0, depth)
    for k, spot_rows in enumerate(spots):
        grad = mm_nt(dpre_ref[spot_rows, :], weight)
        unit, scale = norm_parts(x1_ref[spot_rows, :])
        wide_cot = masked_cot(cot_ref, ids_ref, k, spot_rows)
        dx1 = wide_cot + norm_back(grad, unit, scale, norms[2:3])
        x1_ref[spot_rows, :] = dx1
        low = dx1.astype(BF)
        dyb_ref[spot_rows, :] = low
        dybt_ref[:, spot_rows] = low.T
        line_ref[2:3, :] += jnp.sum(grad * unit, axis=0, keepdims=True)
        line_ref[3:4, :] += jnp.sum(grad, axis=0, keepdims=True)
        line_ref[4:5, :] += jnp.sum(dx1, axis=0, keepdims=True)
        line_ref[5:6, :] += jnp.sum(wide_cot, axis=0, keepdims=True)
    reduce_f.to_side(0)
    reduce_f.to_side(1)

    reduce_a = Reduce(mail, ga_ref, red_a, where)
    lane = lax.broadcasted_iota(jnp.int32, (depth, LANES), 1)
    width = 3 * LANES

    def back_heads(slot):
        weight = wa_ref[flip(t, slot), :, width : width + LANES]
        for base in bases:
            low = dyb_ref[base : base + PACK, :]
            ka_ref[base : base + PACK, 0:LANES] = mm(low, weight).astype(BF)
        places = [(slot, base, 0, 0) for base in bases]
        attention_back(qqkv_ref, qa_ref, lse_ref, ka_ref, dqkv_ref, places, sides)

    def back_weights(slot):
        group = flip(t, slot)
        entry = mm(h1t_ref[...], dqkv_ref[...])
        hidden = jnp.broadcast_to(hid_ref[pl.ds(group, 1), :], (LANES, depth)).T
        ga_ref[group, :, 0:LANES] = jnp.where(lane == HIDDEN_AT, hidden, entry[:, :LANES]).astype(BF)
        ga_ref[group, :, LANES:width] = entry[:, LANES:].astype(BF)
        mixed = qa_ref[:, slot * LANES : (slot + 1) * LANES]
        ga_ref[group, :, width : width + LANES] = mm(dybt_ref[...], mixed).astype(BF)

    def back_rows(slot, spot_rows, more):
        grad = mm_nt(dqkv_ref[spot_rows, :], wa_ref[flip(t, slot), :, 0:width])
        return kx1_ref[spot_rows, :] + grad if more else grad

    back_heads(1)
    back_weights(1)
    reduce_a.to_core(0)
    for spot_rows in spots:
        kx1_ref[spot_rows, :] = back_rows(1, spot_rows, False)
    spread_key.forward()
    reduce_f.to_line(0)
    back_heads(0)
    back_weights(0)
    reduce_a.to_side(0)
    for spot_rows in spots:
        kx1_ref[spot_rows, :] = back_rows(0, spot_rows, True)
    reduce_f.to_line(1)
    back_heads(3)
    back_weights(3)
    reduce_a.to_core(1)
    for spot_rows in spots:
        kx1_ref[spot_rows, :] = back_rows(3, spot_rows, True)
    reduce_f.to_across(0)
    reduce_a.to_line(0)
    back_heads(2)
    back_weights(2)
    reduce_a.to_side(1)
    spread_grad = []
    for k, spot_rows in enumerate(spots):
        grad = back_rows(2, spot_rows, True)
        unit, scale = unit_ref[spot_rows, :], scale_ref[spot_rows, 0:1]
        back = norm_back(grad, unit, scale, norms[0:1])
        grad_rows[spot_rows, :] = (x1_ref[spot_rows, :] + back).astype(BF)
        spread_grad.append(
            Spread(
                mail,
                where,
                grad_rows.at[spot_rows],
                input_grad,
                (k * PACK, count),
                local_sem.at[8 + k],
            )
        )
        line_ref[0:1, :] += jnp.sum(grad * unit, axis=0, keepdims=True)
        line_ref[1:2, :] += jnp.sum(grad, axis=0, keepdims=True)
    reduce_f.to_across(1)
    spread_block.forward()
    reduce_a.to_line(1)
    reduce_a.to_across(0)
    grad_f = reduce_f.result()
    reduce_a.to_across(1)
    for item in spread_grad:
        item.forward()
    grad_a = reduce_a.result()

    total = jnp.zeros((8, LANES), F32)
    lane = lax.broadcasted_iota(jnp.int32, (rows, LANES), 1)
    for k in range(4):
        block = grad_a[:, k * LANES : (k + 1) * LANES]
        share = jnp.where(lane < USED, 1.0, jnp.where(lane == HIDDEN_AT, 0.0 if k else 1.0, 0.0))
        total = total + fold(block * block * share)
    for k in range(2 * depth // LANES):
        block = grad_f[:, k * LANES : (k + 1) * LANES]
        total = total + fold(block * block)
    near_ref[t, 0:8, :] = line_ref[...]
    near_ref[t, 8:16, :] = jnp.concatenate([total] + [jnp.zeros_like(total)] * 2, axis=1)
    near = [send(near_ref.at[t], near_ref.at[t], (dp, flip(t, k))) for k in (1, 2, 3)]
    own_a[...] = grad_a
    own_f[...] = grad_f
    arrived(near)
    far_ref[dp] = (near_ref[0] + near_ref[1]) + (near_ref[2] + near_ref[3])
    wide_sends = [send(far_ref.at[dp], far_ref.at[dp], (flip(dp, k), t)) for k in range(1, 8)]
    arrived(wide_sends)
    total = far_ref[0]
    for k in range(1, 8):
        total = total + far_ref[k]
    lines = total[0:8]
    squares = fold(total[8:16, 0:LANES])
    for k in range(depth // LANES):
        block = lines[:, k * LANES : (k + 1) * LANES]
        squares = squares + block * block
    squares = jnp.sum(jnp.sum(squares, axis=0, keepdims=True), axis=1, keepdims=True)
    norm_ref[...] = jnp.broadcast_to(jnp.sqrt(squares), norm_ref.shape)
    turn_ref[...] = jnp.concatenate([lines, jnp.zeros((LANES - 8, depth), F32)], axis=0).T
    own_s[...] = turn_ref[pl.ds(pl.multiple_of(dp * rows, 16), rows), :]
    for item in [spread_key, spread_block] + spread_grad:
        item.finish()
    mail.close()


def lay(entry, leave, up, down, small, hidden):
    return [entry.transpose(1, 0, 2), leave.T, up, down.T, small, hidden.reshape(1, -1)]


def run_block(masters, keys, tokens, cotangent, key_tokens, ids, dp, tensor):
    key_entry, key_leave, key_up, key_down, key_small, key_hidden = keys
    rows, depth = masters[2].shape
    all_rows = tokens.shape[0]
    count = all_rows // tensor
    args = lay(*masters)
    args += [key_entry.transpose(1, 2, 0), key_leave, key_up, key_down, key_small]
    args.append(key_hidden.reshape(1, -1))

    def all_of(shape):
        return pl.BlockSpec(shape, lambda i: (0,) * len(shape))

    anywhere = pl.BlockSpec(memory_space=pl.ANY)
    hidden = tensor * depth
    scratch = [
        ((count, depth), BF),
        ((count, depth), BF),
        ((count, depth), BF),
        ((count // PACK, 1, PACK), jnp.int32),
        ((rows, ATT), BF),
        ((rows, 2 * depth), BF),
        ((tensor, depth, ATT + 2 * depth), BF),
        ((tensor, depth, ATT), BF),
        ((tensor, depth, 2 * depth), BF),
        ((count, tensor * 3 * LANES), BF),
        ((count, tensor * 3 * LANES), BF),
        ((count, tensor * LANES), BF),
        ((count, tensor * LANES), BF),
        ((16, count), F32),
        ((count, depth), BF),
        ((count, depth), BF),
        ((count, depth), F32),
        ((count, depth), F32),
        ((count, hidden), BF),
        ((count, hidden), BF),
        ((count, depth), BF),
        ((depth + 16, count), BF),
        ((count, depth), BF),
        ((depth, count), BF),
        ((1, hidden), F32),
        ((8, depth), F32),
        ((8, depth), F32),
        ((count, depth), F32),
        ((count, LANES), F32),
        ((depth, count), BF),
        ((count, depth), BF),
        ((depth, count), BF),
        ((count, 3 * LANES), BF),
        ((tensor, depth, ATT), BF),
        ((tensor, depth, 2 * depth), BF),
        ((count, depth), BF),
        ((count, depth), BF),
        ((count, depth), BF),
        ((tensor, 16, depth), F32),
        ((dp, 16, depth), F32),
        ((depth, LANES), F32),
    ]
    for wide in (ATT, 2 * depth):
        scratch += [
            ((2, depth, wide), BF),
            ((2, 8, rows, wide), BF),
            ((2, 4, rows, wide), BF),
            ((2, 4, rows, wide), BF),
            ((2, 3, rows, wide), BF),
            ((2, rows, wide), BF),
            ((rows, wide), BF),
        ]
    outs = [
        ((all_rows, depth), BF),
        ((all_rows, depth), BF),
        ((all_rows, depth), BF),
        ((8, LANES), F32),
        ((rows, ATT), F32),
        ((rows, 2 * depth), F32),
        ((rows, LANES), F32),
    ]
    return pl.pallas_call(
        block_kernel,
        grid=(1,),
        in_specs=[all_of(item.shape) for item in args] + [anywhere] * 4,
        out_specs=[anywhere] * 3 + [all_of(shape) for shape, _ in outs[3:]],
        scratch_shapes=[VMEM(shape, kind) for shape, kind in scratch]
        + [
            pltpu.SemaphoreType.DMA((SENDS,)),
            pltpu.SemaphoreType.DMA((SENDS,)),
            pltpu.SemaphoreType.DMA((10,)),
        ],
        out_shape=[jax.ShapeDtypeStruct(shape, kind) for shape, kind in outs],
        compiler_params=pltpu.CompilerParams(
            collective_id=1, has_side_effects=True, vmem_limit_bytes=63 * 2**20
        ),
        name="block_forward_and_backward",
    )(*args, tokens, cotangent, key_tokens, ids)


def step_kernel(norm_ref, ga_ref, gb_ref, gs_ref, *refs):
    masters, firsts, seconds = refs[0:6], refs[6:12], refs[12:18]
    value_ref, outs = refs[18], refs[19:]
    norm_value = norm_ref[0:1, 0:1]
    value_ref[...] = norm_value
    factor = CLIP / jnp.maximum(norm_value, CLIP)
    grad_a = ga_ref[...] * factor
    grad_b = gb_ref[...] * factor
    depth = grad_b.shape[1] // 2

    def update(k, at, grad):
        new = adamw(grad, firsts[k][at], seconds[k][at], masters[k][at], DECAYS[k], RATES[k])
        for j in range(3):
            outs[3 * k + j][at] = new[j]

    for j in range(3):
        update(0, j, grad_a[:, j * LANES : j * LANES + USED])
    update(1, slice(None), grad_a[:, 3 * LANES : 3 * LANES + USED])
    update(2, slice(None), grad_b[:, :depth])
    update(3, slice(None), grad_b[:, depth:])
    update(4, slice(None), (gs_ref[...] * factor).T[0:6])
    update(5, slice(None), grad_a[:, :LANES].T[HIDDEN_AT : HIDDEN_AT + 1])


def run_step(norm_tile, grad_a, grad_b, grad_s, masters, firsts, seconds):
    state = lay(*masters) + lay(*firsts) + lay(*seconds)
    shapes = [jax.ShapeDtypeStruct((1, 1), F32)]
    for item in state[:6]:
        shapes.extend([jax.ShapeDtypeStruct(item.shape, F32)] * 3)
    args = [norm_tile, grad_a, grad_b, grad_s] + state

    def all_of(shape):
        return pl.BlockSpec(shape, lambda i: (0,) * len(shape))

    result = pl.pallas_call(
        step_kernel,
        grid=(1,),
        in_specs=[all_of(item.shape) for item in args],
        out_specs=[all_of(item.shape) for item in shapes],
        out_shape=shapes,
        name="optimizer_step",
    )(*args)
    outs = list(result[1:])
    for k in range(3):
        outs[k] = outs[k].transpose(1, 0, 2)
        outs[3 + k] = outs[3 + k].T
        outs[9 + k] = outs[9 + k].T
        outs[15 + k] = outs[15 + k].reshape(-1)
    return (result[0].reshape(()), outs)


def on_device(*args):
    tokens, crop_ids, cotangent, key_tokens = args[:4]
    masters, firsts, seconds, keys = args[4:10], args[10:16], args[16:22], args[22:28]
    count, groups = lax.axis_size("dp"), lax.axis_size("tensor")
    ids = crop_ids.reshape(-1, 1, PACK)
    if count == 8 and groups == 4:
        result = run_block(masters, keys, tokens, cotangent, key_tokens, ids, count, groups)
        norm_value, outs = run_step(*result[3:], masters, firsts, seconds)
        return (*result[:3], norm_value, *outs)
    rows = tokens.shape[0] // groups
    place = lax.axis_index("tensor").astype(jnp.int32)[None]
    key_weights = lax.all_gather(pack_piece(*keys), "tensor", axis=0)
    weights = lax.all_gather(pack_piece(*masters), "dp", axis=0, tiled=True)
    weights = lax.all_gather(weights, "tensor", axis=0)

    def spread(own):
        return lax.all_gather(own, "tensor", axis=0, tiled=True)

    key_out = spread(run_key(place, key_tokens, ids, key_weights, rows))
    forward = run_query(place, tokens, cotangent, ids, weights, rows)
    block_out = spread(forward[0])
    qkv, a, lse, h1, dx1, grad_ffn, lines, hidden = forward[1:]
    grad_rows, grad_att = run_back(
        place, tokens, ids, weights, (qkv, a, lse, h1, dx1, lines, hidden), rows
    )
    input_grad = spread(grad_rows)
    norm_value, outs = finish_plain(grad_att, grad_ffn, masters, firsts, seconds)
    return (block_out, key_out, input_grad, norm_value, *outs)


def solution(mesh):
    rows, line = P("dp", None), P("dp")
    entry, leave, up, down = P("dp", None, "tensor"), P("tensor", "dp"), P("dp", "tensor"), P("tensor", "dp")
    state = (entry, leave, up, down, P(None, "dp"), P(("tensor", "dp")))
    keys = (P(None, None, "tensor"), P("tensor", None), P(None, "tensor"), P("tensor", None), P(), P("tensor"))
    outs = tuple(spec for spec in state for _ in range(3))
    return jax.shard_map(
        on_device,
        mesh=mesh,
        in_specs=(rows, line, rows, rows) + state * 3 + keys,
        out_specs=(rows, rows, rows, P()) + outs,
        check_vma=False,
    )
```

```python
import math
from functools import partial

import jax
import jax.numpy as jnp
from jax import lax
from jax.experimental import pallas as pl
from jax.experimental.pallas import tpu as pltpu
from jax.sharding import PartitionSpec as P

HEAD_DIM = 32
PACK = 512
CROPS = 5
STEP = 10
LN_EPS = 1e-06
CLIP = 1.0
RATE_MATRIX = 0.03
RATE_EXIT = 0.2
RATE_SMALL = 0.5
RATE_BIAS = 0.3
BETA_ONE = 0.9
BETA_TWO = 0.999
ADAM_EPS = 1e-08
DECAY = 0.05
MASKED = -1e30

SCALE = HEAD_DIM ** (-0.5)
EXP_SCALE = SCALE * math.log2(math.e)
LOG_TWO = math.log(2.0)
LANES = 128
TILE = 2 * LANES
PIECE = 64
HEADS_HERE = 3
USED = HEADS_HERE * HEAD_DIM
ONES = USED + CROPS + 1
ATT = 4 * LANES
SMALL_AT = USED
HIDDEN_AT = USED + 6
MESH = pl.DeviceIdType.MESH
BF = jnp.bfloat16
F32 = jnp.float32
VMEM = pltpu.VMEM
NT = (((1,), (1,)), ((), ()))
TN = (((0,), (0,)), ((), ()))

def mm(left, right):
    return jnp.dot(left, right, preferred_element_type=F32)


def mm_nt(left, right):
    return lax.dot_general(left, right, NT, preferred_element_type=F32)


def norm_parts(values):
    mean = jnp.mean(values, axis=1, keepdims=True)
    centred = values - mean
    spread = jnp.mean(centred * centred, axis=1, keepdims=True)
    scale = lax.rsqrt(spread + LN_EPS)
    return (centred * scale, scale)


def norm_back(grad, unit, scale, gain):
    scaled = grad * gain
    first = jnp.mean(scaled, axis=1, keepdims=True)
    second = jnp.mean(scaled * unit, axis=1, keepdims=True)
    return scale * (scaled - first - unit * second)


def below(pre):
    return 0.5 + 0.5 * lax.erf(pre * math.sqrt(0.5))


def below_and_slope(pre):
    phi = below(pre)
    bell = jnp.exp2((pre * (-0.5 * math.log2(math.e))) * pre)
    return (phi, phi + (pre * (1.0 / math.sqrt(2.0 * math.pi))) * bell)


def small_rows_of(weight):
    return weight.astype(F32).T[SMALL_AT : SMALL_AT + 6]


def hidden_line(weight):
    return weight.astype(F32).T[HIDDEN_AT : HIDDEN_AT + 1]


def small_rows(w_ref):
    return small_rows_of(w_ref[0, :, 0:LANES])


def hidden_row(w_ref, t):
    return hidden_line(w_ref[t, :, 0:LANES])


def id_lanes(ids):
    place = lax.broadcasted_iota(jnp.int32, (LANES, PACK), 0)
    match = (place - USED) == ids
    ones = (place >= ONES) & (place < ONES + 3)
    key_side = jnp.where(match | ones, 1.0, 0.0).T
    crop = (place >= USED) & (place < ONES)
    query_side = jnp.where(crop & jnp.logical_not(match), MASKED, 0.0).astype(BF)
    return (key_side, query_side)


def attention(qkv_ref, a_ref, lse_ref, places, sides):
    place = lax.broadcasted_iota(jnp.int32, (LANES, PACK), 0) // HEAD_DIM
    ones = jnp.ones((16, PACK), BF)
    blank = jnp.zeros((LANES - USED, PACK), F32)
    heads = [(k, h) for k in range(len(places)) for h in range(HEADS_HERE)]
    held, outs = {}, {}

    def scores_of(k, h):
        if k not in held:
            slot, base = places[k]
            rows, at = pl.ds(base, PACK), slot * 3 * LANES
            query = qkv_ref[rows, at : at + LANES].T
            keys = qkv_ref[rows, at + LANES : at + 2 * LANES]
            values = qkv_ref[rows, at + 2 * LANES : at + 3 * LANES].T
            held[k] = (query, keys, values)
        query, keys, _ = held[k]
        return mm(keys, jnp.where(place == h, query, sides[k]))

    def mix(k, h, top, probs):
        slot, base = places[k]
        rows = pl.ds(base, PACK)
        values = held[k][2][h * HEAD_DIM : (h + 1) * HEAD_DIM]
        mixed = mm(jnp.concatenate([values, ones], axis=0), probs)
        total = mixed[HEAD_DIM : HEAD_DIM + 1]
        outs[(k, h)] = mixed[:HEAD_DIM] * (1.0 / total)
        if lse_ref is not None:
            line = slot * HEADS_HERE + h
            lse_ref[line : line + 1, rows] = top + jnp.log2(total)
        if h == HEADS_HERE - 1:
            parts = [outs[(k, n)] for n in range(HEADS_HERE)] + [blank]
            a_ref[rows, slot * LANES : (slot + 1) * LANES] = (
                jnp.concatenate(parts, axis=0).T.astype(BF)
            )

    scores = scores_of(*heads[0])
    waiting = None
    for n, head in enumerate(heads):
        later = scores_of(*heads[n + 1]) if n + 1 < len(heads) else None
        if waiting is not None:
            mix(*waiting)
        top = jnp.max(scores, axis=0, keepdims=True)
        waiting = head + (top, jnp.exp2(scores - top).astype(BF))
        scores = later
    mix(*waiting)


def enter(x_ref, ids_ref, small, h1_ref, base, pack):
    rows = pl.ds(base, PACK)
    values = x_ref[rows, :].astype(F32)
    unit, _ = norm_parts(values)
    first = (unit * small[0:1] + small[1:2]).astype(BF)
    h1_ref[rows, :] = first
    return id_lanes(ids_ref[pack])


def project(first, weight, qkv_ref, key_side, base, slot):
    rows, at = pl.ds(base, PACK), slot * 3 * LANES
    packed = mm(first, weight)
    qkv_ref[rows, at : at + LANES] = (packed[:, :LANES] * EXP_SCALE).astype(BF)
    for k in (1, 2):
        part = packed[:, k * LANES : (k + 1) * LANES] + key_side
        qkv_ref[rows, at + k * LANES : at + (k + 1) * LANES] = part.astype(BF)


def project_all(first, w_ref, qkv_ref, key_side, base):
    for g in range(w_ref.shape[0]):
        project(first, w_ref[g, :, 0 : 3 * LANES], qkv_ref, key_side, base, g)


def leaving(w_ref):
    return gathered(w_ref, 3 * LANES, LANES)


def leave(x_ref, weight, small, a_ref, x1_ref, base):
    rows = pl.ds(base, PACK)
    branch = mm_nt(a_ref[rows, :], weight)
    x1 = x_ref[rows, :].astype(F32) + branch + small[4:5]
    x1_ref[rows, :] = x1
    unit, _ = norm_parts(x1)
    return (unit * small[2:3] + small[3:4]).astype(BF)


def gathered(w_ref, at, width):
    parts = [w_ref[t, :, at : at + width] for t in range(w_ref.shape[0])]
    return jnp.concatenate(parts, axis=1)


def tile_of(w_ref, j, first):
    depth = w_ref.shape[1]
    per = depth // LANES
    parts = []
    for b in range(j * TILE // LANES, (j + 1) * TILE // LANES):
        at = first + (b % per) * LANES
        parts.append(w_ref[b // per, :, at : at + LANES])
    return jnp.concatenate(parts, axis=1)


def key_kernel(
    place_ref, x_ref, ids_ref, w_ref, out_ref, qkv_ref, a_ref, x1_ref, h1_ref, act_ref, bias_ref
):
    rows_here, depth = x_ref.shape
    groups = w_ref.shape[0]
    small = small_rows(w_ref)
    for t in range(groups):
        bias_ref[:, t * depth : (t + 1) * depth] = hidden_row(w_ref, t)

    @pl.loop(0, rows_here // PACK)
    def _(pack):
        base = pl.multiple_of(pack * PACK, PACK)
        rows = pl.ds(base, PACK)
        key_side, query_side = enter(x_ref, ids_ref, small, h1_ref, base, pack)
        project_all(h1_ref[rows, :], w_ref, qkv_ref, key_side, base)
        attention(qkv_ref, a_ref, None, [(g, base) for g in range(groups)], [query_side] * groups)
        second = leave(x_ref, leaving(w_ref), small, a_ref, x1_ref, base)
        feed(second, w_ref, bias_ref, act_ref)
        product = mm_nt(act_ref[...], gathered(w_ref, ATT + depth, depth))
        out_ref[rows, :] = (x1_ref[rows, :] + product + small[5:6]).astype(BF)


def feed(second, w_ref, bias_ref, act_ref, first=ATT):
    tiles = act_ref.shape[1] // TILE
    pre = mm(second, tile_of(w_ref, 0, first))
    for j in range(tiles):
        later = mm(second, tile_of(w_ref, j + 1, first)) if j + 1 < tiles else None
        cols = slice(j * TILE, (j + 1) * TILE)
        bias = bias_ref[:, cols]
        for i in range(0, pre.shape[0], PIECE):
            piece = pre[i : i + PIECE] + bias
            act_ref[i : i + PIECE, cols] = (piece * below(piece)).astype(BF)
        pre = later


def query_kernel(
    place_ref,
    x_ref,
    cot_ref,
    ids_ref,
    w_ref,
    out_ref,
    qkv_ref,
    a_ref,
    lse_ref,
    h1_ref,
    dx1_ref,
    grad_ref,
    line_ref,
    hidden_ref,
    x1_ref,
    h2_ref,
    h2t_ref,
    eb_ref,
    ebt_ref,
    act_ref,
    dpre_ref,
    bias_ref,
):
    rows_here, depth = x_ref.shape
    groups = w_ref.shape[0]
    small = small_rows(w_ref)
    for t in range(groups):
        bias_ref[:, t * depth : (t + 1) * depth] = hidden_row(w_ref, t)

    lse_ref[...] = jnp.zeros_like(lse_ref)
    line_ref[...] = jnp.zeros_like(line_ref)
    h2t_ref[depth:, :] = jnp.ones((h2t_ref.shape[0] - depth, rows_here), BF)

    @pl.loop(0, rows_here // PACK)
    def _(pack):
        base = pl.multiple_of(pack * PACK, PACK)
        rows = pl.ds(base, PACK)
        key_side, query_side = enter(x_ref, ids_ref, small, h1_ref, base, pack)
        project_all(h1_ref[rows, :], w_ref, qkv_ref, key_side, base)
        attention(
            qkv_ref, a_ref, lse_ref, [(g, base) for g in range(groups)], [query_side] * groups
        )
        second = leave(x_ref, leaving(w_ref), small, a_ref, x1_ref, base)
        h2_ref[rows, :] = second
        h2t_ref[0:depth, rows] = second.T
        low = masked_cot(cot_ref, ids_ref, pack, rows).astype(BF)
        eb_ref[rows, :] = low
        ebt_ref[:, rows] = low.T

    feed_back(
        w_ref, ATT, h2_ref, h2t_ref, eb_ref, ebt_ref, bias_ref, act_ref, dpre_ref, grad_ref, hidden_ref
    )

    @pl.loop(0, rows_here // PACK)
    def _(pack):
        rows = pl.ds(pl.multiple_of(pack * PACK, PACK), PACK)
        x1 = x1_ref[rows, :]
        product = mm_nt(act_ref[rows, :], gathered(w_ref, ATT + depth, depth))
        out_ref[rows, :] = (x1 + product + small[5:6]).astype(BF)
        grad = mm_nt(dpre_ref[rows, :], gathered(w_ref, ATT, depth))
        unit, scale = norm_parts(x1)
        wide = masked_cot(cot_ref, ids_ref, pack, rows)
        dx1 = wide + norm_back(grad, unit, scale, small[2:3])
        dx1_ref[rows, :] = dx1
        line_ref[2:3, :] += jnp.sum(grad * unit, axis=0, keepdims=True)
        line_ref[3:4, :] += jnp.sum(grad, axis=0, keepdims=True)
        line_ref[4:5, :] += jnp.sum(dx1, axis=0, keepdims=True)
        line_ref[5:6, :] += jnp.sum(wide, axis=0, keepdims=True)


def feed_back(
    w_ref, first, h2_ref, h2t_ref, eb_ref, ebt_ref, bias_ref, act_ref, dpre_ref, grad_ref, hidden_ref
):
    rows_here, depth = h2_ref.shape
    tiles = act_ref.shape[1] // TILE
    per = depth // LANES
    step = PACK
    units = [(j, r) for j in range(tiles) for r in range(rows_here // step)]

    def start(unit):
        j, r = unit
        rows = slice(r * step, (r + 1) * step)
        pre = mm(h2_ref[rows, :], tile_of(w_ref, j, first))
        return (pre, mm(eb_ref[rows, :], tile_of(w_ref, j, first + depth)))

    now = start(units[0])
    for k, (j, r) in enumerate(units):
        later = start(units[k + 1]) if k + 1 < len(units) else None
        cols = slice(j * TILE, (j + 1) * TILE)
        bias = bias_ref[:, cols]
        pre, da = now
        for i in range(0, step, PIECE):
            rows = slice(r * step + i, r * step + i + PIECE)
            piece = pre[i : i + PIECE] + bias
            phi, slope = below_and_slope(piece)
            act_ref[rows, cols] = (piece * phi).astype(BF)
            dpre_ref[rows, cols] = (da[i : i + PIECE] * slope).astype(BF)
        now = later
        if (r + 1) * step == rows_here:
            gup = mm(h2t_ref[...], dpre_ref[:, cols])
            gdown = mm(ebt_ref[...], act_ref[:, cols])
            for n, b in enumerate((2 * j, 2 * j + 1)):
                t, o = b // per, (b % per) * LANES
                part = slice(n * LANES, (n + 1) * LANES)
                grad_ref[t, :, o : o + LANES] = gup[:depth, part].astype(BF)
                grad_ref[t, :, depth + o : depth + o + LANES] = gdown[:, part].astype(BF)
                hidden_ref[t : t + 1, o : o + LANES] = gup[depth : depth + 1, part]


def masked_cot(cot_ref, ids_ref, pack, rows):
    valid = jnp.where(ids_ref[pack] < CROPS, 1.0, 0.0)
    valid = jnp.broadcast_to(valid, (LANES, PACK)).T[:, 0:1]
    return cot_ref[rows, :].astype(F32) * valid


def attention_back(qkv_ref, a_ref, lse_ref, da_ref, dqkv_ref, places, sides):
    place = lax.broadcasted_iota(jnp.int32, (LANES, PACK), 0)
    head_of = place // HEAD_DIM
    lane = lax.broadcasted_iota(jnp.int32, (PACK, LANES), 1) // HEAD_DIM
    none = jnp.zeros((PACK, LANES), BF)

    def split(line):
        high = line.astype(BF).astype(F32)
        rest = line - high
        middle = rest.astype(BF).astype(F32)
        low = rest - middle
        block = jnp.where(
            place == ONES,
            high,
            jnp.where(place == ONES + 1, middle, jnp.where(place == ONES + 2, low, 0.0)),
        )
        return block.astype(BF)

    held, made = {}, {}
    heads = [(k, h) for k in range(len(places)) for h in range(HEADS_HERE)]

    def load(k):
        slot, base, da_at, _ = places[k]
        rows, at = pl.ds(base, PACK), slot * 3 * LANES
        query = qkv_ref[rows, at : at + LANES]
        keys = qkv_ref[rows, at + LANES : at + 2 * LANES]
        values = qkv_ref[rows, at + 2 * LANES : at + 3 * LANES]
        grad = da_ref[rows, da_at * LANES : (da_at + 1) * LANES]
        grad_t = grad.T
        mixed = a_ref[rows, slot * LANES : (slot + 1) * LANES].T
        both = mixed.astype(F32) * grad_t.astype(F32)
        held[k] = (query, keys, values, grad, query.T, keys.T, grad_t, both)

    def scores_of(k, h):
        if k not in held:
            load(k)
        slot, base, _, _ = places[k]
        query, keys, values, grad, query_t, keys_t, grad_t, both = held[k]
        part = slice(h * HEAD_DIM, (h + 1) * HEAD_DIM)
        line = slot * HEADS_HERE + h
        lse = lse_ref[line : line + 1, pl.ds(base, PACK)]
        side = jnp.where(place < ONES, sides[k], split(-lse))
        scores = mm(keys, jnp.where(head_of == h, query_t, side))
        inner = jnp.sum(both[part], axis=0, keepdims=True)
        pull = mm(values, jnp.where(head_of == h, grad_t, split(-inner)))
        return (scores, pull)

    def finish(k, h, low, dscores):
        query, keys, values, grad, query_t, keys_t, grad_t, both = held[k]
        part = slice(h * HEAD_DIM, (h + 1) * HEAD_DIM)
        dv = mm(low, jnp.where(lane == h, grad, none))
        dk = mm(dscores, jnp.where(lane == h, query, none))
        dq = mm(keys_t[part], dscores)
        if h:
            last = made[k]
            made[k] = (last[0] + [dq], last[1] + dk, last[2] + dv)
        else:
            made[k] = ([dq], dk, dv)
        if h == HEADS_HERE - 1:
            dqs, dk, dv = made[k]
            dqs = jnp.concatenate(dqs + [jnp.zeros((LANES - USED, PACK), F32)], axis=0)
            _, base, _, slot = places[k]
            rows, at = pl.ds(base, PACK), slot * 3 * LANES
            dqkv_ref[rows, at : at + LANES] = (dqs.T * SCALE).astype(BF)
            dqkv_ref[rows, at + LANES : at + 2 * LANES] = (dk * LOG_TWO).astype(BF)
            dqkv_ref[rows, at + 2 * LANES : at + 3 * LANES] = dv.astype(BF)

    now = scores_of(*heads[0])
    waiting = None
    for n, head in enumerate(heads):
        later = scores_of(*heads[n + 1]) if n + 1 < len(heads) else None
        if waiting is not None:
            finish(*waiting)
        scores, pull = now
        probs = jnp.exp2(scores)
        waiting = head + (probs.astype(BF), (probs * pull).astype(BF))
        now = later
    finish(*waiting)


def back_kernel(
    place_ref,
    x_ref,
    ids_ref,
    w_ref,
    qkv_ref,
    a_ref,
    lse_ref,
    h1_ref,
    dx1_ref,
    line_ref,
    hidden_ref,
    out_ref,
    grad_ref,
    da_ref,
    dqkv_ref,
    h1t_ref,
    dybt_ref,
    sums_ref,
):
    rows_here, depth = x_ref.shape
    groups = w_ref.shape[0]
    small = small_rows(w_ref)
    sums_ref[...] = jnp.zeros_like(sums_ref)
    sums_ref[SMALL_AT : SMALL_AT + 8, :] = line_ref[...]

    @pl.loop(0, rows_here // PACK)
    def _(pack):
        base = pl.multiple_of(pack * PACK, PACK)
        rows = pl.ds(base, PACK)
        _, query_side = id_lanes(ids_ref[pack])
        low = dx1_ref[rows, :].astype(BF)
        dybt_ref[:, rows] = low.T
        h1t_ref[:, rows] = h1_ref[rows, :].T
        for g in range(groups):
            da_ref[rows, g * LANES : (g + 1) * LANES] = mm(
                low, w_ref[g, :, 3 * LANES : 4 * LANES]
            ).astype(BF)
        places = [(g, base, g, g) for g in range(groups)]
        attention_back(qkv_ref, a_ref, lse_ref, da_ref, dqkv_ref, places, [query_side] * groups)
        width = 3 * LANES
        grad = mm_nt(dqkv_ref[rows, 0:width], w_ref[0, :, 0:width])
        for g in range(1, groups):
            grad += mm_nt(dqkv_ref[rows, g * width : (g + 1) * width], w_ref[g, :, 0:width])
        unit, scale = norm_parts(x_ref[rows, :].astype(F32))
        back = norm_back(grad, unit, scale, small[0:1])
        out_ref[rows, :] = (dx1_ref[rows, :] + back).astype(BF)
        sums_ref[SMALL_AT : SMALL_AT + 1, :] += jnp.sum(grad * unit, axis=0, keepdims=True)
        sums_ref[SMALL_AT + 1 : SMALL_AT + 2, :] += jnp.sum(grad, axis=0, keepdims=True)

    lane = lax.broadcasted_iota(jnp.int32, (depth, LANES), 1)
    for g in range(groups):
        width = 3 * LANES
        sums_ref[HIDDEN_AT : HIDDEN_AT + 1, :] = hidden_ref[g : g + 1, :]
        extra = sums_ref[...].T
        entry = mm(h1t_ref[...], dqkv_ref[:, g * width : (g + 1) * width])
        grad_ref[g, :, 0:LANES] = jnp.where(lane < USED, entry[:, :LANES], extra).astype(BF)
        grad_ref[g, :, LANES:width] = entry[:, LANES:].astype(BF)
        grad_ref[g, :, width : width + LANES] = mm(
            dybt_ref[...], a_ref[:, g * LANES : (g + 1) * LANES]
        ).astype(BF)


def params():
    return pltpu.CompilerParams(vmem_limit_bytes=60 * 2**20)


def whole(shape):
    return pl.BlockSpec(shape, lambda i, place: (0,) * len(shape))


def own_rows(rows, depth):
    return pl.BlockSpec((rows, depth), lambda i, place: (place[0], 0))


def own_ids(packs):
    return pl.BlockSpec((packs, 1, PACK), lambda i, place: (place[0], 0, 0))


def run_key(place, tokens, ids, weights, rows):
    depth = tokens.shape[1]
    groups, _, width = weights.shape
    return pl.pallas_call(
        key_kernel,
        grid_spec=pltpu.PrefetchScalarGridSpec(
            num_scalar_prefetch=1,
            grid=(1,),
            in_specs=[own_rows(rows, depth), own_ids(rows // PACK), whole(weights.shape)],
            out_specs=whole((rows, depth)),
            scratch_shapes=[
                VMEM((rows, groups * 3 * LANES), BF),
                VMEM((rows, groups * LANES), BF),
                VMEM((rows, depth), F32),
                VMEM((rows, depth), BF),
                VMEM((PACK, groups * depth), BF),
                VMEM((1, groups * depth), F32),
            ],
        ),
        out_shape=jax.ShapeDtypeStruct((rows, depth), BF),
        compiler_params=params(),
        name="key_block",
    )(place, tokens, ids, weights)


def run_query(place, tokens, cotangent, ids, weights, rows):
    depth = tokens.shape[1]
    groups = weights.shape[0]
    outs = [
        ((rows, depth), BF),
        ((rows, groups * 3 * LANES), BF),
        ((rows, groups * LANES), BF),
        ((16, rows), F32),
        ((rows, depth), BF),
        ((rows, depth), F32),
        ((groups, depth, 2 * depth), BF),
        ((8, depth), F32),
        ((groups, depth), F32),
    ]
    return pl.pallas_call(
        query_kernel,
        grid_spec=pltpu.PrefetchScalarGridSpec(
            num_scalar_prefetch=1,
            grid=(1,),
            in_specs=[
                own_rows(rows, depth),
                own_rows(rows, depth),
                own_ids(rows // PACK),
                whole(weights.shape),
            ],
            out_specs=[whole(shape) for shape, _ in outs],
            scratch_shapes=[
                VMEM((rows, depth), F32),
                VMEM((rows, depth), BF),
                VMEM((depth + 16, rows), BF),
                VMEM((rows, depth), BF),
                VMEM((depth, rows), BF),
                VMEM((rows, groups * depth), BF),
                VMEM((rows, groups * depth), BF),
                VMEM((1, groups * depth), F32),
            ],
        ),
        out_shape=[jax.ShapeDtypeStruct(shape, kind) for shape, kind in outs],
        compiler_params=params(),
        name="query_block",
    )(place, tokens, cotangent, ids, weights)


def run_back(place, tokens, ids, weights, kept, rows):
    depth = tokens.shape[1]
    groups = weights.shape[0]
    return pl.pallas_call(
        back_kernel,
        grid_spec=pltpu.PrefetchScalarGridSpec(
            num_scalar_prefetch=1,
            grid=(1,),
            in_specs=[own_rows(rows, depth), own_ids(rows // PACK), whole((groups, depth, ATT))]
            + [whole(item.shape) for item in kept],
            out_specs=[whole((rows, depth)), whole((groups, depth, ATT))],
            scratch_shapes=[
                VMEM((rows, groups * LANES), BF),
                VMEM((rows, groups * 3 * LANES), BF),
                VMEM((depth, rows), BF),
                VMEM((depth, rows), BF),
                VMEM((LANES, depth), F32),
            ],
        ),
        out_shape=[
            jax.ShapeDtypeStruct((rows, depth), BF),
            jax.ShapeDtypeStruct((groups, depth, ATT), BF),
        ],
        compiler_params=params(),
        name="back_block",
    )(place, tokens, ids, weights, *kept)


def pack_piece(entry, leave, up, down, small, hidden):
    def fill(block, *extra):
        block = jnp.concatenate([block] + [item.astype(block.dtype) for item in extra], axis=1)
        return jnp.pad(block, ((0, 0), (0, LANES - block.shape[1])))

    parts = [
        fill(entry[:, 0], small.T, hidden[:, None]),
        fill(entry[:, 1]),
        fill(entry[:, 2]),
        fill(leave.T),
        up,
        down.T,
    ]
    return jnp.concatenate([part.astype(BF) for part in parts], axis=1)


def unpack_piece(piece, depth):
    entry = jnp.stack([piece[:, k * LANES : k * LANES + USED] for k in range(3)], axis=1)
    leave = piece[:, 3 * LANES : 3 * LANES + USED].T
    up = piece[:, ATT : ATT + depth]
    down = piece[:, ATT + depth :].T
    small = piece[:, SMALL_AT : SMALL_AT + 6].T
    return (entry, leave, up, down, small, piece[:, HIDDEN_AT])


def adamw(grad, first, second, master, decay, rate):
    moment = BETA_ONE * first + (1.0 - BETA_ONE) * grad
    square = BETA_TWO * second + (1.0 - BETA_TWO) * grad * grad
    ahead = moment / (1.0 - BETA_ONE**STEP)
    spread = square / (1.0 - BETA_TWO**STEP)
    return (
        moment,
        square,
        master - rate * (ahead / (jnp.sqrt(spread) + ADAM_EPS) + decay * master),
    )


DECAYS = (DECAY, DECAY, DECAY, DECAY, 0.0, 0.0)
RATES = (RATE_MATRIX, RATE_EXIT, RATE_MATRIX, RATE_MATRIX, RATE_SMALL, RATE_BIAS)


def finish_plain(grad_att, grad_ffn, masters, firsts, seconds):
    depth = grad_att.shape[1]
    grads = jnp.concatenate([grad_att, grad_ffn], axis=2).astype(F32)
    own = lax.psum_scatter(grads, "tensor", scatter_dimension=0, tiled=False)
    own = lax.psum_scatter(own, "dp", scatter_dimension=0, tiled=True)
    shares = unpack_piece(own, depth)
    copies = float(lax.axis_size("tensor"))
    total = jnp.sum(shares[4] * shares[4]) / copies
    for k in (0, 1, 2, 3, 5):
        total = total + jnp.sum(shares[k] * shares[k])
    norm_value = jnp.sqrt(lax.psum(total, ("dp", "tensor")))
    factor = CLIP / jnp.maximum(norm_value, CLIP)
    outs = []
    for k in range(6):
        outs.extend(
            adamw(shares[k] * factor, firsts[k], seconds[k], masters[k], DECAYS[k], RATES[k])
        )
    return (norm_value, outs)


def spot():
    dp, t = lax.axis_index("dp"), lax.axis_index("tensor")
    return (dp, t)


def flip(value, bits):
    for bit in (1, 2, 4):
        if bits & bit:
            value = value + bit - 2 * bit * ((value // bit) % 2)
    return value


def hello(peers):
    barrier = pltpu.get_barrier_semaphore()
    for peer in peers:
        pl.semaphore_signal(barrier, inc=1, device_id=peer, device_id_type=MESH)


def wait_for(peers):
    pl.semaphore_wait(pltpu.get_barrier_semaphore(), len(peers))


KEY_PARTS = 3
SENDS = 62 + 9 + 12 + 51 + 10


class Mail:
    def __init__(self, send_sem, recv_sem):
        self.send_sem, self.recv_sem = send_sem, recv_sem
        self.count, self.sent = 0, []

    def send(self, src, dst, peer):
        copy = pltpu.make_async_remote_copy(
            src_ref=src,
            dst_ref=dst,
            send_sem=self.send_sem.at[self.count],
            recv_sem=self.recv_sem.at[self.count],
            device_id=peer,
            device_id_type=MESH,
        )
        copy.start()
        self.count += 1
        self.sent.append(copy)
        return copy

    def close(self):
        for copy in self.sent:
            copy.wait_send()


def arrived(copies):
    for copy in copies:
        copy.wait_recv()


def load_rows(src, dst, t, sem):
    count = dst.shape[0]
    copy = pltpu.make_async_copy(src.at[pl.ds(t * count, count)], dst, sem)
    copy.start()
    return copy


def fold(block):
    out = block[0:8]
    for k in range(8, block.shape[0], 8):
        out = out + block[k : k + 8]
    return out


class Reduce:
    def __init__(self, mail, grad_ref, refs, where):
        self.mail, self.grad = mail, grad_ref
        self.rc, self.s0, self.r1, self.s1, self.r2, self.s2, self.r3 = refs
        self.where = where
        self.core = [None, None]
        self.side = [None, None]
        self.line = [None, None]
        self.across = None

    def slab(self, group, k):
        rows = self.s1.shape[2]
        return self.grad.at[group, pl.ds(pl.multiple_of(k * rows, 16), rows)]

    def to_core(self, q):
        dp, t, core, across, side, line = self.where
        self.core[q] = self.mail.send(self.grad.at[flip(t, 1 + 2 * q)], self.rc.at[q], core)

    def to_side(self, q):
        dp, t, core, across, side, line = self.where
        self.core[q].wait_recv()
        own = flip(t, 2 * q)
        y = dp % 2
        rows = self.s1.shape[2]

        @pl.loop(0, 8)
        def _(k):
            part = pl.ds(pl.multiple_of(k * rows, 16), rows)
            left = self.grad[own, part, :].astype(F32)
            self.s0[q, k] = (left + self.rc[q, part, :].astype(F32)).astype(BF)

        self.side[q] = [
            self.mail.send(self.s0.at[q, 2 * w + 1 - y], self.r1.at[q, w], side) for w in range(4)
        ]

    def to_line(self, q):
        dp, t, core, across, side, line = self.where
        arrived(self.side[q])
        y = dp % 2

        @pl.loop(0, 4)
        def _(w):
            left = self.s0[q, 2 * w + y].astype(F32)
            self.s1[q, w] = (left + self.r1[q, w].astype(F32)).astype(BF)

        self.line[q] = [
            self.mail.send(self.s1.at[q, line[j][0] // 2], self.r2.at[q, j - 1], line[j])
            for j in range(1, 4)
        ]

    def to_across(self, q):
        dp, t, core, across, side, line = self.where
        arrived(self.line[q])
        total = self.s1[q, dp // 2].astype(F32)
        for j in range(3):
            total = total + self.r2[q, j].astype(F32)
        self.s2[q] = total.astype(BF)
        if q:
            self.across = self.mail.send(self.s2.at[1], self.r3, across)

    def result(self):
        self.across.wait_recv()
        return self.s2[0].astype(F32) + self.r3[...].astype(F32)


class Spread:
    def __init__(self, mail, where, own_ref, out_ref, first, sem):
        dp, t, core, across, side, line = where
        self.mail, self.where, self.out = mail, where, out_ref
        self.count = own_ref.shape[0]
        self.first = first
        here = self.part(t)
        self.across = mail.send(own_ref, here, across)
        self.core = [mail.send(own_ref, here, core)]
        self.local = pltpu.make_async_copy(own_ref, here, sem)
        self.local.start()

    def part(self, t):
        at = t * self.first[1] + self.first[0]
        return self.out.at[pl.ds(pl.multiple_of(at, 16), self.count)]

    def forward(self):
        dp, t, core, across, side, line = self.where
        self.across.wait_recv()
        far = self.part(flip(t, 2))
        self.core.append(self.mail.send(far, far, core))

    def finish(self):
        arrived(self.core)
        self.local.wait()


class Gather:
    def __init__(self, mail, where, own_ref, all_ref, sem):
        self.mail, self.where, self.own, self.all = mail, where, own_ref, all_ref
        dp, t, core, across, side, line = where
        self.local = pltpu.make_async_copy(own_ref, self.piece(t, dp), sem)
        self.local.start()

    def piece(self, group, dp):
        rows = self.own.shape[0]
        return self.all.at[group, pl.ds(pl.multiple_of(dp * rows, 16), rows)]

    def start_across(self):
        dp, t, core, across, side, line = self.where
        self.across = self.mail.send(self.own, self.piece(t, dp), across)

    def start(self):
        dp, t, core, across, side, line = self.where
        send, here = self.mail.send, self.piece(t, dp)
        self.line = [[send(self.own, here, line[j])] for j in range(1, 4)]
        self.side = [[send(self.own, here, side)], [], [], []]
        self.core = [[send(self.own, here, core)], []]

    def pass_across(self):
        dp, t, core, across, side, line = self.where
        send, far = self.mail.send, self.piece(flip(t, 2), dp)
        self.across.wait_recv()
        for j in range(1, 4):
            self.line[j - 1].append(send(far, far, line[j]))
        self.side[0].append(send(far, far, side))
        self.core[1].append(send(far, far, core))

    def pass_line(self, k):
        dp, t, core, across, side, line = self.where
        for j in range(1, 4):
            self.line[j - 1][k].wait_recv()
            piece = self.piece(flip(t, 2 * k), line[j][0])
            self.side[j].append(self.mail.send(piece, piece, side))
            self.core[k].append(self.mail.send(piece, piece, core))

    def pass_side(self, k):
        dp, t, core, across, side, line = self.where
        for j in range(4):
            self.side[j][k].wait_recv()
            piece = self.piece(flip(t, 2 * k), flip(line[j][0], 1))
            self.core[k].append(self.mail.send(piece, piece, core))

    def finish(self, k):
        arrived(self.core[k])


def block_kernel(*refs):
    entry_ref, leave_ref, up_ref, down_ref, small_ref, hidden_ref = refs[0:6]
    key_entry, key_leave, key_up, key_down, key_small, key_hidden = refs[6:12]
    tokens_ref, cot_all_ref, key_tokens_ref, crops_ref = refs[12:16]
    block_out, key_out, input_grad, norm_ref, own_a, own_f, own_s = refs[16:23]
    (
        kx_ref, qx_ref, cot_ref, ids_ref, pa_ref, pf_ref, keys_ref, wa_ref, wf_ref,
        kqkv_ref, qqkv_ref, ka_ref, qa_ref, lse_ref, kh_ref, h1_ref, kx1_ref, x1_ref,
        act_ref, dpre_ref, h2_ref, h2t_ref, eb_ref, ebt_ref, bias_ref, hid_ref, line_ref,
        unit_ref, scale_ref, h1t_ref, dyb_ref, dybt_ref, dqkv_ref, ga_ref, ge_ref, gf_ref,
        key_rows, block_rows, grad_rows, near_ref, far_ref, turn_ref,
    ) = refs[23:65]
    red_a, red_e, red_f = refs[65:72], refs[72:79], refs[79:86]
    send_sem, recv_sem, local_sem = refs[86:]
    dp, t = spot()
    far = flip(t, 2)
    core, across = (dp, flip(t, 1)), (dp, far)
    side = (flip(dp, 1), t)
    line = [(flip(dp, 2 * j), t) for j in range(4)]
    where = (dp, t, core, across, side, line)
    mail = Mail(send_sem, recv_sem)
    send = mail.send
    loads = [
        load_rows(src, dst, t, local_sem.at[k])
        for k, (src, dst) in enumerate(
            ((key_tokens_ref, kx_ref), (crops_ref, ids_ref), (tokens_ref, qx_ref), (cot_all_ref, cot_ref))
        )
    ]

    peers = [(dp, flip(t, k)) for k in (1, 2, 3)] + [(flip(dp, k), t) for k in range(1, 8)]
    hello(peers)
    rows, depth = up_ref.shape
    wide = LANES - USED
    extra = [small_ref[...], hidden_ref[...], jnp.zeros((wide - 7, rows), F32)]
    extra = jnp.concatenate(extra, axis=0).T
    blank = jnp.zeros((rows, wide), F32)
    for k, block in enumerate([entry_ref[0], entry_ref[1], entry_ref[2], leave_ref[...]]):
        block = jnp.concatenate([block, blank if k else extra], axis=1)
        pa_ref[:, k * LANES : (k + 1) * LANES] = block.astype(BF)
    wait_for(peers)
    gather_a = Gather(mail, where, pa_ref, wa_ref, local_sem.at[4])
    gather_a.start_across()
    gather_a.start()

    parts = [pl.ds(0, ATT), pl.ds(ATT, depth), pl.ds(ATT + depth, depth)]

    def key_part(group, k):
        return keys_ref.at[group, :, parts[k]]

    def key_send(k, peer):
        return send(key_part(t, k), key_part(t, k), peer)

    blank = jnp.zeros((wide, depth), BF)
    extra = [key_small[...], key_hidden[...], jnp.zeros((wide - 7, depth), BF)]
    for k, block in enumerate([key_entry[0], key_entry[1], key_entry[2], key_leave[...]]):
        block = jnp.concatenate([block] + ([blank] if k else extra), axis=0)
        keys_ref[t, :, k * LANES : (k + 1) * LANES] = block.T
    key_across = [key_send(0, across)]
    key_core = [key_send(0, core)]
    pf_ref[:, 0:depth] = up_ref[...].astype(BF)
    pf_ref[:, depth:] = down_ref[...].astype(BF)
    gather_f = Gather(mail, where, pf_ref, wf_ref, local_sem.at[5])
    gather_f.start_across()
    keys_ref[t, :, ATT : ATT + depth] = key_up[...]
    keys_ref[t, :, ATT + depth :] = key_down[...].T
    key_across += [key_send(k, across) for k in (1, 2)]
    key_core += [key_send(k, core) for k in (1, 2)]

    packs = kx_ref.shape[0] // PACK
    bases = [pack * PACK for pack in range(packs)]
    spots = [slice(base, base + PACK) for base in bases]
    loads[0].wait()
    loads[1].wait()
    key_norms = small_rows_of(keys_ref[t, :, 0:LANES])
    masks = [enter(kx_ref, ids_ref, key_norms, kh_ref, base, k) for k, base in enumerate(bases)]
    sides = [query_side for _, query_side in masks]

    def heads_of(slot, weight, first_ref, qkv_ref, a_ref, lse):
        for base, (key_side, _) in zip(bases, masks):
            project(first_ref[base : base + PACK, :], weight, qkv_ref, key_side, base, slot)
        attention(qkv_ref, a_ref, lse, [(slot, base) for base in bases], sides)

    def key_heads(slot):
        heads_of(slot, keys_ref[flip(t, slot), :, 0 : 3 * LANES], kh_ref, kqkv_ref, ka_ref, None)

    def query_heads(slot):
        heads_of(slot, wa_ref[flip(t, slot), :, 0 : 3 * LANES], h1_ref, qqkv_ref, qa_ref, lse_ref)

    def pass_key(k):
        key_across[k].wait_recv()
        return send(key_part(far, k), key_part(far, k), core)

    key_heads(0)
    gather_a.pass_across()
    gather_f.start()
    arrived(key_core[:1])
    key_heads(1)
    gather_a.pass_line(0)
    loads[2].wait()
    loads[3].wait()
    for k, spot_rows in enumerate(spots):
        low = masked_cot(cot_ref, ids_ref, k, spot_rows).astype(BF)
        eb_ref[spot_rows, :] = low
        ebt_ref[:, spot_rows] = low.T
        unit, scale = norm_parts(qx_ref[spot_rows, :].astype(F32))
        unit_ref[spot_rows, :] = unit
        scale_ref[spot_rows, :] = jnp.broadcast_to(scale, (PACK, LANES))
    gather_a.pass_side(0)
    gather_a.local.wait()
    norms = small_rows_of(wa_ref[t, :, 0:LANES])
    for spot_rows in spots:
        first = (unit_ref[spot_rows, :] * norms[0:1] + norms[1:2]).astype(BF)
        h1_ref[spot_rows, :] = first
        h1t_ref[:, spot_rows] = first.T
    query_heads(0)
    gather_a.pass_line(1)
    key_far = [pass_key(0)]
    gather_f.pass_across()
    key_heads(2)
    arrived(key_far)
    key_heads(3)
    gather_f.pass_line(0)
    gather_a.pass_side(1)
    gather_a.finish(0)
    query_heads(1)
    query_heads(2)
    gather_a.finish(1)
    gather_f.pass_side(0)
    query_heads(3)
    gather_f.pass_line(1)
    key_far.append(pass_key(1))

    def leaving_of(w_ref):
        weights = [w_ref[flip(t, k), :, 3 * LANES : 4 * LANES] for k in range(4)]
        return jnp.concatenate(weights, axis=1)

    weight = leaving_of(keys_ref)
    for base in bases:
        second = leave(kx_ref, weight, key_norms, ka_ref, kx1_ref, base)
        kh_ref[base : base + PACK, :] = second
    for k in range(4):
        bias_ref[:, k * depth : (k + 1) * depth] = hidden_line(keys_ref[k, :, 0:LANES])
    arrived(key_core[1:2] + key_far[1:2])
    feed(kh_ref[spots[0], :], keys_ref, bias_ref, act_ref.at[spots[0]])
    key_far.append(pass_key(2))
    feed(kh_ref[spots[1], :], keys_ref, bias_ref, act_ref.at[spots[1]])
    gather_f.pass_side(1)
    arrived(key_core[2:] + key_far[2:])
    weight = gathered(keys_ref, ATT + depth, depth)
    for spot_rows in spots:
        product = mm_nt(act_ref[spot_rows, :], weight)
        key_rows[spot_rows, :] = (kx1_ref[spot_rows, :] + product + key_norms[5:6]).astype(BF)
    count = key_rows.shape[0]
    spread_key = Spread(mail, where, key_rows, key_out, (0, count), local_sem.at[6])
    weight = leaving_of(wa_ref)
    for base in bases:
        second = leave(qx_ref, weight, norms, qa_ref, x1_ref, base)
        h2_ref[base : base + PACK, :] = second
        h2t_ref[0:depth, base : base + PACK] = second.T
    h2t_ref[depth:, :] = jnp.ones((h2t_ref.shape[0] - depth, h2t_ref.shape[1]), BF)
    gather_f.finish(0)
    gather_f.finish(1)
    gather_f.local.wait()
    for k in range(4):
        bias_ref[:, k * depth : (k + 1) * depth] = hidden_line(wa_ref[k, :, 0:LANES])
    feed_back(
        wf_ref, 0, h2_ref, h2t_ref, eb_ref, ebt_ref, bias_ref, act_ref, dpre_ref, gf_ref, hid_ref
    )
    reduce_f = Reduce(mail, gf_ref, red_f, where)
    reduce_f.to_core(0)
    reduce_f.to_core(1)
    weight = gathered(wf_ref, depth, depth)
    for spot_rows in spots:
        product = mm_nt(act_ref[spot_rows, :], weight)
        block_rows[spot_rows, :] = (x1_ref[spot_rows, :] + product + norms[5:6]).astype(BF)
    spread_block = Spread(mail, where, block_rows, block_out, (0, count), local_sem.at[7])
    line_ref[...] = jnp.zeros_like(line_ref)
    weight = gathered(wf_ref, 0, depth)
    for k, spot_rows in enumerate(spots):
        grad = mm_nt(dpre_ref[spot_rows, :], weight)
        unit, scale = norm_parts(x1_ref[spot_rows, :])
        wide_cot = masked_cot(cot_ref, ids_ref, k, spot_rows)
        dx1 = wide_cot + norm_back(grad, unit, scale, norms[2:3])
        x1_ref[spot_rows, :] = dx1
        low = dx1.astype(BF)
        dyb_ref[spot_rows, :] = low
        dybt_ref[:, spot_rows] = low.T
        line_ref[2:3, :] += jnp.sum(grad * unit, axis=0, keepdims=True)
        line_ref[3:4, :] += jnp.sum(grad, axis=0, keepdims=True)
        line_ref[4:5, :] += jnp.sum(dx1, axis=0, keepdims=True)
        line_ref[5:6, :] += jnp.sum(wide_cot, axis=0, keepdims=True)
    mixed = mm(dybt_ref[...], qa_ref[...]).astype(BF)
    for slot in range(4):
        ge_ref[flip(t, slot)] = mixed[:, slot * LANES : (slot + 1) * LANES]
    reduce_f.to_side(0)
    reduce_f.to_side(1)

    reduce_a = Reduce(mail, ga_ref, red_a, where)
    reduce_e = Reduce(mail, ge_ref, red_e, where)
    reduce_e.to_core(0)
    reduce_e.to_core(1)
    lane = lax.broadcasted_iota(jnp.int32, (depth, LANES), 1)
    width = 3 * LANES

    weight = leaving_of(wa_ref)
    for base in bases:
        ka_ref[base : base + PACK, :] = mm(dyb_ref[base : base + PACK, :], weight).astype(BF)

    def back_heads(slots, pack):
        places = [(slot, bases[pack], slot, slot) for slot in slots]
        side = [sides[pack]] * len(slots)
        attention_back(qqkv_ref, qa_ref, lse_ref, ka_ref, dqkv_ref, places, side)

    def back_weights(slot):
        group = flip(t, slot)
        entry = mm(h1t_ref[...], dqkv_ref[:, slot * width : (slot + 1) * width])
        hidden = jnp.broadcast_to(hid_ref[pl.ds(group, 1), :], (LANES, depth)).T
        ga_ref[group, :, 0:LANES] = jnp.where(lane == HIDDEN_AT, hidden, entry[:, :LANES]).astype(BF)
        ga_ref[group, :, LANES:width] = entry[:, LANES:].astype(BF)

    def back_rows(pack):
        spot_rows = spots[pack]
        weight = jnp.concatenate([wa_ref[flip(t, k), :, 0:width] for k in range(4)], axis=1)
        grad = mm_nt(dqkv_ref[spot_rows, :], weight)
        unit, scale = unit_ref[spot_rows, :], scale_ref[spot_rows, 0:1]
        back = norm_back(grad, unit, scale, norms[0:1])
        grad_rows[spot_rows, :] = (x1_ref[spot_rows, :] + back).astype(BF)
        first = (pack * PACK, count)
        sem = local_sem.at[8 + pack]
        item = Spread(mail, where, grad_rows.at[spot_rows], input_grad, first, sem)
        line_ref[0:1, :] += jnp.sum(grad * unit, axis=0, keepdims=True)
        line_ref[1:2, :] += jnp.sum(grad, axis=0, keepdims=True)
        return item

    back_heads((3, 2), 0)
    reduce_e.to_side(0)
    reduce_e.to_side(1)
    spread_key.forward()
    back_heads((1, 0), 0)
    reduce_f.to_line(0)
    spread_grad = [back_rows(0)]
    back_heads((3,), 1)
    back_weights(3)
    reduce_a.to_core(1)
    reduce_f.to_line(1)
    back_heads((2,), 1)
    back_weights(2)
    reduce_a.to_side(1)
    reduce_e.to_line(0)
    reduce_e.to_line(1)
    spread_block.forward()
    back_heads((1,), 1)
    back_weights(1)
    reduce_a.to_core(0)
    reduce_a.to_line(1)
    reduce_f.to_across(0)
    reduce_f.to_across(1)
    reduce_e.to_across(0)
    reduce_e.to_across(1)
    back_heads((0,), 1)
    back_weights(0)
    reduce_a.to_side(0)
    reduce_a.to_across(1)
    spread_grad.append(back_rows(1))
    reduce_a.to_line(0)
    grad_e = reduce_e.result()
    grad_f = reduce_f.result()
    spread_grad[0].forward()
    reduce_a.to_across(0)
    grad_a = jnp.concatenate([reduce_a.result(), grad_e], axis=1)

    total = jnp.zeros((8, LANES), F32)
    lane = lax.broadcasted_iota(jnp.int32, (rows, LANES), 1)
    for k in range(4):
        block = grad_a[:, k * LANES : (k + 1) * LANES]
        share = jnp.where(lane < USED, 1.0, jnp.where(lane == HIDDEN_AT, 0.0 if k else 1.0, 0.0))
        total = total + fold(block * block * share)
    for k in range(2 * depth // LANES):
        block = grad_f[:, k * LANES : (k + 1) * LANES]
        total = total + fold(block * block)
    near_ref[t, 0:8, :] = line_ref[...]
    near_ref[t, 8:16, :] = jnp.concatenate([total] + [jnp.zeros_like(total)] * 2, axis=1)
    near = [send(near_ref.at[t], near_ref.at[t], (dp, flip(t, k))) for k in (1, 2, 3)]
    own_a[...] = grad_a
    own_f[...] = grad_f
    spread_grad[1].forward()
    arrived(near)
    far_ref[dp] = (near_ref[0] + near_ref[1]) + (near_ref[2] + near_ref[3])
    wide_sends = [send(far_ref.at[dp], far_ref.at[dp], (flip(dp, k), t)) for k in range(1, 8)]
    arrived(wide_sends)
    total = far_ref[0]
    for k in range(1, 8):
        total = total + far_ref[k]
    lines = total[0:8]
    squares = fold(total[8:16, 0:LANES])
    for k in range(depth // LANES):
        block = lines[:, k * LANES : (k + 1) * LANES]
        squares = squares + block * block
    squares = jnp.sum(jnp.sum(squares, axis=0, keepdims=True), axis=1, keepdims=True)
    norm_ref[...] = jnp.broadcast_to(jnp.sqrt(squares), norm_ref.shape)
    turn_ref[...] = jnp.concatenate([lines, jnp.zeros((LANES - 8, depth), F32)], axis=0).T
    own_s[...] = turn_ref[pl.ds(pl.multiple_of(dp * rows, 16), rows), :]
    for item in [spread_key, spread_block] + spread_grad:
        item.finish()
    mail.close()


def lay(entry, leave, up, down, small, hidden):
    return [entry.transpose(1, 0, 2), leave.T, up, down.T, small, hidden.reshape(1, -1)]


def run_block(masters, keys, tokens, cotangent, key_tokens, ids, dp, tensor):
    key_entry, key_leave, key_up, key_down, key_small, key_hidden = keys
    rows, depth = masters[2].shape
    all_rows = tokens.shape[0]
    count = all_rows // tensor
    args = lay(*masters)
    args += [key_entry.transpose(1, 2, 0), key_leave, key_up, key_down, key_small]
    args.append(key_hidden.reshape(1, -1))

    def all_of(shape):
        return pl.BlockSpec(shape, lambda i: (0,) * len(shape))

    anywhere = pl.BlockSpec(memory_space=pl.ANY)
    hidden = tensor * depth
    scratch = [
        ((count, depth), BF),
        ((count, depth), BF),
        ((count, depth), BF),
        ((count // PACK, 1, PACK), jnp.int32),
        ((rows, ATT), BF),
        ((rows, 2 * depth), BF),
        ((tensor, depth, ATT + 2 * depth), BF),
        ((tensor, depth, ATT), BF),
        ((tensor, depth, 2 * depth), BF),
        ((count, tensor * 3 * LANES), BF),
        ((count, tensor * 3 * LANES), BF),
        ((count, tensor * LANES), BF),
        ((count, tensor * LANES), BF),
        ((16, count), F32),
        ((count, depth), BF),
        ((count, depth), BF),
        ((count, depth), F32),
        ((count, depth), F32),
        ((count, hidden), BF),
        ((count, hidden), BF),
        ((count, depth), BF),
        ((depth + 16, count), BF),
        ((count, depth), BF),
        ((depth, count), BF),
        ((1, hidden), F32),
        ((8, depth), F32),
        ((8, depth), F32),
        ((count, depth), F32),
        ((count, LANES), F32),
        ((depth, count), BF),
        ((count, depth), BF),
        ((depth, count), BF),
        ((count, tensor * 3 * LANES), BF),
        ((tensor, depth, 3 * LANES), BF),
        ((tensor, depth, LANES), BF),
        ((tensor, depth, 2 * depth), BF),
        ((count, depth), BF),
        ((count, depth), BF),
        ((count, depth), BF),
        ((tensor, 16, depth), F32),
        ((dp, 16, depth), F32),
        ((depth, LANES), F32),
    ]
    for wide in (3 * LANES, LANES, 2 * depth):
        scratch += [
            ((2, depth, wide), BF),
            ((2, 8, rows, wide), BF),
            ((2, 4, rows, wide), BF),
            ((2, 4, rows, wide), BF),
            ((2, 3, rows, wide), BF),
            ((2, rows, wide), BF),
            ((rows, wide), BF),
        ]
    outs = [
        ((all_rows, depth), BF),
        ((all_rows, depth), BF),
        ((all_rows, depth), BF),
        ((8, LANES), F32),
        ((rows, ATT), F32),
        ((rows, 2 * depth), F32),
        ((rows, LANES), F32),
    ]
    return pl.pallas_call(
        block_kernel,
        grid=(1,),
        in_specs=[all_of(item.shape) for item in args] + [anywhere] * 4,
        out_specs=[anywhere] * 3 + [all_of(shape) for shape, _ in outs[3:]],
        scratch_shapes=[VMEM(shape, kind) for shape, kind in scratch]
        + [
            pltpu.SemaphoreType.DMA((SENDS,)),
            pltpu.SemaphoreType.DMA((SENDS,)),
            pltpu.SemaphoreType.DMA((10,)),
        ],
        out_shape=[jax.ShapeDtypeStruct(shape, kind) for shape, kind in outs],
        compiler_params=pltpu.CompilerParams(
            collective_id=1, has_side_effects=True, vmem_limit_bytes=63 * 2**20
        ),
        name="block_forward_and_backward",
    )(*args, tokens, cotangent, key_tokens, ids)


def step_kernel(*refs):
    for src, dst in zip(refs[0:3], refs[25:28]):
        dst[...] = src[...]

    @pl.when(pl.program_id(0) == 0)
    def _():
        step_states(*refs[3:25], *refs[28:])


def step_states(norm_ref, ga_ref, gb_ref, gs_ref, *refs):
    masters, firsts, seconds = refs[0:6], refs[6:12], refs[12:18]
    value_ref, outs = refs[18], refs[19:]
    norm_value = norm_ref[0:1, 0:1]
    value_ref[...] = norm_value
    factor = CLIP / jnp.maximum(norm_value, CLIP)
    grad_a = ga_ref[...] * factor
    grad_b = gb_ref[...] * factor
    depth = grad_b.shape[1] // 2

    def update(k, at, grad):
        new = adamw(grad, firsts[k][at], seconds[k][at], masters[k][at], DECAYS[k], RATES[k])
        for j in range(3):
            outs[3 * k + j][at] = new[j]

    for j in range(3):
        update(0, j, grad_a[:, j * LANES : j * LANES + USED])
    update(1, slice(None), grad_a[:, 3 * LANES : 3 * LANES + USED])
    update(2, slice(None), grad_b[:, :depth])
    update(3, slice(None), grad_b[:, depth:])
    update(4, slice(None), (gs_ref[...] * factor).T[0:6])
    update(5, slice(None), grad_a[:, :LANES].T[HIDDEN_AT : HIDDEN_AT + 1])


def run_step(large, norm_tile, grad_a, grad_b, grad_s, masters, firsts, seconds):
    state = lay(*masters) + lay(*firsts) + lay(*seconds)
    shapes = [jax.ShapeDtypeStruct((1, 1), F32)]
    for item in state[:6]:
        shapes.extend([jax.ShapeDtypeStruct(item.shape, F32)] * 3)
    args = [norm_tile, grad_a, grad_b, grad_s] + state

    def all_of(shape):
        return pl.BlockSpec(shape, lambda i: (0,) * len(shape))

    rows, depth = large[0].shape
    block = pl.BlockSpec((PACK, depth), lambda i: (i, 0))
    result = pl.pallas_call(
        step_kernel,
        grid=(rows // PACK,),
        in_specs=[block] * 3 + [all_of(item.shape) for item in args],
        out_specs=[block] * 3 + [all_of(item.shape) for item in shapes],
        out_shape=[jax.ShapeDtypeStruct(item.shape, item.dtype) for item in large] + shapes,
        compiler_params=pltpu.CompilerParams(vmem_limit_bytes=63 * 2**20),
        name="optimizer_step",
    )(*large, *args)
    large, result = result[:3], result[3:]
    outs = list(result[1:])
    for k in range(3):
        outs[k] = outs[k].transpose(1, 0, 2)
        outs[3 + k] = outs[3 + k].T
        outs[9 + k] = outs[9 + k].T
        outs[15 + k] = outs[15 + k].reshape(-1)
    return (large, result[0].reshape(()), outs)


def on_device(*args):
    tokens, crop_ids, cotangent, key_tokens = args[:4]
    masters, firsts, seconds, keys = args[4:10], args[10:16], args[16:22], args[22:28]
    count, groups = lax.axis_size("dp"), lax.axis_size("tensor")
    ids = crop_ids.reshape(-1, 1, PACK)
    if count == 8 and groups == 4:
        result = run_block(masters, keys, tokens, cotangent, key_tokens, ids, count, groups)
        large, norm_value, outs = run_step(result[:3], *result[3:], masters, firsts, seconds)
        return (*large, norm_value, *outs)
    rows = tokens.shape[0] // groups
    place = lax.axis_index("tensor").astype(jnp.int32)[None]
    key_weights = lax.all_gather(pack_piece(*keys), "tensor", axis=0)
    weights = lax.all_gather(pack_piece(*masters), "dp", axis=0, tiled=True)
    weights = lax.all_gather(weights, "tensor", axis=0)

    def spread(own):
        return lax.all_gather(own, "tensor", axis=0, tiled=True)

    key_out = spread(run_key(place, key_tokens, ids, key_weights, rows))
    forward = run_query(place, tokens, cotangent, ids, weights, rows)
    block_out = spread(forward[0])
    qkv, a, lse, h1, dx1, grad_ffn, lines, hidden = forward[1:]
    grad_rows, grad_att = run_back(
        place, tokens, ids, weights, (qkv, a, lse, h1, dx1, lines, hidden), rows
    )
    input_grad = spread(grad_rows)
    norm_value, outs = finish_plain(grad_att, grad_ffn, masters, firsts, seconds)
    return (block_out, key_out, input_grad, norm_value, *outs)


def solution(mesh):
    rows, line = P("dp", None), P("dp")
    entry, leave, up, down = P("dp", None, "tensor"), P("tensor", "dp"), P("dp", "tensor"), P("tensor", "dp")
    state = (entry, leave, up, down, P(None, "dp"), P(("tensor", "dp")))
    keys = (P(None, None, "tensor"), P("tensor", None), P(None, "tensor"), P("tensor", None), P(), P("tensor"))
    outs = tuple(spec for spec in state for _ in range(3))
    return jax.shard_map(
        on_device,
        mesh=mesh,
        in_specs=(rows, line, rows, rows) + state * 3 + keys,
        out_specs=(rows, rows, rows, P()) + outs,
        check_vma=False,
    )
```

```python
import math
from functools import partial

import jax
import jax.numpy as jnp
from jax import lax
from jax.experimental import pallas as pl
from jax.experimental.pallas import tpu as pltpu
from jax.sharding import PartitionSpec as P

HEAD_DIM = 32
PACK = 512
CROPS = 5
STEP = 10
LN_EPS = 1e-06
CLIP = 1.0
RATE_MATRIX = 0.03
RATE_EXIT = 0.2
RATE_SMALL = 0.5
RATE_BIAS = 0.3
BETA_ONE = 0.9
BETA_TWO = 0.999
ADAM_EPS = 1e-08
DECAY = 0.05
MASKED = -1e30

SCALE = HEAD_DIM ** (-0.5)
EXP_SCALE = SCALE * math.log2(math.e)
LOG_TWO = math.log(2.0)
LANES = 128
TILE = 2 * LANES
PIECE = 64
HEADS_HERE = 3
USED = HEADS_HERE * HEAD_DIM
ONES = USED + CROPS + 1
ATT = 4 * LANES
SMALL_AT = USED
HIDDEN_AT = USED + 6
MESH = pl.DeviceIdType.MESH
BF = jnp.bfloat16
F32 = jnp.float32
VMEM = pltpu.VMEM
NT = (((1,), (1,)), ((), ()))
TN = (((0,), (0,)), ((), ()))

def mm(left, right):
    return jnp.dot(left, right, preferred_element_type=F32)


def mm_nt(left, right):
    return lax.dot_general(left, right, NT, preferred_element_type=F32)


def norm_parts(values):
    mean = jnp.mean(values, axis=1, keepdims=True)
    centred = values - mean
    spread = jnp.mean(centred * centred, axis=1, keepdims=True)
    scale = lax.rsqrt(spread + LN_EPS)
    return (centred * scale, scale)


def norm_back(grad, unit, scale, gain):
    scaled = grad * gain
    first = jnp.mean(scaled, axis=1, keepdims=True)
    second = jnp.mean(scaled * unit, axis=1, keepdims=True)
    return scale * (scaled - first - unit * second)


def below(pre):
    return 0.5 + 0.5 * lax.erf(pre * math.sqrt(0.5))


def below_and_slope(pre):
    phi = below(pre)
    bell = jnp.exp2((pre * (-0.5 * math.log2(math.e))) * pre)
    return (phi, phi + (pre * (1.0 / math.sqrt(2.0 * math.pi))) * bell)


def small_rows_of(weight):
    return weight.astype(F32).T[SMALL_AT : SMALL_AT + 6]


def hidden_line(weight):
    return weight.astype(F32).T[HIDDEN_AT : HIDDEN_AT + 1]


def small_rows(w_ref):
    return small_rows_of(w_ref[0, :, 0:LANES])


def hidden_row(w_ref, t):
    return hidden_line(w_ref[t, :, 0:LANES])


def crop_line(ids_ref, pack):
    if len(ids_ref.shape) == 1:
        return ids_ref[pl.ds(pack * PACK, PACK)].reshape(1, PACK)
    return ids_ref[pack]


def id_lanes(ids):
    place = lax.broadcasted_iota(jnp.int32, (LANES, PACK), 0)
    match = (place - USED) == ids
    ones = (place >= ONES) & (place < ONES + 3)
    key_side = jnp.where(match | ones, 1.0, 0.0).T
    crop = (place >= USED) & (place < ONES)
    query_side = jnp.where(crop & jnp.logical_not(match), MASKED, 0.0).astype(BF)
    return (key_side, query_side)


def attention(qkv_ref, a_ref, lse_ref, places, sides):
    place = lax.broadcasted_iota(jnp.int32, (LANES, PACK), 0) // HEAD_DIM
    ones = jnp.ones((16, PACK), BF)
    blank = jnp.zeros((LANES - USED, PACK), F32)
    heads = [(k, h) for k in range(len(places)) for h in range(HEADS_HERE)]
    held, outs = {}, {}

    def scores_of(k, h):
        if k not in held:
            slot, base = places[k]
            rows, at = pl.ds(base, PACK), slot * 3 * LANES
            query = qkv_ref[rows, at : at + LANES].T
            keys = qkv_ref[rows, at + LANES : at + 2 * LANES]
            values = qkv_ref[rows, at + 2 * LANES : at + 3 * LANES].T
            held[k] = (query, keys, values)
        query, keys, _ = held[k]
        return mm(keys, jnp.where(place == h, query, sides[k]))

    def mix(k, h, top, probs):
        slot, base = places[k]
        rows = pl.ds(base, PACK)
        values = held[k][2][h * HEAD_DIM : (h + 1) * HEAD_DIM]
        mixed = mm(jnp.concatenate([values, ones], axis=0), probs)
        total = mixed[HEAD_DIM : HEAD_DIM + 1]
        outs[(k, h)] = mixed[:HEAD_DIM] * (1.0 / total)
        if lse_ref is not None:
            line = slot * HEADS_HERE + h
            lse_ref[line : line + 1, rows] = top + jnp.log2(total)
        if h == HEADS_HERE - 1:
            parts = [outs[(k, n)] for n in range(HEADS_HERE)] + [blank]
            a_ref[rows, slot * LANES : (slot + 1) * LANES] = (
                jnp.concatenate(parts, axis=0).T.astype(BF)
            )

    scores = scores_of(*heads[0])
    waiting = None
    for n, head in enumerate(heads):
        later = scores_of(*heads[n + 1]) if n + 1 < len(heads) else None
        if waiting is not None:
            mix(*waiting)
        top = jnp.max(scores, axis=0, keepdims=True)
        waiting = head + (top, jnp.exp2(scores - top).astype(BF))
        scores = later
    mix(*waiting)


def enter(x_ref, ids_ref, small, h1_ref, base, pack):
    rows = pl.ds(base, PACK)
    values = x_ref[rows, :].astype(F32)
    unit, _ = norm_parts(values)
    first = (unit * small[0:1] + small[1:2]).astype(BF)
    h1_ref[rows, :] = first
    return id_lanes(crop_line(ids_ref, pack))


def project(first, weight, qkv_ref, key_side, base, slot):
    rows, at = pl.ds(base, PACK), slot * 3 * LANES
    packed = mm(first, weight)
    qkv_ref[rows, at : at + LANES] = (packed[:, :LANES] * EXP_SCALE).astype(BF)
    for k in (1, 2):
        part = packed[:, k * LANES : (k + 1) * LANES] + key_side
        qkv_ref[rows, at + k * LANES : at + (k + 1) * LANES] = part.astype(BF)


def project_all(first, w_ref, qkv_ref, key_side, base):
    for g in range(w_ref.shape[0]):
        project(first, w_ref[g, :, 0 : 3 * LANES], qkv_ref, key_side, base, g)


def leaving(w_ref):
    return gathered(w_ref, 3 * LANES, LANES)


def leave(x_ref, weight, small, a_ref, x1_ref, base):
    rows = pl.ds(base, PACK)
    branch = mm_nt(a_ref[rows, :], weight)
    x1 = x_ref[rows, :].astype(F32) + branch + small[4:5]
    x1_ref[rows, :] = x1
    unit, _ = norm_parts(x1)
    return (unit * small[2:3] + small[3:4]).astype(BF)


def gathered(w_ref, at, width):
    parts = [w_ref[t, :, at : at + width] for t in range(w_ref.shape[0])]
    return jnp.concatenate(parts, axis=1)


def tile_of(w_ref, j, first):
    depth = w_ref.shape[1]
    per = depth // LANES
    parts = []
    for b in range(j * TILE // LANES, (j + 1) * TILE // LANES):
        at = first + (b % per) * LANES
        parts.append(w_ref[b // per, :, at : at + LANES])
    return jnp.concatenate(parts, axis=1)


def key_kernel(
    place_ref, x_ref, ids_ref, w_ref, out_ref, qkv_ref, a_ref, x1_ref, h1_ref, act_ref, bias_ref
):
    rows_here, depth = x_ref.shape
    groups = w_ref.shape[0]
    small = small_rows(w_ref)
    for t in range(groups):
        bias_ref[:, t * depth : (t + 1) * depth] = hidden_row(w_ref, t)

    @pl.loop(0, rows_here // PACK)
    def _(pack):
        base = pl.multiple_of(pack * PACK, PACK)
        rows = pl.ds(base, PACK)
        key_side, query_side = enter(x_ref, ids_ref, small, h1_ref, base, pack)
        project_all(h1_ref[rows, :], w_ref, qkv_ref, key_side, base)
        attention(qkv_ref, a_ref, None, [(g, base) for g in range(groups)], [query_side] * groups)
        second = leave(x_ref, leaving(w_ref), small, a_ref, x1_ref, base)
        feed(second, w_ref, bias_ref, act_ref)
        product = mm_nt(act_ref[...], gathered(w_ref, ATT + depth, depth))
        out_ref[rows, :] = (x1_ref[rows, :] + product + small[5:6]).astype(BF)


def feed(second, w_ref, bias_ref, act_ref, first=ATT):
    tiles = act_ref.shape[1] // TILE
    pre = mm(second, tile_of(w_ref, 0, first))
    for j in range(tiles):
        later = mm(second, tile_of(w_ref, j + 1, first)) if j + 1 < tiles else None
        cols = slice(j * TILE, (j + 1) * TILE)
        bias = bias_ref[:, cols]
        for i in range(0, pre.shape[0], PIECE):
            piece = pre[i : i + PIECE] + bias
            act_ref[i : i + PIECE, cols] = (piece * below(piece)).astype(BF)
        pre = later


def query_kernel(
    place_ref,
    x_ref,
    cot_ref,
    ids_ref,
    w_ref,
    out_ref,
    qkv_ref,
    a_ref,
    lse_ref,
    h1_ref,
    dx1_ref,
    grad_ref,
    line_ref,
    hidden_ref,
    x1_ref,
    h2_ref,
    h2t_ref,
    eb_ref,
    ebt_ref,
    act_ref,
    dpre_ref,
    bias_ref,
):
    rows_here, depth = x_ref.shape
    groups = w_ref.shape[0]
    small = small_rows(w_ref)
    for t in range(groups):
        bias_ref[:, t * depth : (t + 1) * depth] = hidden_row(w_ref, t)

    lse_ref[...] = jnp.zeros_like(lse_ref)
    line_ref[...] = jnp.zeros_like(line_ref)
    h2t_ref[depth:, :] = jnp.ones((h2t_ref.shape[0] - depth, rows_here), BF)

    @pl.loop(0, rows_here // PACK)
    def _(pack):
        base = pl.multiple_of(pack * PACK, PACK)
        rows = pl.ds(base, PACK)
        key_side, query_side = enter(x_ref, ids_ref, small, h1_ref, base, pack)
        project_all(h1_ref[rows, :], w_ref, qkv_ref, key_side, base)
        attention(
            qkv_ref, a_ref, lse_ref, [(g, base) for g in range(groups)], [query_side] * groups
        )
        second = leave(x_ref, leaving(w_ref), small, a_ref, x1_ref, base)
        h2_ref[rows, :] = second
        h2t_ref[0:depth, rows] = second.T
        low = masked_cot(cot_ref, ids_ref, pack, rows).astype(BF)
        eb_ref[rows, :] = low
        ebt_ref[:, rows] = low.T

    feed_back(
        w_ref, ATT, h2_ref, h2t_ref, eb_ref, ebt_ref, bias_ref, act_ref, dpre_ref, grad_ref, hidden_ref
    )

    @pl.loop(0, rows_here // PACK)
    def _(pack):
        rows = pl.ds(pl.multiple_of(pack * PACK, PACK), PACK)
        x1 = x1_ref[rows, :]
        product = mm_nt(act_ref[rows, :], gathered(w_ref, ATT + depth, depth))
        out_ref[rows, :] = (x1 + product + small[5:6]).astype(BF)
        grad = mm_nt(dpre_ref[rows, :], gathered(w_ref, ATT, depth))
        unit, scale = norm_parts(x1)
        wide = masked_cot(cot_ref, ids_ref, pack, rows)
        dx1 = wide + norm_back(grad, unit, scale, small[2:3])
        dx1_ref[rows, :] = dx1
        line_ref[2:3, :] += jnp.sum(grad * unit, axis=0, keepdims=True)
        line_ref[3:4, :] += jnp.sum(grad, axis=0, keepdims=True)
        line_ref[4:5, :] += jnp.sum(dx1, axis=0, keepdims=True)
        line_ref[5:6, :] += jnp.sum(wide, axis=0, keepdims=True)


def feed_back(
    w_ref, first, h2_ref, h2t_ref, eb_ref, ebt_ref, bias_ref, act_ref, dpre_ref, grad_ref, hidden_ref
):
    rows_here, depth = h2_ref.shape
    tiles = act_ref.shape[1] // TILE
    per = depth // LANES
    step = PACK
    units = [(j, r) for j in range(tiles) for r in range(rows_here // step)]

    def start(unit):
        j, r = unit
        rows = slice(r * step, (r + 1) * step)
        pre = mm(h2_ref[rows, :], tile_of(w_ref, j, first))
        return (pre, mm(eb_ref[rows, :], tile_of(w_ref, j, first + depth)))

    now = start(units[0])
    for k, (j, r) in enumerate(units):
        later = start(units[k + 1]) if k + 1 < len(units) else None
        cols = slice(j * TILE, (j + 1) * TILE)
        bias = bias_ref[:, cols]
        pre, da = now
        for i in range(0, step, PIECE):
            rows = slice(r * step + i, r * step + i + PIECE)
            piece = pre[i : i + PIECE] + bias
            phi, slope = below_and_slope(piece)
            act_ref[rows, cols] = (piece * phi).astype(BF)
            dpre_ref[rows, cols] = (da[i : i + PIECE] * slope).astype(BF)
        now = later
        if (r + 1) * step == rows_here:
            gup = mm(h2t_ref[...], dpre_ref[:, cols])
            gdown = mm(ebt_ref[...], act_ref[:, cols])
            for n, b in enumerate((2 * j, 2 * j + 1)):
                t, o = b // per, (b % per) * LANES
                part = slice(n * LANES, (n + 1) * LANES)
                grad_ref[t, :, o : o + LANES] = gup[:depth, part].astype(BF)
                grad_ref[t, :, depth + o : depth + o + LANES] = gdown[:, part].astype(BF)
                hidden_ref[t : t + 1, o : o + LANES] = gup[depth : depth + 1, part]


def masked_cot(cot_ref, ids_ref, pack, rows):
    valid = jnp.where(crop_line(ids_ref, pack) < CROPS, 1.0, 0.0)
    valid = jnp.broadcast_to(valid, (LANES, PACK)).T[:, 0:1]
    return cot_ref[rows, :].astype(F32) * valid


def attention_back(qkv_ref, a_ref, lse_ref, da_ref, dqkv_ref, places, sides):
    place = lax.broadcasted_iota(jnp.int32, (LANES, PACK), 0)
    head_of = place // HEAD_DIM
    lane = lax.broadcasted_iota(jnp.int32, (PACK, LANES), 1) // HEAD_DIM
    none = jnp.zeros((PACK, LANES), BF)

    def split(line):
        high = line.astype(BF).astype(F32)
        rest = line - high
        middle = rest.astype(BF).astype(F32)
        low = rest - middle
        block = jnp.where(
            place == ONES,
            high,
            jnp.where(place == ONES + 1, middle, jnp.where(place == ONES + 2, low, 0.0)),
        )
        return block.astype(BF)

    held, made = {}, {}
    heads = [(k, h) for k in range(len(places)) for h in range(HEADS_HERE)]

    def load(k):
        slot, base, da_at, _ = places[k]
        rows, at = pl.ds(base, PACK), slot * 3 * LANES
        query = qkv_ref[rows, at : at + LANES]
        keys = qkv_ref[rows, at + LANES : at + 2 * LANES]
        values = qkv_ref[rows, at + 2 * LANES : at + 3 * LANES]
        grad = da_ref[rows, da_at * LANES : (da_at + 1) * LANES]
        grad_t = grad.T
        mixed = a_ref[rows, slot * LANES : (slot + 1) * LANES].T
        both = mixed.astype(F32) * grad_t.astype(F32)
        held[k] = (query, keys, values, grad, query.T, keys.T, grad_t, both)

    def scores_of(k, h):
        if k not in held:
            load(k)
        slot, base, _, _ = places[k]
        query, keys, values, grad, query_t, keys_t, grad_t, both = held[k]
        part = slice(h * HEAD_DIM, (h + 1) * HEAD_DIM)
        line = slot * HEADS_HERE + h
        lse = lse_ref[line : line + 1, pl.ds(base, PACK)]
        side = jnp.where(place < ONES, sides[k], split(-lse))
        scores = mm(keys, jnp.where(head_of == h, query_t, side))
        inner = jnp.sum(both[part], axis=0, keepdims=True)
        pull = mm(values, jnp.where(head_of == h, grad_t, split(-inner)))
        return (scores, pull)

    def finish(k, h, low, dscores):
        query, keys, values, grad, query_t, keys_t, grad_t, both = held[k]
        part = slice(h * HEAD_DIM, (h + 1) * HEAD_DIM)
        dv = mm(low, jnp.where(lane == h, grad, none))
        dk = mm(dscores, jnp.where(lane == h, query, none))
        dq = mm(keys_t[part], dscores)
        if h:
            last = made[k]
            made[k] = (last[0] + [dq], last[1] + dk, last[2] + dv)
        else:
            made[k] = ([dq], dk, dv)
        if h == HEADS_HERE - 1:
            dqs, dk, dv = made[k]
            dqs = jnp.concatenate(dqs + [jnp.zeros((LANES - USED, PACK), F32)], axis=0)
            _, base, _, slot = places[k]
            rows, at = pl.ds(base, PACK), slot * 3 * LANES
            dqkv_ref[rows, at : at + LANES] = (dqs.T * SCALE).astype(BF)
            dqkv_ref[rows, at + LANES : at + 2 * LANES] = (dk * LOG_TWO).astype(BF)
            dqkv_ref[rows, at + 2 * LANES : at + 3 * LANES] = dv.astype(BF)

    now = scores_of(*heads[0])
    waiting = None
    for n, head in enumerate(heads):
        later = scores_of(*heads[n + 1]) if n + 1 < len(heads) else None
        if waiting is not None:
            finish(*waiting)
        scores, pull = now
        probs = jnp.exp2(scores)
        waiting = head + (probs.astype(BF), (probs * pull).astype(BF))
        now = later
    finish(*waiting)


def back_kernel(
    place_ref,
    x_ref,
    ids_ref,
    w_ref,
    qkv_ref,
    a_ref,
    lse_ref,
    h1_ref,
    dx1_ref,
    line_ref,
    hidden_ref,
    out_ref,
    grad_ref,
    da_ref,
    dqkv_ref,
    h1t_ref,
    dybt_ref,
    sums_ref,
):
    rows_here, depth = x_ref.shape
    groups = w_ref.shape[0]
    small = small_rows(w_ref)
    sums_ref[...] = jnp.zeros_like(sums_ref)
    sums_ref[SMALL_AT : SMALL_AT + 8, :] = line_ref[...]

    @pl.loop(0, rows_here // PACK)
    def _(pack):
        base = pl.multiple_of(pack * PACK, PACK)
        rows = pl.ds(base, PACK)
        _, query_side = id_lanes(ids_ref[pack])
        low = dx1_ref[rows, :].astype(BF)
        dybt_ref[:, rows] = low.T
        h1t_ref[:, rows] = h1_ref[rows, :].T
        for g in range(groups):
            da_ref[rows, g * LANES : (g + 1) * LANES] = mm(
                low, w_ref[g, :, 3 * LANES : 4 * LANES]
            ).astype(BF)
        places = [(g, base, g, g) for g in range(groups)]
        attention_back(qkv_ref, a_ref, lse_ref, da_ref, dqkv_ref, places, [query_side] * groups)
        width = 3 * LANES
        grad = mm_nt(dqkv_ref[rows, 0:width], w_ref[0, :, 0:width])
        for g in range(1, groups):
            grad += mm_nt(dqkv_ref[rows, g * width : (g + 1) * width], w_ref[g, :, 0:width])
        unit, scale = norm_parts(x_ref[rows, :].astype(F32))
        back = norm_back(grad, unit, scale, small[0:1])
        out_ref[rows, :] = (dx1_ref[rows, :] + back).astype(BF)
        sums_ref[SMALL_AT : SMALL_AT + 1, :] += jnp.sum(grad * unit, axis=0, keepdims=True)
        sums_ref[SMALL_AT + 1 : SMALL_AT + 2, :] += jnp.sum(grad, axis=0, keepdims=True)

    lane = lax.broadcasted_iota(jnp.int32, (depth, LANES), 1)
    for g in range(groups):
        width = 3 * LANES
        sums_ref[HIDDEN_AT : HIDDEN_AT + 1, :] = hidden_ref[g : g + 1, :]
        extra = sums_ref[...].T
        entry = mm(h1t_ref[...], dqkv_ref[:, g * width : (g + 1) * width])
        grad_ref[g, :, 0:LANES] = jnp.where(lane < USED, entry[:, :LANES], extra).astype(BF)
        grad_ref[g, :, LANES:width] = entry[:, LANES:].astype(BF)
        grad_ref[g, :, width : width + LANES] = mm(
            dybt_ref[...], a_ref[:, g * LANES : (g + 1) * LANES]
        ).astype(BF)


def params():
    return pltpu.CompilerParams(vmem_limit_bytes=60 * 2**20)


def whole(shape):
    return pl.BlockSpec(shape, lambda i, place: (0,) * len(shape))


def own_rows(rows, depth):
    return pl.BlockSpec((rows, depth), lambda i, place: (place[0], 0))


def own_ids(packs):
    return pl.BlockSpec((packs, 1, PACK), lambda i, place: (place[0], 0, 0))


def run_key(place, tokens, ids, weights, rows):
    depth = tokens.shape[1]
    groups, _, width = weights.shape
    return pl.pallas_call(
        key_kernel,
        grid_spec=pltpu.PrefetchScalarGridSpec(
            num_scalar_prefetch=1,
            grid=(1,),
            in_specs=[own_rows(rows, depth), own_ids(rows // PACK), whole(weights.shape)],
            out_specs=whole((rows, depth)),
            scratch_shapes=[
                VMEM((rows, groups * 3 * LANES), BF),
                VMEM((rows, groups * LANES), BF),
                VMEM((rows, depth), F32),
                VMEM((rows, depth), BF),
                VMEM((PACK, groups * depth), BF),
                VMEM((1, groups * depth), F32),
            ],
        ),
        out_shape=jax.ShapeDtypeStruct((rows, depth), BF),
        compiler_params=params(),
        name="key_block",
    )(place, tokens, ids, weights)


def run_query(place, tokens, cotangent, ids, weights, rows):
    depth = tokens.shape[1]
    groups = weights.shape[0]
    outs = [
        ((rows, depth), BF),
        ((rows, groups * 3 * LANES), BF),
        ((rows, groups * LANES), BF),
        ((16, rows), F32),
        ((rows, depth), BF),
        ((rows, depth), F32),
        ((groups, depth, 2 * depth), BF),
        ((8, depth), F32),
        ((groups, depth), F32),
    ]
    return pl.pallas_call(
        query_kernel,
        grid_spec=pltpu.PrefetchScalarGridSpec(
            num_scalar_prefetch=1,
            grid=(1,),
            in_specs=[
                own_rows(rows, depth),
                own_rows(rows, depth),
                own_ids(rows // PACK),
                whole(weights.shape),
            ],
            out_specs=[whole(shape) for shape, _ in outs],
            scratch_shapes=[
                VMEM((rows, depth), F32),
                VMEM((rows, depth), BF),
                VMEM((depth + 16, rows), BF),
                VMEM((rows, depth), BF),
                VMEM((depth, rows), BF),
                VMEM((rows, groups * depth), BF),
                VMEM((rows, groups * depth), BF),
                VMEM((1, groups * depth), F32),
            ],
        ),
        out_shape=[jax.ShapeDtypeStruct(shape, kind) for shape, kind in outs],
        compiler_params=params(),
        name="query_block",
    )(place, tokens, cotangent, ids, weights)


def run_back(place, tokens, ids, weights, kept, rows):
    depth = tokens.shape[1]
    groups = weights.shape[0]
    return pl.pallas_call(
        back_kernel,
        grid_spec=pltpu.PrefetchScalarGridSpec(
            num_scalar_prefetch=1,
            grid=(1,),
            in_specs=[own_rows(rows, depth), own_ids(rows // PACK), whole((groups, depth, ATT))]
            + [whole(item.shape) for item in kept],
            out_specs=[whole((rows, depth)), whole((groups, depth, ATT))],
            scratch_shapes=[
                VMEM((rows, groups * LANES), BF),
                VMEM((rows, groups * 3 * LANES), BF),
                VMEM((depth, rows), BF),
                VMEM((depth, rows), BF),
                VMEM((LANES, depth), F32),
            ],
        ),
        out_shape=[
            jax.ShapeDtypeStruct((rows, depth), BF),
            jax.ShapeDtypeStruct((groups, depth, ATT), BF),
        ],
        compiler_params=params(),
        name="back_block",
    )(place, tokens, ids, weights, *kept)


def pack_piece(entry, leave, up, down, small, hidden):
    def fill(block, *extra):
        block = jnp.concatenate([block] + [item.astype(block.dtype) for item in extra], axis=1)
        return jnp.pad(block, ((0, 0), (0, LANES - block.shape[1])))

    parts = [
        fill(entry[:, 0], small.T, hidden[:, None]),
        fill(entry[:, 1]),
        fill(entry[:, 2]),
        fill(leave.T),
        up,
        down.T,
    ]
    return jnp.concatenate([part.astype(BF) for part in parts], axis=1)


def unpack_piece(piece, depth):
    entry = jnp.stack([piece[:, k * LANES : k * LANES + USED] for k in range(3)], axis=1)
    leave = piece[:, 3 * LANES : 3 * LANES + USED].T
    up = piece[:, ATT : ATT + depth]
    down = piece[:, ATT + depth :].T
    small = piece[:, SMALL_AT : SMALL_AT + 6].T
    return (entry, leave, up, down, small, piece[:, HIDDEN_AT])


def adamw(grad, first, second, master, decay, rate):
    moment = BETA_ONE * first + (1.0 - BETA_ONE) * grad
    square = BETA_TWO * second + (1.0 - BETA_TWO) * grad * grad
    ahead = moment / (1.0 - BETA_ONE**STEP)
    spread = square / (1.0 - BETA_TWO**STEP)
    return (
        moment,
        square,
        master - rate * (ahead / (jnp.sqrt(spread) + ADAM_EPS) + decay * master),
    )


DECAYS = (DECAY, DECAY, DECAY, DECAY, 0.0, 0.0)
RATES = (RATE_MATRIX, RATE_EXIT, RATE_MATRIX, RATE_MATRIX, RATE_SMALL, RATE_BIAS)


def finish_plain(grad_att, grad_ffn, masters, firsts, seconds):
    depth = grad_att.shape[1]
    grads = jnp.concatenate([grad_att, grad_ffn], axis=2).astype(F32)
    own = lax.psum_scatter(grads, "tensor", scatter_dimension=0, tiled=False)
    own = lax.psum_scatter(own, "dp", scatter_dimension=0, tiled=True)
    shares = unpack_piece(own, depth)
    copies = float(lax.axis_size("tensor"))
    total = jnp.sum(shares[4] * shares[4]) / copies
    for k in (0, 1, 2, 3, 5):
        total = total + jnp.sum(shares[k] * shares[k])
    norm_value = jnp.sqrt(lax.psum(total, ("dp", "tensor")))
    factor = CLIP / jnp.maximum(norm_value, CLIP)
    outs = []
    for k in range(6):
        outs.extend(
            adamw(shares[k] * factor, firsts[k], seconds[k], masters[k], DECAYS[k], RATES[k])
        )
    return (norm_value, outs)


def spot():
    dp, t = lax.axis_index("dp"), lax.axis_index("tensor")
    return (dp, t)


def flip(value, bits):
    for bit in (1, 2, 4):
        if bits & bit:
            value = value + bit - 2 * bit * ((value // bit) % 2)
    return value


def hello(peers):
    barrier = pltpu.get_barrier_semaphore()
    for peer in peers:
        pl.semaphore_signal(barrier, inc=1, device_id=peer, device_id_type=MESH)


def wait_for(peers):
    pl.semaphore_wait(pltpu.get_barrier_semaphore(), len(peers))


KEY_PARTS = 3
SENDS = 62 + 9 + 18 + 51 + 10


class Mail:
    def __init__(self, send_sem, recv_sem):
        self.send_sem, self.recv_sem = send_sem, recv_sem
        self.count, self.sent = 0, []

    def send(self, src, dst, peer):
        copy = pltpu.make_async_remote_copy(
            src_ref=src,
            dst_ref=dst,
            send_sem=self.send_sem.at[self.count],
            recv_sem=self.recv_sem.at[self.count],
            device_id=peer,
            device_id_type=MESH,
        )
        copy.start()
        self.count += 1
        self.sent.append(copy)
        return copy

    def close(self):
        for copy in self.sent:
            copy.wait_send()


def arrived(copies):
    for copy in copies:
        copy.wait_recv()


def load_rows(src, dst, t, sem):
    count = dst.shape[0]
    copy = pltpu.make_async_copy(src.at[pl.ds(t * count, count)], dst, sem)
    copy.start()
    return copy


def fold(block):
    out = block[0:8]
    for k in range(8, block.shape[0], 8):
        out = out + block[k : k + 8]
    return out


class Reduce:
    def __init__(self, mail, grad_ref, refs, where):
        self.mail, self.grad = mail, grad_ref
        self.rc, self.s0, self.r1, self.s1, self.r2, self.s2, self.r3 = refs
        self.where = where
        self.core = [None, None]
        self.side = [None, None]
        self.line = [None, None]
        self.across = None

    def slab(self, group, k):
        rows = self.s1.shape[2]
        return self.grad.at[group, pl.ds(pl.multiple_of(k * rows, 16), rows)]

    def to_core(self, q):
        dp, t, core, across, side, line = self.where
        self.core[q] = self.mail.send(self.grad.at[flip(t, 1 + 2 * q)], self.rc.at[q], core)

    def to_side(self, q):
        dp, t, core, across, side, line = self.where
        self.core[q].wait_recv()
        own = flip(t, 2 * q)
        y = dp % 2
        rows = self.s1.shape[2]

        @pl.loop(0, 8)
        def _(k):
            part = pl.ds(pl.multiple_of(k * rows, 16), rows)
            left = self.grad[own, part, :].astype(F32)
            self.s0[q, k] = (left + self.rc[q, part, :].astype(F32)).astype(BF)

        self.side[q] = [
            self.mail.send(self.s0.at[q, 2 * w + 1 - y], self.r1.at[q, w], side) for w in range(4)
        ]

    def to_line(self, q):
        dp, t, core, across, side, line = self.where
        arrived(self.side[q])
        y = dp % 2

        @pl.loop(0, 4)
        def _(w):
            left = self.s0[q, 2 * w + y].astype(F32)
            self.s1[q, w] = (left + self.r1[q, w].astype(F32)).astype(BF)

        self.line[q] = [
            self.mail.send(self.s1.at[q, line[j][0] // 2], self.r2.at[q, j - 1], line[j])
            for j in range(1, 4)
        ]

    def to_across(self, q):
        dp, t, core, across, side, line = self.where
        arrived(self.line[q])
        total = self.s1[q, dp // 2].astype(F32)
        for j in range(3):
            total = total + self.r2[q, j].astype(F32)
        self.s2[q] = total.astype(BF)
        if q:
            self.across = self.mail.send(self.s2.at[1], self.r3, across)

    def result(self):
        self.across.wait_recv()
        return self.s2[0].astype(F32) + self.r3[...].astype(F32)


class Spread:
    def __init__(self, mail, where, own_ref, out_ref, first, sem):
        dp, t, core, across, side, line = where
        self.mail, self.where, self.out = mail, where, out_ref
        self.count = own_ref.shape[0]
        self.first = first
        here = self.part(t)
        self.across = mail.send(own_ref, here, across)
        self.core = [mail.send(own_ref, here, core)]
        self.local = pltpu.make_async_copy(own_ref, here, sem)
        self.local.start()

    def part(self, t):
        at = t * self.first[1] + self.first[0]
        return self.out.at[pl.ds(pl.multiple_of(at, 16), self.count)]

    def forward(self):
        dp, t, core, across, side, line = self.where
        self.across.wait_recv()
        far = self.part(flip(t, 2))
        self.core.append(self.mail.send(far, far, core))

    def finish(self):
        arrived(self.core)
        self.local.wait()


class Gather:
    def __init__(self, mail, where, own_ref, all_ref, sem):
        self.mail, self.where, self.own, self.all = mail, where, own_ref, all_ref
        dp, t, core, across, side, line = where
        self.local = pltpu.make_async_copy(own_ref, self.piece(t, dp), sem)
        self.local.start()

    def piece(self, group, dp):
        rows = self.own.shape[0]
        return self.all.at[group, pl.ds(pl.multiple_of(dp * rows, 16), rows)]

    def start_across(self):
        dp, t, core, across, side, line = self.where
        self.across = self.mail.send(self.own, self.piece(t, dp), across)

    def start(self):
        dp, t, core, across, side, line = self.where
        send, here = self.mail.send, self.piece(t, dp)
        self.line = [[send(self.own, here, line[j])] for j in range(1, 4)]
        self.side = [[send(self.own, here, side)], [], [], []]
        self.core = [[send(self.own, here, core)], []]

    def pass_across(self):
        dp, t, core, across, side, line = self.where
        send, far = self.mail.send, self.piece(flip(t, 2), dp)
        self.across.wait_recv()
        for j in range(1, 4):
            self.line[j - 1].append(send(far, far, line[j]))
        self.side[0].append(send(far, far, side))
        self.core[1].append(send(far, far, core))

    def pass_line(self, k):
        dp, t, core, across, side, line = self.where
        for j in range(1, 4):
            self.line[j - 1][k].wait_recv()
            piece = self.piece(flip(t, 2 * k), line[j][0])
            self.side[j].append(self.mail.send(piece, piece, side))
            self.core[k].append(self.mail.send(piece, piece, core))

    def pass_side(self, k):
        dp, t, core, across, side, line = self.where
        for j in range(4):
            self.side[j][k].wait_recv()
            piece = self.piece(flip(t, 2 * k), flip(line[j][0], 1))
            self.core[k].append(self.mail.send(piece, piece, core))

    def finish(self, k):
        arrived(self.core[k])


def block_kernel(*refs):
    entry_ref, leave_ref, up_ref, down_ref, small_ref, hidden_ref = refs[0:6]
    key_entry, key_leave, key_up, key_down, key_small, key_hidden = refs[6:12]
    tokens_ref, cot_all_ref, key_tokens_ref, crops_ref = refs[12:16]
    block_out, key_out, input_grad, norm_ref, own_a, own_f, own_s = refs[16:23]
    (
        kx_ref, qx_ref, cot_ref, ids_ref, pa_ref, pf_ref, keys_ref, wa_ref, wf_ref,
        kqkv_ref, qqkv_ref, ka_ref, qa_ref, lse_ref, kh_ref, h1_ref, kx1_ref, x1_ref,
        act_ref, dpre_ref, h2_ref, h2t_ref, eb_ref, ebt_ref, bias_ref, hid_ref, line_ref,
        unit_ref, scale_ref, h1t_ref, dyb_ref, dybt_ref, dqkv_ref, ga_ref, ge_ref, gf_ref,
        key_rows, block_rows, grad_rows, near_ref, far_ref, turn_ref,
    ) = refs[23:65]
    red_a, red_e, red_f = refs[65:72], refs[72:79], refs[79:86]
    send_sem, recv_sem, local_sem = refs[86:]
    dp, t = spot()
    far = flip(t, 2)
    core, across = (dp, flip(t, 1)), (dp, far)
    side = (flip(dp, 1), t)
    line = [(flip(dp, 2 * j), t) for j in range(4)]
    where = (dp, t, core, across, side, line)
    mail = Mail(send_sem, recv_sem)
    send = mail.send
    loads = [
        load_rows(src, dst, t, local_sem.at[k])
        for k, (src, dst) in enumerate(
            ((key_tokens_ref, kx_ref), (crops_ref, ids_ref), (tokens_ref, qx_ref), (cot_all_ref, cot_ref))
        )
    ]

    peers = [(dp, flip(t, k)) for k in (1, 2, 3)] + [(flip(dp, k), t) for k in range(1, 8)]
    hello(peers)
    rows, depth = up_ref.shape
    wide = LANES - USED
    extra = [small_ref[...], hidden_ref[...], jnp.zeros((wide - 7, rows), F32)]
    extra = jnp.concatenate(extra, axis=0).T
    blank = jnp.zeros((rows, wide), F32)
    for k, block in enumerate([entry_ref[0], entry_ref[1], entry_ref[2], leave_ref[...]]):
        block = jnp.concatenate([block, blank if k else extra], axis=1)
        pa_ref[:, k * LANES : (k + 1) * LANES] = block.astype(BF)
    wait_for(peers)
    gather_a = Gather(mail, where, pa_ref, wa_ref, local_sem.at[4])
    gather_a.start_across()
    gather_a.start()

    parts = [pl.ds(0, ATT), pl.ds(ATT, depth), pl.ds(ATT + depth, depth)]

    def key_part(group, k):
        return keys_ref.at[group, :, parts[k]]

    def key_send(k, peer):
        return send(key_part(t, k), key_part(t, k), peer)

    blank = jnp.zeros((wide, depth), BF)
    extra = [key_small[...], key_hidden[...].reshape(1, depth), jnp.zeros((wide - 7, depth), BF)]
    for k, block in enumerate([key_entry[0], key_entry[1], key_entry[2], key_leave[...]]):
        block = jnp.concatenate([block] + ([blank] if k else extra), axis=0)
        keys_ref[t, :, k * LANES : (k + 1) * LANES] = block.T
    key_across = [key_send(0, across)]
    key_core = [key_send(0, core)]
    pf_ref[:, 0:depth] = up_ref[...].astype(BF)
    pf_ref[:, depth:] = down_ref[...].astype(BF)
    gather_f = Gather(mail, where, pf_ref, wf_ref, local_sem.at[5])
    gather_f.start_across()
    keys_ref[t, :, ATT : ATT + depth] = key_up[...]
    keys_ref[t, :, ATT + depth :] = key_down[...].T
    key_across += [key_send(k, across) for k in (1, 2)]
    key_core += [key_send(k, core) for k in (1, 2)]

    packs = kx_ref.shape[0] // PACK
    bases = [pack * PACK for pack in range(packs)]
    spots = [slice(base, base + PACK) for base in bases]
    loads[0].wait()
    loads[1].wait()
    key_norms = small_rows_of(keys_ref[t, :, 0:LANES])
    masks = [enter(kx_ref, ids_ref, key_norms, kh_ref, base, k) for k, base in enumerate(bases)]
    sides = [query_side for _, query_side in masks]

    def heads_of(slot, weight, first_ref, qkv_ref, a_ref, lse):
        for base, (key_side, _) in zip(bases, masks):
            project(first_ref[base : base + PACK, :], weight, qkv_ref, key_side, base, slot)
        attention(qkv_ref, a_ref, lse, [(slot, base) for base in bases], sides)

    def key_heads(slot):
        heads_of(slot, keys_ref[flip(t, slot), :, 0 : 3 * LANES], kh_ref, kqkv_ref, ka_ref, None)

    def query_heads(slot):
        heads_of(slot, wa_ref[flip(t, slot), :, 0 : 3 * LANES], h1_ref, qqkv_ref, qa_ref, lse_ref)

    def pass_key(k):
        key_across[k].wait_recv()
        return send(key_part(far, k), key_part(far, k), core)

    key_heads(0)
    gather_a.pass_across()
    gather_f.start()
    arrived(key_core[:1])
    key_heads(1)
    gather_a.pass_line(0)
    loads[2].wait()
    loads[3].wait()
    for k, spot_rows in enumerate(spots):
        low = masked_cot(cot_ref, ids_ref, k, spot_rows).astype(BF)
        eb_ref[spot_rows, :] = low
        ebt_ref[:, spot_rows] = low.T
        unit, scale = norm_parts(qx_ref[spot_rows, :].astype(F32))
        unit_ref[spot_rows, :] = unit
        scale_ref[spot_rows, :] = jnp.broadcast_to(scale, (PACK, LANES))
    gather_a.pass_side(0)
    gather_a.local.wait()
    norms = small_rows_of(wa_ref[t, :, 0:LANES])
    for spot_rows in spots:
        first = (unit_ref[spot_rows, :] * norms[0:1] + norms[1:2]).astype(BF)
        h1_ref[spot_rows, :] = first
        h1t_ref[:, spot_rows] = first.T
    query_heads(0)
    gather_a.pass_line(1)
    key_far = [pass_key(0)]
    gather_f.pass_across()
    key_heads(2)
    arrived(key_far)
    key_heads(3)
    gather_f.pass_line(0)
    gather_a.pass_side(1)

    def leaving_of(w_ref):
        weights = [w_ref[flip(t, k), :, 3 * LANES : 4 * LANES] for k in range(4)]
        return jnp.concatenate(weights, axis=1)

    weight = leaving_of(keys_ref)
    for base in bases:
        second = leave(kx_ref, weight, key_norms, ka_ref, kx1_ref, base)
        kh_ref[base : base + PACK, :] = second
    for k in range(4):
        bias_ref[:, k * depth : (k + 1) * depth] = hidden_line(keys_ref[k, :, 0:LANES])
    gather_a.finish(0)
    query_heads(1)
    key_far.append(pass_key(1))
    gather_f.pass_line(1)
    arrived(key_core[1:2] + key_far[1:2])
    feed(kh_ref[spots[0], :], keys_ref, bias_ref, act_ref.at[spots[0]])
    gather_f.pass_side(0)
    feed(kh_ref[spots[1], :], keys_ref, bias_ref, act_ref.at[spots[1]])
    key_far.append(pass_key(2))
    gather_a.finish(1)
    query_heads(2)
    arrived(key_core[2:] + key_far[2:])
    weight = gathered(keys_ref, ATT + depth, depth)
    count = key_rows.shape[0]
    spread_key = []
    for k, spot_rows in enumerate(spots):
        product = mm_nt(act_ref[spot_rows, :], weight)
        key_rows[spot_rows, :] = (kx1_ref[spot_rows, :] + product + key_norms[5:6]).astype(BF)
        part = key_rows.at[spot_rows]
        first = (k * PACK, count)
        spread_key.append(Spread(mail, where, part, key_out, first, local_sem.at[(6, 10)[k]]))
    gather_f.pass_side(1)
    query_heads(3)
    weight = leaving_of(wa_ref)
    for base in bases:
        second = leave(qx_ref, weight, norms, qa_ref, x1_ref, base)
        h2_ref[base : base + PACK, :] = second
        h2t_ref[0:depth, base : base + PACK] = second.T
    h2t_ref[depth:, :] = jnp.ones((h2t_ref.shape[0] - depth, h2t_ref.shape[1]), BF)
    gather_f.finish(0)
    gather_f.finish(1)
    gather_f.local.wait()
    for k in range(4):
        bias_ref[:, k * depth : (k + 1) * depth] = hidden_line(wa_ref[k, :, 0:LANES])
    feed_back(
        wf_ref, 0, h2_ref, h2t_ref, eb_ref, ebt_ref, bias_ref, act_ref, dpre_ref, gf_ref, hid_ref
    )
    reduce_f = Reduce(mail, gf_ref, red_f, where)
    reduce_f.to_core(0)
    reduce_f.to_core(1)
    weight = gathered(wf_ref, depth, depth)
    spread_block = []
    for k, spot_rows in enumerate(spots):
        product = mm_nt(act_ref[spot_rows, :], weight)
        block_rows[spot_rows, :] = (x1_ref[spot_rows, :] + product + norms[5:6]).astype(BF)
        part = block_rows.at[spot_rows]
        first = (k * PACK, count)
        spread_block.append(Spread(mail, where, part, block_out, first, local_sem.at[(7, 11)[k]]))
    line_ref[...] = jnp.zeros_like(line_ref)
    weight = gathered(wf_ref, 0, depth)
    for k, spot_rows in enumerate(spots):
        grad = mm_nt(dpre_ref[spot_rows, :], weight)
        unit, scale = norm_parts(x1_ref[spot_rows, :])
        wide_cot = masked_cot(cot_ref, ids_ref, k, spot_rows)
        dx1 = wide_cot + norm_back(grad, unit, scale, norms[2:3])
        x1_ref[spot_rows, :] = dx1
        low = dx1.astype(BF)
        dyb_ref[spot_rows, :] = low
        dybt_ref[:, spot_rows] = low.T
        line_ref[2:3, :] += jnp.sum(grad * unit, axis=0, keepdims=True)
        line_ref[3:4, :] += jnp.sum(grad, axis=0, keepdims=True)
        line_ref[4:5, :] += jnp.sum(dx1, axis=0, keepdims=True)
        line_ref[5:6, :] += jnp.sum(wide_cot, axis=0, keepdims=True)
    mixed = mm(dybt_ref[...], qa_ref[...]).astype(BF)
    for slot in range(4):
        ge_ref[flip(t, slot)] = mixed[:, slot * LANES : (slot + 1) * LANES]
    reduce_f.to_side(0)
    reduce_f.to_side(1)

    reduce_a = Reduce(mail, ga_ref, red_a, where)
    reduce_e = Reduce(mail, ge_ref, red_e, where)
    reduce_e.to_core(0)
    reduce_e.to_core(1)
    lane = lax.broadcasted_iota(jnp.int32, (depth, LANES), 1)
    width = 3 * LANES

    weight = leaving_of(wa_ref)
    for base in bases:
        ka_ref[base : base + PACK, :] = mm(dyb_ref[base : base + PACK, :], weight).astype(BF)

    def back_heads(slots, pack):
        places = [(slot, bases[pack], slot, slot) for slot in slots]
        side = [sides[pack]] * len(slots)
        attention_back(qqkv_ref, qa_ref, lse_ref, ka_ref, dqkv_ref, places, side)

    def back_weights(slot):
        group = flip(t, slot)
        entry = mm(h1t_ref[...], dqkv_ref[:, slot * width : (slot + 1) * width])
        hidden = jnp.broadcast_to(hid_ref[pl.ds(group, 1), :], (LANES, depth)).T
        ga_ref[group, :, 0:LANES] = jnp.where(lane == HIDDEN_AT, hidden, entry[:, :LANES]).astype(BF)
        ga_ref[group, :, LANES:width] = entry[:, LANES:].astype(BF)

    def back_rows(pack):
        spot_rows = spots[pack]
        weight = jnp.concatenate([wa_ref[flip(t, k), :, 0:width] for k in range(4)], axis=1)
        grad = mm_nt(dqkv_ref[spot_rows, :], weight)
        unit, scale = unit_ref[spot_rows, :], scale_ref[spot_rows, 0:1]
        back = norm_back(grad, unit, scale, norms[0:1])
        grad_rows[spot_rows, :] = (x1_ref[spot_rows, :] + back).astype(BF)
        first = (pack * PACK, count)
        sem = local_sem.at[8 + pack]
        item = Spread(mail, where, grad_rows.at[spot_rows], input_grad, first, sem)
        line_ref[0:1, :] += jnp.sum(grad * unit, axis=0, keepdims=True)
        line_ref[1:2, :] += jnp.sum(grad, axis=0, keepdims=True)
        return item

    back_heads((3, 2), 0)
    reduce_e.to_side(0)
    reduce_e.to_side(1)
    for item in spread_key:
        item.forward()
    back_heads((1, 0), 0)
    reduce_f.to_line(0)
    spread_grad = [back_rows(0)]
    back_heads((3,), 1)
    back_weights(3)
    reduce_a.to_core(1)
    reduce_f.to_line(1)
    back_heads((2,), 1)
    back_weights(2)
    reduce_a.to_side(1)
    reduce_e.to_line(0)
    reduce_e.to_line(1)
    for item in spread_block:
        item.forward()
    back_heads((1,), 1)
    back_weights(1)
    reduce_a.to_core(0)
    reduce_a.to_line(1)
    reduce_f.to_across(0)
    reduce_f.to_across(1)
    reduce_e.to_across(0)
    reduce_e.to_across(1)
    back_heads((0,), 1)
    back_weights(0)
    reduce_a.to_side(0)
    reduce_a.to_across(1)
    spread_grad.append(back_rows(1))
    reduce_a.to_line(0)
    grad_e = reduce_e.result()
    grad_f = reduce_f.result()
    spread_grad[0].forward()
    reduce_a.to_across(0)
    grad_a = jnp.concatenate([reduce_a.result(), grad_e], axis=1)

    total = jnp.zeros((8, LANES), F32)
    lane = lax.broadcasted_iota(jnp.int32, (rows, LANES), 1)
    for k in range(4):
        block = grad_a[:, k * LANES : (k + 1) * LANES]
        share = jnp.where(lane < USED, 1.0, jnp.where(lane == HIDDEN_AT, 0.0 if k else 1.0, 0.0))
        total = total + fold(block * block * share)
    for k in range(2 * depth // LANES):
        block = grad_f[:, k * LANES : (k + 1) * LANES]
        total = total + fold(block * block)
    near_ref[t, 0:8, :] = line_ref[...]
    near_ref[t, 8:16, :] = jnp.concatenate([total] + [jnp.zeros_like(total)] * 2, axis=1)
    near = [send(near_ref.at[t], near_ref.at[t], (dp, flip(t, k))) for k in (1, 2, 3)]
    arrived(near)
    far_ref[dp] = (near_ref[0] + near_ref[1]) + (near_ref[2] + near_ref[3])
    wide_sends = [send(far_ref.at[dp], far_ref.at[dp], (flip(dp, k), t)) for k in range(1, 8)]
    own_a[...] = grad_a
    own_f[...] = grad_f
    spread_grad[1].forward()
    arrived(wide_sends)
    total = far_ref[0]
    for k in range(1, 8):
        total = total + far_ref[k]
    lines = total[0:8]
    squares = fold(total[8:16, 0:LANES])
    for k in range(depth // LANES):
        block = lines[:, k * LANES : (k + 1) * LANES]
        squares = squares + block * block
    squares = jnp.sum(jnp.sum(squares, axis=0, keepdims=True), axis=1, keepdims=True)
    norm_ref[...] = jnp.broadcast_to(jnp.sqrt(squares), norm_ref.shape)
    turn_ref[...] = jnp.concatenate([lines, jnp.zeros((LANES - 8, depth), F32)], axis=0).T
    own_s[...] = turn_ref[pl.ds(pl.multiple_of(dp * rows, 16), rows), :]
    for item in spread_key + spread_block + spread_grad:
        item.finish()
    mail.close()


def lay(entry, leave, up, down, small, hidden):
    return [entry.transpose(1, 0, 2), leave.T, up, down.T, small, hidden.reshape(1, -1)]


def run_block(masters, keys, tokens, cotangent, key_tokens, ids, dp, tensor):
    key_entry, key_leave, key_up, key_down, key_small, key_hidden = keys
    rows, depth = masters[2].shape
    all_rows = tokens.shape[0]
    count = all_rows // tensor
    args = lay(*masters)
    args += [key_entry.transpose(1, 2, 0), key_leave, key_up, key_down, key_small]
    args.append(key_hidden)

    def all_of(shape):
        return pl.BlockSpec(shape, lambda i: (0,) * len(shape))

    anywhere = pl.BlockSpec(memory_space=pl.ANY)
    hidden = tensor * depth
    scratch = [
        ((count, depth), BF),
        ((count, depth), BF),
        ((count, depth), BF),
        ((count,), jnp.int32),
        ((rows, ATT), BF),
        ((rows, 2 * depth), BF),
        ((tensor, depth, ATT + 2 * depth), BF),
        ((tensor, depth, ATT), BF),
        ((tensor, depth, 2 * depth), BF),
        ((count, tensor * 3 * LANES), BF),
        ((count, tensor * 3 * LANES), BF),
        ((count, tensor * LANES), BF),
        ((count, tensor * LANES), BF),
        ((16, count), F32),
        ((count, depth), BF),
        ((count, depth), BF),
        ((count, depth), F32),
        ((count, depth), F32),
        ((count, hidden), BF),
        ((count, hidden), BF),
        ((count, depth), BF),
        ((depth + 16, count), BF),
        ((count, depth), BF),
        ((depth, count), BF),
        ((1, hidden), F32),
        ((8, depth), F32),
        ((8, depth), F32),
        ((count, depth), F32),
        ((count, LANES), F32),
        ((depth, count), BF),
        ((count, depth), BF),
        ((depth, count), BF),
        ((count, tensor * 3 * LANES), BF),
        ((tensor, depth, 3 * LANES), BF),
        ((tensor, depth, LANES), BF),
        ((tensor, depth, 2 * depth), BF),
        ((count, depth), BF),
        ((count, depth), BF),
        ((count, depth), BF),
        ((tensor, 16, depth), F32),
        ((dp, 16, depth), F32),
        ((depth, LANES), F32),
    ]
    for wide in (3 * LANES, LANES, 2 * depth):
        scratch += [
            ((2, depth, wide), BF),
            ((2, 8, rows, wide), BF),
            ((2, 4, rows, wide), BF),
            ((2, 4, rows, wide), BF),
            ((2, 3, rows, wide), BF),
            ((2, rows, wide), BF),
            ((rows, wide), BF),
        ]
    outs = [
        ((all_rows, depth), BF),
        ((all_rows, depth), BF),
        ((all_rows, depth), BF),
        ((8, LANES), F32),
        ((rows, ATT), F32),
        ((rows, 2 * depth), F32),
        ((rows, LANES), F32),
    ]
    return pl.pallas_call(
        block_kernel,
        grid=(1,),
        in_specs=[all_of(item.shape) for item in args] + [anywhere] * 4,
        out_specs=[anywhere] * 3 + [all_of(shape) for shape, _ in outs[3:]],
        scratch_shapes=[VMEM(shape, kind) for shape, kind in scratch]
        + [
            pltpu.SemaphoreType.DMA((SENDS,)),
            pltpu.SemaphoreType.DMA((SENDS,)),
            pltpu.SemaphoreType.DMA((12,)),
        ],
        out_shape=[jax.ShapeDtypeStruct(shape, kind) for shape, kind in outs],
        compiler_params=pltpu.CompilerParams(
            collective_id=1, has_side_effects=True, vmem_limit_bytes=63 * 2**20
        ),
        name="block_forward_and_backward",
    )(*args, tokens, cotangent, key_tokens, ids)


def step_kernel(*refs):
    held, load_sem, store_sem, state_sem = refs[47:51]
    states = refs[51:]
    chunks, rows = held.shape[0] // 3, held.shape[1]
    loads, stores = [], []
    for k in range(3):
        for c in range(chunks):
            n, part = k * chunks + c, pl.ds(c * rows, rows)
            loads.append(pltpu.make_async_copy(refs[k].at[part], held.at[n], load_sem.at[n]))
            stores.append(pltpu.make_async_copy(held.at[n], refs[25 + k].at[part], store_sem.at[n]))
    inputs = [
        pltpu.make_async_copy(src, dst, state_sem.at[k])
        for k, (src, dst) in enumerate(zip(refs[3:25], states))
    ]
    for copy in inputs + loads:
        copy.start()
    for copy in inputs:
        copy.wait()
    step_states(*states, *refs[28:47])
    for load, store in zip(loads, stores):
        load.wait()
        store.start()
    for copy in stores:
        copy.wait()


def step_states(norm_ref, ga_ref, gb_ref, gs_ref, *refs):
    masters, firsts, seconds = refs[0:6], refs[6:12], refs[12:18]
    value_ref, outs = refs[18], refs[19:]
    norm_value = norm_ref[0:1, 0:1]
    value_ref[...] = norm_value
    factor = CLIP / jnp.maximum(norm_value, CLIP)
    grad_a = ga_ref[...] * factor
    grad_b = gb_ref[...] * factor
    depth = grad_b.shape[1] // 2

    def update(k, at, grad):
        new = adamw(grad, firsts[k][at], seconds[k][at], masters[k][at], DECAYS[k], RATES[k])
        for j in range(3):
            outs[3 * k + j][at] = new[j]

    for j in range(3):
        update(0, j, grad_a[:, j * LANES : j * LANES + USED])
    update(1, slice(None), grad_a[:, 3 * LANES : 3 * LANES + USED])
    update(2, slice(None), grad_b[:, :depth])
    update(3, slice(None), grad_b[:, depth:])
    update(4, slice(None), (gs_ref[...] * factor).T[0:6])
    update(5, slice(None), grad_a[:, :LANES].T[HIDDEN_AT : HIDDEN_AT + 1])


def run_step(large, norm_tile, grad_a, grad_b, grad_s, masters, firsts, seconds):
    state = lay(*masters) + lay(*firsts) + lay(*seconds)
    shapes = [jax.ShapeDtypeStruct((1, 1), F32)]
    for item in state[:6]:
        shapes.extend([jax.ShapeDtypeStruct(item.shape, F32)] * 3)
    args = [norm_tile, grad_a, grad_b, grad_s] + state

    def all_of(shape):
        return pl.BlockSpec(shape, lambda i: (0,) * len(shape))

    rows, depth = large[0].shape
    anywhere = pl.BlockSpec(memory_space=pl.ANY)
    result = pl.pallas_call(
        step_kernel,
        grid=(1,),
        in_specs=[anywhere] * (3 + len(args)),
        out_specs=[anywhere] * 3 + [all_of(item.shape) for item in shapes],
        out_shape=[jax.ShapeDtypeStruct(item.shape, item.dtype) for item in large] + shapes,
        scratch_shapes=[
            VMEM((12, rows // 4, depth), BF),
            pltpu.SemaphoreType.DMA((12,)),
            pltpu.SemaphoreType.DMA((12,)),
            pltpu.SemaphoreType.DMA((len(args),)),
        ]
        + [VMEM(item.shape, item.dtype) for item in args],
        compiler_params=pltpu.CompilerParams(vmem_limit_bytes=63 * 2**20),
        name="optimizer_step",
    )(*large, *args)
    large, result = result[:3], result[3:]
    outs = list(result[1:])
    for k in range(3):
        outs[k] = outs[k].transpose(1, 0, 2)
        outs[3 + k] = outs[3 + k].T
        outs[9 + k] = outs[9 + k].T
        outs[15 + k] = outs[15 + k].reshape(-1)
    return (large, result[0].reshape(()), outs)


def on_device(*args):
    tokens, crop_ids, cotangent, key_tokens = args[:4]
    masters, firsts, seconds, keys = args[4:10], args[10:16], args[16:22], args[22:28]
    count, groups = lax.axis_size("dp"), lax.axis_size("tensor")
    if count == 8 and groups == 4:
        result = run_block(masters, keys, tokens, cotangent, key_tokens, crop_ids, count, groups)
        large, norm_value, outs = run_step(result[:3], *result[3:], masters, firsts, seconds)
        return (*large, norm_value, *outs)
    ids = crop_ids.reshape(-1, 1, PACK)
    rows = tokens.shape[0] // groups
    place = lax.axis_index("tensor").astype(jnp.int32)[None]
    key_weights = lax.all_gather(pack_piece(*keys), "tensor", axis=0)
    weights = lax.all_gather(pack_piece(*masters), "dp", axis=0, tiled=True)
    weights = lax.all_gather(weights, "tensor", axis=0)

    def spread(own):
        return lax.all_gather(own, "tensor", axis=0, tiled=True)

    key_out = spread(run_key(place, key_tokens, ids, key_weights, rows))
    forward = run_query(place, tokens, cotangent, ids, weights, rows)
    block_out = spread(forward[0])
    qkv, a, lse, h1, dx1, grad_ffn, lines, hidden = forward[1:]
    grad_rows, grad_att = run_back(
        place, tokens, ids, weights, (qkv, a, lse, h1, dx1, lines, hidden), rows
    )
    input_grad = spread(grad_rows)
    norm_value, outs = finish_plain(grad_att, grad_ffn, masters, firsts, seconds)
    return (block_out, key_out, input_grad, norm_value, *outs)


def solution(mesh):
    rows, line = P("dp", None), P("dp")
    entry, leave, up, down = P("dp", None, "tensor"), P("tensor", "dp"), P("dp", "tensor"), P("tensor", "dp")
    state = (entry, leave, up, down, P(None, "dp"), P(("tensor", "dp")))
    keys = (P(None, None, "tensor"), P("tensor", None), P(None, "tensor"), P("tensor", None), P(), P("tensor"))
    outs = tuple(spec for spec in state for _ in range(3))
    return jax.shard_map(
        on_device,
        mesh=mesh,
        in_specs=(rows, line, rows, rows) + state * 3 + keys,
        out_specs=(rows, rows, rows, P()) + outs,
        check_vma=False,
    )
```

```python
import math
from functools import partial

import jax
import jax.numpy as jnp
from jax import lax
from jax.experimental import pallas as pl
from jax.experimental.pallas import tpu as pltpu
from jax.sharding import PartitionSpec as P

HEAD_DIM = 32
PACK = 512
CROPS = 5
STEP = 10
LN_EPS = 1e-06
CLIP = 1.0
RATE_MATRIX = 0.03
RATE_EXIT = 0.2
RATE_SMALL = 0.5
RATE_BIAS = 0.3
BETA_ONE = 0.9
BETA_TWO = 0.999
ADAM_EPS = 1e-08
DECAY = 0.05
MASKED = -1e30

SCALE = HEAD_DIM ** (-0.5)
EXP_SCALE = SCALE * math.log2(math.e)
LOG_TWO = math.log(2.0)
LANES = 128
TILE = 2 * LANES
PIECE = 64
HEADS_HERE = 3
USED = HEADS_HERE * HEAD_DIM
ONES = USED + CROPS + 1
ATT = 4 * LANES
SMALL_AT = USED
HIDDEN_AT = USED + 6
MESH = pl.DeviceIdType.MESH
BF = jnp.bfloat16
F32 = jnp.float32
VMEM = pltpu.VMEM
NT = (((1,), (1,)), ((), ()))
TN = (((0,), (0,)), ((), ()))

def mm(left, right):
    return jnp.dot(left, right, preferred_element_type=F32)


def mm_nt(left, right):
    return lax.dot_general(left, right, NT, preferred_element_type=F32)


def norm_parts(values):
    mean = jnp.mean(values, axis=1, keepdims=True)
    centred = values - mean
    spread = jnp.mean(centred * centred, axis=1, keepdims=True)
    scale = lax.rsqrt(spread + LN_EPS)
    return (centred * scale, scale)


def norm_back(grad, unit, scale, gain):
    scaled = grad * gain
    first = jnp.mean(scaled, axis=1, keepdims=True)
    second = jnp.mean(scaled * unit, axis=1, keepdims=True)
    return scale * (scaled - first - unit * second)


def below(pre):
    return 0.5 + 0.5 * lax.erf(pre * math.sqrt(0.5))


def below_and_slope(pre):
    phi = below(pre)
    bell = jnp.exp2((pre * (-0.5 * math.log2(math.e))) * pre)
    return (phi, phi + (pre * (1.0 / math.sqrt(2.0 * math.pi))) * bell)


def small_rows_of(weight):
    return weight.astype(F32).T[SMALL_AT : SMALL_AT + 6]


def hidden_line(weight):
    return weight.astype(F32).T[HIDDEN_AT : HIDDEN_AT + 1]


def small_rows(w_ref):
    return small_rows_of(w_ref[0, :, 0:LANES])


def hidden_row(w_ref, t):
    return hidden_line(w_ref[t, :, 0:LANES])


def crop_line(ids_ref, pack):
    if len(ids_ref.shape) == 1:
        return ids_ref[pl.ds(pack * PACK, PACK)].reshape(1, PACK)
    return ids_ref[pack]


def id_lanes(ids):
    place = lax.broadcasted_iota(jnp.int32, (LANES, PACK), 0)
    match = (place - USED) == ids
    ones = (place >= ONES) & (place < ONES + 3)
    key_side = jnp.where(match | ones, 1.0, 0.0).T
    crop = (place >= USED) & (place < ONES)
    query_side = jnp.where(crop & jnp.logical_not(match), MASKED, 0.0).astype(BF)
    return (key_side, query_side)


def one_head(turned, h, side):
    blank = jnp.zeros((HEAD_DIM, turned.shape[1]), turned.dtype)
    parts = [blank] * HEADS_HERE
    parts[h] = turned[h * HEAD_DIM : (h + 1) * HEAD_DIM]
    return jnp.concatenate(parts + [side], axis=0)


def attention(qkv_ref, a_ref, lse_ref, places, sides):
    ones = jnp.ones((16, PACK), BF)
    blank = jnp.zeros((LANES - USED, PACK), F32)
    heads = [(k, h) for k in range(len(places)) for h in range(HEADS_HERE)]
    held, outs = {}, {}

    def scores_of(k, h):
        if k not in held:
            slot, base = places[k]
            rows, at = pl.ds(base, PACK), slot * 3 * LANES
            query = qkv_ref[rows, at : at + LANES].T
            keys = qkv_ref[rows, at + LANES : at + 2 * LANES]
            values = qkv_ref[rows, at + 2 * LANES : at + 3 * LANES].T
            held[k] = (query, keys, values)
        query, keys, _ = held[k]
        return mm(keys, one_head(query, h, sides[k][USED:]))

    def mix(k, h, top, probs):
        slot, base = places[k]
        rows = pl.ds(base, PACK)
        values = held[k][2][h * HEAD_DIM : (h + 1) * HEAD_DIM]
        mixed = mm(jnp.concatenate([values, ones], axis=0), probs)
        total = mixed[HEAD_DIM : HEAD_DIM + 1]
        outs[(k, h)] = mixed[:HEAD_DIM] * (1.0 / total)
        if lse_ref is not None:
            line = slot * HEADS_HERE + h
            lse_ref[line : line + 1, rows] = top + jnp.log2(total)
        if h == HEADS_HERE - 1:
            parts = [outs[(k, n)] for n in range(HEADS_HERE)] + [blank]
            a_ref[rows, slot * LANES : (slot + 1) * LANES] = (
                jnp.concatenate(parts, axis=0).T.astype(BF)
            )

    scores = scores_of(*heads[0])
    waiting = None
    for n, head in enumerate(heads):
        later = scores_of(*heads[n + 1]) if n + 1 < len(heads) else None
        if waiting is not None:
            mix(*waiting)
        top = jnp.max(scores, axis=0, keepdims=True)
        waiting = head + (top, jnp.exp2(scores - top).astype(BF))
        scores = later
    mix(*waiting)


def enter(x_ref, ids_ref, small, h1_ref, base, pack):
    rows = pl.ds(base, PACK)
    values = x_ref[rows, :].astype(F32)
    unit, _ = norm_parts(values)
    first = (unit * small[0:1] + small[1:2]).astype(BF)
    h1_ref[rows, :] = first
    return id_lanes(crop_line(ids_ref, pack))


def project(first, weight, qkv_ref, key_side, base, slot):
    rows, at = pl.ds(base, PACK), slot * 3 * LANES
    packed = mm(first, weight)
    qkv_ref[rows, at : at + LANES] = (packed[:, :LANES] * EXP_SCALE).astype(BF)
    for k in (1, 2):
        part = packed[:, k * LANES : (k + 1) * LANES] + key_side
        qkv_ref[rows, at + k * LANES : at + (k + 1) * LANES] = part.astype(BF)


def project_all(first, w_ref, qkv_ref, key_side, base):
    for g in range(w_ref.shape[0]):
        project(first, w_ref[g, :, 0 : 3 * LANES], qkv_ref, key_side, base, g)


def leaving(w_ref):
    return gathered(w_ref, 3 * LANES, LANES)


def leave(x_ref, weight, small, a_ref, x1_ref, base):
    rows = pl.ds(base, PACK)
    branch = mm_nt(a_ref[rows, :], weight)
    x1 = x_ref[rows, :].astype(F32) + branch + small[4:5]
    x1_ref[rows, :] = x1
    unit, _ = norm_parts(x1)
    return (unit * small[2:3] + small[3:4]).astype(BF)


def gathered(w_ref, at, width):
    parts = [w_ref[t, :, at : at + width] for t in range(w_ref.shape[0])]
    return jnp.concatenate(parts, axis=1)


def tile_of(w_ref, j, first):
    depth = w_ref.shape[1]
    per = depth // LANES
    parts = []
    for b in range(j * TILE // LANES, (j + 1) * TILE // LANES):
        at = first + (b % per) * LANES
        parts.append(w_ref[b // per, :, at : at + LANES])
    return jnp.concatenate(parts, axis=1)


def key_kernel(
    place_ref, x_ref, ids_ref, w_ref, out_ref, qkv_ref, a_ref, x1_ref, h1_ref, act_ref, bias_ref
):
    rows_here, depth = x_ref.shape
    groups = w_ref.shape[0]
    small = small_rows(w_ref)
    for t in range(groups):
        bias_ref[:, t * depth : (t + 1) * depth] = hidden_row(w_ref, t)

    @pl.loop(0, rows_here // PACK)
    def _(pack):
        base = pl.multiple_of(pack * PACK, PACK)
        rows = pl.ds(base, PACK)
        key_side, query_side = enter(x_ref, ids_ref, small, h1_ref, base, pack)
        project_all(h1_ref[rows, :], w_ref, qkv_ref, key_side, base)
        attention(qkv_ref, a_ref, None, [(g, base) for g in range(groups)], [query_side] * groups)
        second = leave(x_ref, leaving(w_ref), small, a_ref, x1_ref, base)
        feed(second, w_ref, bias_ref, act_ref)
        product = mm_nt(act_ref[...], gathered(w_ref, ATT + depth, depth))
        out_ref[rows, :] = (x1_ref[rows, :] + product + small[5:6]).astype(BF)


def feed(second, w_ref, bias_ref, act_ref, first=ATT):
    tiles = act_ref.shape[1] // TILE
    pre = mm(second, tile_of(w_ref, 0, first))
    for j in range(tiles):
        later = mm(second, tile_of(w_ref, j + 1, first)) if j + 1 < tiles else None
        cols = slice(j * TILE, (j + 1) * TILE)
        bias = bias_ref[:, cols]
        for i in range(0, pre.shape[0], PIECE):
            piece = pre[i : i + PIECE] + bias
            act_ref[i : i + PIECE, cols] = (piece * below(piece)).astype(BF)
        pre = later


def query_kernel(
    place_ref,
    x_ref,
    cot_ref,
    ids_ref,
    w_ref,
    out_ref,
    qkv_ref,
    a_ref,
    lse_ref,
    h1_ref,
    dx1_ref,
    grad_ref,
    line_ref,
    hidden_ref,
    x1_ref,
    h2_ref,
    h2t_ref,
    eb_ref,
    ebt_ref,
    act_ref,
    dpre_ref,
    bias_ref,
):
    rows_here, depth = x_ref.shape
    groups = w_ref.shape[0]
    small = small_rows(w_ref)
    for t in range(groups):
        bias_ref[:, t * depth : (t + 1) * depth] = hidden_row(w_ref, t)

    lse_ref[...] = jnp.zeros_like(lse_ref)
    line_ref[...] = jnp.zeros_like(line_ref)
    h2t_ref[depth:, :] = jnp.ones((h2t_ref.shape[0] - depth, rows_here), BF)

    @pl.loop(0, rows_here // PACK)
    def _(pack):
        base = pl.multiple_of(pack * PACK, PACK)
        rows = pl.ds(base, PACK)
        key_side, query_side = enter(x_ref, ids_ref, small, h1_ref, base, pack)
        project_all(h1_ref[rows, :], w_ref, qkv_ref, key_side, base)
        attention(
            qkv_ref, a_ref, lse_ref, [(g, base) for g in range(groups)], [query_side] * groups
        )
        second = leave(x_ref, leaving(w_ref), small, a_ref, x1_ref, base)
        h2_ref[rows, :] = second
        h2t_ref[0:depth, rows] = second.T
        low = masked_cot(cot_ref, ids_ref, pack, rows).astype(BF)
        eb_ref[rows, :] = low
        ebt_ref[:, rows] = low.T

    feed_back(w_ref, ATT, h2_ref, eb_ref, bias_ref, act_ref, dpre_ref)
    feed_weights(h2t_ref, ebt_ref, act_ref, dpre_ref, grad_ref, hidden_ref)

    @pl.loop(0, rows_here // PACK)
    def _(pack):
        rows = pl.ds(pl.multiple_of(pack * PACK, PACK), PACK)
        x1 = x1_ref[rows, :]
        product = mm_nt(act_ref[rows, :], gathered(w_ref, ATT + depth, depth))
        out_ref[rows, :] = (x1 + product + small[5:6]).astype(BF)
        grad = mm_nt(dpre_ref[rows, :], gathered(w_ref, ATT, depth))
        unit, scale = norm_parts(x1)
        wide = masked_cot(cot_ref, ids_ref, pack, rows)
        dx1 = wide + norm_back(grad, unit, scale, small[2:3])
        dx1_ref[rows, :] = dx1
        line_ref[2:3, :] += jnp.sum(grad * unit, axis=0, keepdims=True)
        line_ref[3:4, :] += jnp.sum(grad, axis=0, keepdims=True)
        line_ref[4:5, :] += jnp.sum(dx1, axis=0, keepdims=True)
        line_ref[5:6, :] += jnp.sum(wide, axis=0, keepdims=True)


def feed_back(w_ref, first, h2_ref, eb_ref, bias_ref, act_ref, dpre_ref):
    rows_here, depth = h2_ref.shape
    tiles = act_ref.shape[1] // TILE
    per = depth // LANES
    step = PACK
    units = [(j, r) for j in range(tiles) for r in range(rows_here // step)]

    def start(unit):
        j, r = unit
        rows = slice(r * step, (r + 1) * step)
        pre = mm(h2_ref[rows, :], tile_of(w_ref, j, first))
        return (pre, mm(eb_ref[rows, :], tile_of(w_ref, j, first + depth)))

    now = start(units[0])
    for k, (j, r) in enumerate(units):
        later = start(units[k + 1]) if k + 1 < len(units) else None
        cols = slice(j * TILE, (j + 1) * TILE)
        bias = bias_ref[:, cols]
        pre, da = now
        for i in range(0, step, PIECE):
            rows = slice(r * step + i, r * step + i + PIECE)
            piece = pre[i : i + PIECE] + bias
            phi, slope = below_and_slope(piece)
            act_ref[rows, cols] = (piece * phi).astype(BF)
            dpre_ref[rows, cols] = (da[i : i + PIECE] * slope).astype(BF)
        now = later


def feed_weights(h2t_ref, ebt_ref, act_ref, dpre_ref, grad_ref, hidden_ref):
    depth = ebt_ref.shape[0]
    per = depth // LANES
    for j in range(act_ref.shape[1] // TILE):
        cols = slice(j * TILE, (j + 1) * TILE)
        gup = mm(h2t_ref[...], dpre_ref[:, cols])
        gdown = mm(ebt_ref[...], act_ref[:, cols])
        for n, b in enumerate((2 * j, 2 * j + 1)):
            t, o = b // per, (b % per) * LANES
            part = slice(n * LANES, (n + 1) * LANES)
            grad_ref[t, :, o : o + LANES] = gup[:depth, part].astype(BF)
            grad_ref[t, :, depth + o : depth + o + LANES] = gdown[:, part].astype(BF)
            hidden_ref[t : t + 1, o : o + LANES] = gup[depth : depth + 1, part]


def masked_cot(cot_ref, ids_ref, pack, rows):
    valid = jnp.where(crop_line(ids_ref, pack) < CROPS, 1.0, 0.0)
    valid = jnp.broadcast_to(valid, (LANES, PACK)).T[:, 0:1]
    return cot_ref[rows, :].astype(F32) * valid


def attention_back(qkv_ref, a_ref, lse_ref, da_ref, dqkv_ref, places, sides):
    place = lax.broadcasted_iota(jnp.int32, (LANES - USED, PACK), 0) + USED
    lane = lax.broadcasted_iota(jnp.int32, (PACK, LANES), 1) // HEAD_DIM
    none = jnp.zeros((PACK, LANES), BF)

    def split(line):
        high = line.astype(BF).astype(F32)
        rest = line - high
        middle = rest.astype(BF).astype(F32)
        low = rest - middle
        block = jnp.where(
            place == ONES,
            high,
            jnp.where(place == ONES + 1, middle, jnp.where(place == ONES + 2, low, 0.0)),
        )
        return block.astype(BF)

    held, made = {}, {}
    heads = [(k, h) for k in range(len(places)) for h in range(HEADS_HERE)]

    def load(k):
        slot, base, da_at, _ = places[k]
        rows, at = pl.ds(base, PACK), slot * 3 * LANES
        query = qkv_ref[rows, at : at + LANES]
        keys = qkv_ref[rows, at + LANES : at + 2 * LANES]
        values = qkv_ref[rows, at + 2 * LANES : at + 3 * LANES]
        grad = da_ref[rows, da_at * LANES : (da_at + 1) * LANES]
        grad_t = grad.T
        mixed = a_ref[rows, slot * LANES : (slot + 1) * LANES].T
        both = mixed.astype(F32) * grad_t.astype(F32)
        held[k] = (query, keys, values, grad, query.T, keys.T, grad_t, both)

    def scores_of(k, h):
        if k not in held:
            load(k)
        slot, base, _, _ = places[k]
        query, keys, values, grad, query_t, keys_t, grad_t, both = held[k]
        part = slice(h * HEAD_DIM, (h + 1) * HEAD_DIM)
        line = slot * HEADS_HERE + h
        lse = lse_ref[line : line + 1, pl.ds(base, PACK)]
        side = jnp.where(place < ONES, sides[k][USED:], split(-lse))
        scores = mm(keys, one_head(query_t, h, side))
        inner = jnp.sum(both[part], axis=0, keepdims=True)
        pull = mm(values, one_head(grad_t, h, split(-inner)))
        return (scores, pull)

    def finish(k, h, low, dscores):
        query, keys, values, grad, query_t, keys_t, grad_t, both = held[k]
        part = slice(h * HEAD_DIM, (h + 1) * HEAD_DIM)
        dv = mm(low, jnp.where(lane == h, grad, none))
        dk = mm(dscores, jnp.where(lane == h, query, none))
        dq = mm(keys_t[part], dscores)
        if h:
            last = made[k]
            made[k] = (last[0] + [dq], last[1] + dk, last[2] + dv)
        else:
            made[k] = ([dq], dk, dv)
        if h == HEADS_HERE - 1:
            dqs, dk, dv = made[k]
            dqs = jnp.concatenate(dqs + [jnp.zeros((LANES - USED, PACK), F32)], axis=0)
            _, base, _, slot = places[k]
            rows, at = pl.ds(base, PACK), slot * 3 * LANES
            dqkv_ref[rows, at : at + LANES] = (dqs.T * SCALE).astype(BF)
            dqkv_ref[rows, at + LANES : at + 2 * LANES] = (dk * LOG_TWO).astype(BF)
            dqkv_ref[rows, at + 2 * LANES : at + 3 * LANES] = dv.astype(BF)

    now = scores_of(*heads[0])
    waiting = None
    for n, head in enumerate(heads):
        later = scores_of(*heads[n + 1]) if n + 1 < len(heads) else None
        if waiting is not None:
            finish(*waiting)
        scores, pull = now
        probs = jnp.exp2(scores)
        waiting = head + (probs.astype(BF), (probs * pull).astype(BF))
        now = later
    finish(*waiting)


def back_kernel(
    place_ref,
    x_ref,
    ids_ref,
    w_ref,
    qkv_ref,
    a_ref,
    lse_ref,
    h1_ref,
    dx1_ref,
    line_ref,
    hidden_ref,
    out_ref,
    grad_ref,
    da_ref,
    dqkv_ref,
    h1t_ref,
    dybt_ref,
    sums_ref,
):
    rows_here, depth = x_ref.shape
    groups = w_ref.shape[0]
    small = small_rows(w_ref)
    sums_ref[...] = jnp.zeros_like(sums_ref)
    sums_ref[SMALL_AT : SMALL_AT + 8, :] = line_ref[...]

    @pl.loop(0, rows_here // PACK)
    def _(pack):
        base = pl.multiple_of(pack * PACK, PACK)
        rows = pl.ds(base, PACK)
        _, query_side = id_lanes(ids_ref[pack])
        low = dx1_ref[rows, :].astype(BF)
        dybt_ref[:, rows] = low.T
        h1t_ref[:, rows] = h1_ref[rows, :].T
        for g in range(groups):
            da_ref[rows, g * LANES : (g + 1) * LANES] = mm(
                low, w_ref[g, :, 3 * LANES : 4 * LANES]
            ).astype(BF)
        places = [(g, base, g, g) for g in range(groups)]
        attention_back(qkv_ref, a_ref, lse_ref, da_ref, dqkv_ref, places, [query_side] * groups)
        width = 3 * LANES
        grad = mm_nt(dqkv_ref[rows, 0:width], w_ref[0, :, 0:width])
        for g in range(1, groups):
            grad += mm_nt(dqkv_ref[rows, g * width : (g + 1) * width], w_ref[g, :, 0:width])
        unit, scale = norm_parts(x_ref[rows, :].astype(F32))
        back = norm_back(grad, unit, scale, small[0:1])
        out_ref[rows, :] = (dx1_ref[rows, :] + back).astype(BF)
        sums_ref[SMALL_AT : SMALL_AT + 1, :] += jnp.sum(grad * unit, axis=0, keepdims=True)
        sums_ref[SMALL_AT + 1 : SMALL_AT + 2, :] += jnp.sum(grad, axis=0, keepdims=True)

    lane = lax.broadcasted_iota(jnp.int32, (depth, LANES), 1)
    for g in range(groups):
        width = 3 * LANES
        sums_ref[HIDDEN_AT : HIDDEN_AT + 1, :] = hidden_ref[g : g + 1, :]
        extra = sums_ref[...].T
        entry = mm(h1t_ref[...], dqkv_ref[:, g * width : (g + 1) * width])
        grad_ref[g, :, 0:LANES] = jnp.where(lane < USED, entry[:, :LANES], extra).astype(BF)
        grad_ref[g, :, LANES:width] = entry[:, LANES:].astype(BF)
        grad_ref[g, :, width : width + LANES] = mm(
            dybt_ref[...], a_ref[:, g * LANES : (g + 1) * LANES]
        ).astype(BF)


def params():
    return pltpu.CompilerParams(vmem_limit_bytes=60 * 2**20)


def whole(shape):
    return pl.BlockSpec(shape, lambda i, place: (0,) * len(shape))


def own_rows(rows, depth):
    return pl.BlockSpec((rows, depth), lambda i, place: (place[0], 0))


def own_ids(packs):
    return pl.BlockSpec((packs, 1, PACK), lambda i, place: (place[0], 0, 0))


def run_key(place, tokens, ids, weights, rows):
    depth = tokens.shape[1]
    groups, _, width = weights.shape
    return pl.pallas_call(
        key_kernel,
        grid_spec=pltpu.PrefetchScalarGridSpec(
            num_scalar_prefetch=1,
            grid=(1,),
            in_specs=[own_rows(rows, depth), own_ids(rows // PACK), whole(weights.shape)],
            out_specs=whole((rows, depth)),
            scratch_shapes=[
                VMEM((rows, groups * 3 * LANES), BF),
                VMEM((rows, groups * LANES), BF),
                VMEM((rows, depth), F32),
                VMEM((rows, depth), BF),
                VMEM((PACK, groups * depth), BF),
                VMEM((1, groups * depth), F32),
            ],
        ),
        out_shape=jax.ShapeDtypeStruct((rows, depth), BF),
        compiler_params=params(),
        name="key_block",
    )(place, tokens, ids, weights)


def run_query(place, tokens, cotangent, ids, weights, rows):
    depth = tokens.shape[1]
    groups = weights.shape[0]
    outs = [
        ((rows, depth), BF),
        ((rows, groups * 3 * LANES), BF),
        ((rows, groups * LANES), BF),
        ((16, rows), F32),
        ((rows, depth), BF),
        ((rows, depth), F32),
        ((groups, depth, 2 * depth), BF),
        ((8, depth), F32),
        ((groups, depth), F32),
    ]
    return pl.pallas_call(
        query_kernel,
        grid_spec=pltpu.PrefetchScalarGridSpec(
            num_scalar_prefetch=1,
            grid=(1,),
            in_specs=[
                own_rows(rows, depth),
                own_rows(rows, depth),
                own_ids(rows // PACK),
                whole(weights.shape),
            ],
            out_specs=[whole(shape) for shape, _ in outs],
            scratch_shapes=[
                VMEM((rows, depth), F32),
                VMEM((rows, depth), BF),
                VMEM((depth + 16, rows), BF),
                VMEM((rows, depth), BF),
                VMEM((depth, rows), BF),
                VMEM((rows, groups * depth), BF),
                VMEM((rows, groups * depth), BF),
                VMEM((1, groups * depth), F32),
            ],
        ),
        out_shape=[jax.ShapeDtypeStruct(shape, kind) for shape, kind in outs],
        compiler_params=params(),
        name="query_block",
    )(place, tokens, cotangent, ids, weights)


def run_back(place, tokens, ids, weights, kept, rows):
    depth = tokens.shape[1]
    groups = weights.shape[0]
    return pl.pallas_call(
        back_kernel,
        grid_spec=pltpu.PrefetchScalarGridSpec(
            num_scalar_prefetch=1,
            grid=(1,),
            in_specs=[own_rows(rows, depth), own_ids(rows // PACK), whole((groups, depth, ATT))]
            + [whole(item.shape) for item in kept],
            out_specs=[whole((rows, depth)), whole((groups, depth, ATT))],
            scratch_shapes=[
                VMEM((rows, groups * LANES), BF),
                VMEM((rows, groups * 3 * LANES), BF),
                VMEM((depth, rows), BF),
                VMEM((depth, rows), BF),
                VMEM((LANES, depth), F32),
            ],
        ),
        out_shape=[
            jax.ShapeDtypeStruct((rows, depth), BF),
            jax.ShapeDtypeStruct((groups, depth, ATT), BF),
        ],
        compiler_params=params(),
        name="back_block",
    )(place, tokens, ids, weights, *kept)


def pack_piece(entry, leave, up, down, small, hidden):
    def fill(block, *extra):
        block = jnp.concatenate([block] + [item.astype(block.dtype) for item in extra], axis=1)
        return jnp.pad(block, ((0, 0), (0, LANES - block.shape[1])))

    parts = [
        fill(entry[:, 0], small.T, hidden[:, None]),
        fill(entry[:, 1]),
        fill(entry[:, 2]),
        fill(leave.T),
        up,
        down.T,
    ]
    return jnp.concatenate([part.astype(BF) for part in parts], axis=1)


def unpack_piece(piece, depth):
    entry = jnp.stack([piece[:, k * LANES : k * LANES + USED] for k in range(3)], axis=1)
    leave = piece[:, 3 * LANES : 3 * LANES + USED].T
    up = piece[:, ATT : ATT + depth]
    down = piece[:, ATT + depth :].T
    small = piece[:, SMALL_AT : SMALL_AT + 6].T
    return (entry, leave, up, down, small, piece[:, HIDDEN_AT])


def adamw(grad, first, second, master, decay, rate):
    moment = BETA_ONE * first + (1.0 - BETA_ONE) * grad
    square = BETA_TWO * second + (1.0 - BETA_TWO) * grad * grad
    ahead = moment / (1.0 - BETA_ONE**STEP)
    spread = square / (1.0 - BETA_TWO**STEP)
    return (
        moment,
        square,
        master - rate * (ahead / (jnp.sqrt(spread) + ADAM_EPS) + decay * master),
    )


DECAYS = (DECAY, DECAY, DECAY, DECAY, 0.0, 0.0)
RATES = (RATE_MATRIX, RATE_EXIT, RATE_MATRIX, RATE_MATRIX, RATE_SMALL, RATE_BIAS)


def finish_plain(grad_att, grad_ffn, masters, firsts, seconds):
    depth = grad_att.shape[1]
    grads = jnp.concatenate([grad_att, grad_ffn], axis=2).astype(F32)
    own = lax.psum_scatter(grads, "tensor", scatter_dimension=0, tiled=False)
    own = lax.psum_scatter(own, "dp", scatter_dimension=0, tiled=True)
    shares = unpack_piece(own, depth)
    copies = float(lax.axis_size("tensor"))
    total = jnp.sum(shares[4] * shares[4]) / copies
    for k in (0, 1, 2, 3, 5):
        total = total + jnp.sum(shares[k] * shares[k])
    norm_value = jnp.sqrt(lax.psum(total, ("dp", "tensor")))
    factor = CLIP / jnp.maximum(norm_value, CLIP)
    outs = []
    for k in range(6):
        outs.extend(
            adamw(shares[k] * factor, firsts[k], seconds[k], masters[k], DECAYS[k], RATES[k])
        )
    return (norm_value, outs)


def spot():
    dp, t = lax.axis_index("dp"), lax.axis_index("tensor")
    return (dp, t)


def flip(value, bits):
    for bit in (1, 2, 4):
        if bits & bit:
            value = value + bit - 2 * bit * ((value // bit) % 2)
    return value


def hello(peers):
    barrier = pltpu.get_barrier_semaphore()
    for peer in peers:
        pl.semaphore_signal(barrier, inc=1, device_id=peer, device_id_type=MESH)


def wait_for(peers):
    pl.semaphore_wait(pltpu.get_barrier_semaphore(), len(peers))


KEY_PARTS = 3
SENDS = 62 + 9 + 18 + 51 + 10


class Mail:
    def __init__(self, send_sem, recv_sem):
        self.send_sem, self.recv_sem = send_sem, recv_sem
        self.count, self.sent = 0, []

    def send(self, src, dst, peer):
        copy = pltpu.make_async_remote_copy(
            src_ref=src,
            dst_ref=dst,
            send_sem=self.send_sem.at[self.count],
            recv_sem=self.recv_sem.at[self.count],
            device_id=peer,
            device_id_type=MESH,
        )
        copy.start()
        self.count += 1
        self.sent.append(copy)
        return copy

    def close(self):
        for copy in self.sent:
            copy.wait_send()


def arrived(copies):
    for copy in copies:
        copy.wait_recv()


def load_rows(src, dst, t, sem):
    count = dst.shape[0]
    copy = pltpu.make_async_copy(src.at[pl.ds(t * count, count)], dst, sem)
    copy.start()
    return copy


def fold(block):
    out = block[0:8]
    for k in range(8, block.shape[0], 8):
        out = out + block[k : k + 8]
    return out


class Reduce:
    def __init__(self, mail, grad_ref, refs, where):
        self.mail, self.grad = mail, grad_ref
        self.rc, self.s0, self.r1, self.s1, self.r2, self.s2, self.r3 = refs
        self.where = where
        self.core = [None, None]
        self.side = [None, None]
        self.line = [None, None]
        self.across = None

    def slab(self, group, k):
        rows = self.s1.shape[2]
        return self.grad.at[group, pl.ds(pl.multiple_of(k * rows, 16), rows)]

    def to_core(self, q):
        dp, t, core, across, side, line = self.where
        self.core[q] = self.mail.send(self.grad.at[flip(t, 1 + 2 * q)], self.rc.at[q], core)

    def to_side(self, q):
        dp, t, core, across, side, line = self.where
        self.core[q].wait_recv()
        own = flip(t, 2 * q)
        y = dp % 2
        rows = self.s1.shape[2]

        @pl.loop(0, 8)
        def _(k):
            part = pl.ds(pl.multiple_of(k * rows, 16), rows)
            left = self.grad[own, part, :].astype(F32)
            self.s0[q, k] = (left + self.rc[q, part, :].astype(F32)).astype(BF)

        self.side[q] = [
            self.mail.send(self.s0.at[q, 2 * w + 1 - y], self.r1.at[q, w], side) for w in range(4)
        ]

    def to_line(self, q):
        dp, t, core, across, side, line = self.where
        arrived(self.side[q])
        y = dp % 2

        @pl.loop(0, 4)
        def _(w):
            left = self.s0[q, 2 * w + y].astype(F32)
            self.s1[q, w] = (left + self.r1[q, w].astype(F32)).astype(BF)

        self.line[q] = [
            self.mail.send(self.s1.at[q, line[j][0] // 2], self.r2.at[q, j - 1], line[j])
            for j in range(1, 4)
        ]

    def to_across(self, q):
        dp, t, core, across, side, line = self.where
        arrived(self.line[q])
        total = self.s1[q, dp // 2].astype(F32)
        for j in range(3):
            total = total + self.r2[q, j].astype(F32)
        self.s2[q] = total.astype(BF)
        if q:
            self.across = self.mail.send(self.s2.at[1], self.r3, across)

    def result(self):
        self.across.wait_recv()
        return self.s2[0].astype(F32) + self.r3[...].astype(F32)


class Spread:
    def __init__(self, mail, where, own_ref, out_ref, first, sem):
        dp, t, core, across, side, line = where
        self.mail, self.where, self.out = mail, where, out_ref
        self.count = own_ref.shape[0]
        self.first = first
        here = self.part(t)
        self.across = mail.send(own_ref, here, across)
        self.core = [mail.send(own_ref, here, core)]
        self.local = pltpu.make_async_copy(own_ref, here, sem)
        self.local.start()

    def part(self, t):
        at = t * self.first[1] + self.first[0]
        return self.out.at[pl.ds(pl.multiple_of(at, 16), self.count)]

    def forward(self):
        dp, t, core, across, side, line = self.where
        self.across.wait_recv()
        far = self.part(flip(t, 2))
        self.core.append(self.mail.send(far, far, core))

    def finish(self):
        arrived(self.core)
        self.local.wait()


class Gather:
    def __init__(self, mail, where, own_ref, all_ref, sem):
        self.mail, self.where, self.own, self.all = mail, where, own_ref, all_ref
        dp, t, core, across, side, line = where
        self.local = pltpu.make_async_copy(own_ref, self.piece(t, dp), sem)
        self.local.start()

    def piece(self, group, dp):
        rows = self.own.shape[0]
        return self.all.at[group, pl.ds(pl.multiple_of(dp * rows, 16), rows)]

    def start_across(self):
        dp, t, core, across, side, line = self.where
        self.across = self.mail.send(self.own, self.piece(t, dp), across)

    def start(self):
        dp, t, core, across, side, line = self.where
        send, here = self.mail.send, self.piece(t, dp)
        self.line = [[send(self.own, here, line[j])] for j in range(1, 4)]
        self.side = [[send(self.own, here, side)], [], [], []]
        self.core = [[send(self.own, here, core)], []]

    def pass_across(self):
        dp, t, core, across, side, line = self.where
        send, far = self.mail.send, self.piece(flip(t, 2), dp)
        self.across.wait_recv()
        for j in range(1, 4):
            self.line[j - 1].append(send(far, far, line[j]))
        self.side[0].append(send(far, far, side))
        self.core[1].append(send(far, far, core))

    def pass_line(self, k):
        dp, t, core, across, side, line = self.where
        for j in range(1, 4):
            self.line[j - 1][k].wait_recv()
            piece = self.piece(flip(t, 2 * k), line[j][0])
            self.side[j].append(self.mail.send(piece, piece, side))
            self.core[k].append(self.mail.send(piece, piece, core))

    def pass_side(self, k):
        dp, t, core, across, side, line = self.where
        for j in range(4):
            self.side[j][k].wait_recv()
            piece = self.piece(flip(t, 2 * k), flip(line[j][0], 1))
            self.core[k].append(self.mail.send(piece, piece, core))

    def finish(self, k):
        arrived(self.core[k])


def block_kernel(*refs):
    entry_ref, leave_ref, up_ref, down_ref, small_ref, hidden_ref = refs[0:6]
    key_entry, key_leave, key_up, key_down, key_small, key_hidden = refs[6:12]
    tokens_ref, cot_all_ref, key_tokens_ref, crops_ref = refs[12:16]
    block_out, key_out, input_grad, norm_ref, own_a, own_f, own_s = refs[16:23]
    (
        kx_ref, qx_ref, cot_ref, ids_ref, pa_ref, pf_ref, keys_ref, wa_ref, wf_ref,
        kqkv_ref, qqkv_ref, ka_ref, qa_ref, lse_ref, kh_ref, h1_ref, kx1_ref, x1_ref,
        act_ref, dpre_ref, h2_ref, h2t_ref, eb_ref, ebt_ref, bias_ref, hid_ref, line_ref,
        unit_ref, scale_ref, h1t_ref, dyb_ref, dybt_ref, dqkv_ref, ga_ref, ge_ref, gf_ref,
        key_rows, block_rows, grad_rows, near_ref, far_ref, turn_ref,
    ) = refs[23:65]
    red_a, red_e, red_f = refs[65:72], refs[72:79], refs[79:86]
    send_sem, recv_sem, local_sem = refs[86:]
    dp, t = spot()
    far = flip(t, 2)
    core, across = (dp, flip(t, 1)), (dp, far)
    side = (flip(dp, 1), t)
    line = [(flip(dp, 2 * j), t) for j in range(4)]
    where = (dp, t, core, across, side, line)
    mail = Mail(send_sem, recv_sem)
    send = mail.send
    loads = [
        load_rows(src, dst, t, local_sem.at[k])
        for k, (src, dst) in enumerate(
            ((key_tokens_ref, kx_ref), (crops_ref, ids_ref), (tokens_ref, qx_ref), (cot_all_ref, cot_ref))
        )
    ]

    peers = [(dp, flip(t, k)) for k in (1, 2, 3)] + [(flip(dp, k), t) for k in range(1, 8)]
    hello(peers)
    rows, depth = up_ref.shape
    wide = LANES - USED
    extra = [small_ref[...], hidden_ref[...], jnp.zeros((wide - 7, rows), F32)]
    extra = jnp.concatenate(extra, axis=0).T
    blank = jnp.zeros((rows, wide), F32)
    for k, block in enumerate([entry_ref[0], entry_ref[1], entry_ref[2], leave_ref[...]]):
        block = jnp.concatenate([block, blank if k else extra], axis=1)
        pa_ref[:, k * LANES : (k + 1) * LANES] = block.astype(BF)
    wait_for(peers)
    gather_a = Gather(mail, where, pa_ref, wa_ref, local_sem.at[4])
    gather_a.start_across()
    gather_a.start()

    parts = [pl.ds(0, ATT), pl.ds(ATT, depth), pl.ds(ATT + depth, depth)]

    def key_part(group, k):
        return keys_ref.at[group, :, parts[k]]

    def key_send(k, peer):
        return send(key_part(t, k), key_part(t, k), peer)

    blank = jnp.zeros((wide, depth), BF)
    extra = [key_small[...], key_hidden[...].reshape(1, depth), jnp.zeros((wide - 7, depth), BF)]
    for k, block in enumerate([key_entry[0], key_entry[1], key_entry[2], key_leave[...]]):
        block = jnp.concatenate([block] + ([blank] if k else extra), axis=0)
        keys_ref[t, :, k * LANES : (k + 1) * LANES] = block.T
    key_across = [key_send(0, across)]
    key_core = [key_send(0, core)]
    pf_ref[:, 0:depth] = up_ref[...].astype(BF)
    pf_ref[:, depth:] = down_ref[...].astype(BF)
    gather_f = Gather(mail, where, pf_ref, wf_ref, local_sem.at[5])
    gather_f.start_across()
    keys_ref[t, :, ATT : ATT + depth] = key_up[...]
    keys_ref[t, :, ATT + depth :] = key_down[...].T
    key_across += [key_send(k, across) for k in (1, 2)]
    key_core += [key_send(k, core) for k in (1, 2)]

    packs = kx_ref.shape[0] // PACK
    bases = [pack * PACK for pack in range(packs)]
    spots = [slice(base, base + PACK) for base in bases]
    loads[0].wait()
    loads[1].wait()
    key_norms = small_rows_of(keys_ref[t, :, 0:LANES])
    masks = [enter(kx_ref, ids_ref, key_norms, kh_ref, base, k) for k, base in enumerate(bases)]
    sides = [query_side for _, query_side in masks]

    def heads_of(slot, weight, first_ref, qkv_ref, a_ref, lse):
        for base, (key_side, _) in zip(bases, masks):
            project(first_ref[base : base + PACK, :], weight, qkv_ref, key_side, base, slot)
        attention(qkv_ref, a_ref, lse, [(slot, base) for base in bases], sides)

    def key_heads(slot):
        heads_of(slot, keys_ref[flip(t, slot), :, 0 : 3 * LANES], kh_ref, kqkv_ref, ka_ref, None)

    def query_heads(slot):
        heads_of(slot, wa_ref[flip(t, slot), :, 0 : 3 * LANES], h1_ref, qqkv_ref, qa_ref, lse_ref)

    def pass_key(k):
        key_across[k].wait_recv()
        return send(key_part(far, k), key_part(far, k), core)

    key_heads(0)
    gather_a.pass_across()
    gather_f.start()
    arrived(key_core[:1])
    key_heads(1)
    gather_a.pass_line(0)
    loads[2].wait()
    loads[3].wait()
    for k, spot_rows in enumerate(spots):
        low = masked_cot(cot_ref, ids_ref, k, spot_rows).astype(BF)
        eb_ref[spot_rows, :] = low
        ebt_ref[:, spot_rows] = low.T
        unit, scale = norm_parts(qx_ref[spot_rows, :].astype(F32))
        unit_ref[spot_rows, :] = unit
        scale_ref[spot_rows, :] = jnp.broadcast_to(scale, (PACK, LANES))
    gather_a.pass_side(0)
    gather_a.local.wait()
    norms = small_rows_of(wa_ref[t, :, 0:LANES])
    for spot_rows in spots:
        first = (unit_ref[spot_rows, :] * norms[0:1] + norms[1:2]).astype(BF)
        h1_ref[spot_rows, :] = first
        h1t_ref[:, spot_rows] = first.T
    query_heads(0)
    gather_a.pass_line(1)
    key_far = [pass_key(0)]
    gather_f.pass_across()
    key_heads(2)
    arrived(key_far)
    key_heads(3)
    gather_f.pass_line(0)
    gather_a.pass_side(1)

    def leaving_of(w_ref):
        weights = [w_ref[flip(t, k), :, 3 * LANES : 4 * LANES] for k in range(4)]
        return jnp.concatenate(weights, axis=1)

    weight = leaving_of(keys_ref)
    for base in bases:
        second = leave(kx_ref, weight, key_norms, ka_ref, kx1_ref, base)
        kh_ref[base : base + PACK, :] = second
    for k in range(4):
        bias_ref[:, k * depth : (k + 1) * depth] = hidden_line(keys_ref[k, :, 0:LANES])
    gather_a.finish(0)
    query_heads(1)
    key_far.append(pass_key(1))
    gather_f.pass_line(1)
    arrived(key_core[1:2] + key_far[1:2])
    feed(kh_ref[spots[0], :], keys_ref, bias_ref, act_ref.at[spots[0]])
    gather_f.pass_side(0)
    feed(kh_ref[spots[1], :], keys_ref, bias_ref, act_ref.at[spots[1]])
    key_far.append(pass_key(2))
    gather_a.finish(1)
    query_heads(2)
    arrived(key_core[2:] + key_far[2:])
    weight = gathered(keys_ref, ATT + depth, depth)
    count = key_rows.shape[0]
    spread_key = []
    for k, spot_rows in enumerate(spots):
        product = mm_nt(act_ref[spot_rows, :], weight)
        key_rows[spot_rows, :] = (kx1_ref[spot_rows, :] + product + key_norms[5:6]).astype(BF)
        part = key_rows.at[spot_rows]
        first = (k * PACK, count)
        spread_key.append(Spread(mail, where, part, key_out, first, local_sem.at[(6, 10)[k]]))
    gather_f.pass_side(1)
    query_heads(3)
    weight = leaving_of(wa_ref)
    for base in bases:
        second = leave(qx_ref, weight, norms, qa_ref, x1_ref, base)
        h2_ref[base : base + PACK, :] = second
        h2t_ref[0:depth, base : base + PACK] = second.T
    h2t_ref[depth:, :] = jnp.ones((h2t_ref.shape[0] - depth, h2t_ref.shape[1]), BF)
    gather_f.finish(0)
    gather_f.finish(1)
    gather_f.local.wait()
    for k in range(4):
        bias_ref[:, k * depth : (k + 1) * depth] = hidden_line(wa_ref[k, :, 0:LANES])
    feed_back(wf_ref, 0, h2_ref, eb_ref, bias_ref, act_ref, dpre_ref)
    weight = gathered(wf_ref, depth, depth)
    spread_block = []
    for k, spot_rows in enumerate(spots):
        product = mm_nt(act_ref[spot_rows, :], weight)
        block_rows[spot_rows, :] = (x1_ref[spot_rows, :] + product + norms[5:6]).astype(BF)
        part = block_rows.at[spot_rows]
        first = (k * PACK, count)
        spread_block.append(Spread(mail, where, part, block_out, first, local_sem.at[(7, 11)[k]]))
    feed_weights(h2t_ref, ebt_ref, act_ref, dpre_ref, gf_ref, hid_ref)
    reduce_f = Reduce(mail, gf_ref, red_f, where)
    reduce_f.to_core(0)
    reduce_f.to_core(1)
    line_ref[...] = jnp.zeros_like(line_ref)
    weight = gathered(wf_ref, 0, depth)
    for k, spot_rows in enumerate(spots):
        grad = mm_nt(dpre_ref[spot_rows, :], weight)
        unit, scale = norm_parts(x1_ref[spot_rows, :])
        wide_cot = masked_cot(cot_ref, ids_ref, k, spot_rows)
        dx1 = wide_cot + norm_back(grad, unit, scale, norms[2:3])
        x1_ref[spot_rows, :] = dx1
        low = dx1.astype(BF)
        dyb_ref[spot_rows, :] = low
        dybt_ref[:, spot_rows] = low.T
        line_ref[2:3, :] += jnp.sum(grad * unit, axis=0, keepdims=True)
        line_ref[3:4, :] += jnp.sum(grad, axis=0, keepdims=True)
        line_ref[4:5, :] += jnp.sum(dx1, axis=0, keepdims=True)
        line_ref[5:6, :] += jnp.sum(wide_cot, axis=0, keepdims=True)
    mixed = mm(dybt_ref[...], qa_ref[...]).astype(BF)
    for slot in range(4):
        ge_ref[flip(t, slot)] = mixed[:, slot * LANES : (slot + 1) * LANES]
    reduce_f.to_side(0)
    reduce_f.to_side(1)

    reduce_a = Reduce(mail, ga_ref, red_a, where)
    reduce_e = Reduce(mail, ge_ref, red_e, where)
    reduce_e.to_core(0)
    reduce_e.to_core(1)
    lane = lax.broadcasted_iota(jnp.int32, (depth, LANES), 1)
    width = 3 * LANES

    weight = leaving_of(wa_ref)
    for base in bases:
        ka_ref[base : base + PACK, :] = mm(dyb_ref[base : base + PACK, :], weight).astype(BF)

    def back_heads(slots, pack):
        places = [(slot, bases[pack], slot, slot) for slot in slots]
        side = [sides[pack]] * len(slots)
        attention_back(qqkv_ref, qa_ref, lse_ref, ka_ref, dqkv_ref, places, side)

    def back_weights(slot):
        group = flip(t, slot)
        entry = mm(h1t_ref[...], dqkv_ref[:, slot * width : (slot + 1) * width])
        hidden = jnp.broadcast_to(hid_ref[pl.ds(group, 1), :], (LANES, depth)).T
        ga_ref[group, :, 0:LANES] = jnp.where(lane == HIDDEN_AT, hidden, entry[:, :LANES]).astype(BF)
        ga_ref[group, :, LANES:width] = entry[:, LANES:].astype(BF)

    def back_rows(pack):
        spot_rows = spots[pack]
        weight = jnp.concatenate([wa_ref[flip(t, k), :, 0:width] for k in range(4)], axis=1)
        grad = mm_nt(dqkv_ref[spot_rows, :], weight)
        unit, scale = unit_ref[spot_rows, :], scale_ref[spot_rows, 0:1]
        back = norm_back(grad, unit, scale, norms[0:1])
        grad_rows[spot_rows, :] = (x1_ref[spot_rows, :] + back).astype(BF)
        first = (pack * PACK, count)
        sem = local_sem.at[8 + pack]
        item = Spread(mail, where, grad_rows.at[spot_rows], input_grad, first, sem)
        line_ref[0:1, :] += jnp.sum(grad * unit, axis=0, keepdims=True)
        line_ref[1:2, :] += jnp.sum(grad, axis=0, keepdims=True)
        return item

    back_heads((3, 2), 0)
    reduce_e.to_side(0)
    reduce_e.to_side(1)
    for item in spread_key:
        item.forward()
    back_heads((1, 0), 0)
    reduce_f.to_line(0)
    spread_grad = [back_rows(0)]
    back_heads((3,), 1)
    back_weights(3)
    reduce_a.to_core(1)
    reduce_f.to_line(1)
    back_heads((2,), 1)
    back_weights(2)
    reduce_a.to_side(1)
    reduce_e.to_line(0)
    reduce_e.to_line(1)
    for item in spread_block:
        item.forward()
    back_heads((1,), 1)
    back_weights(1)
    reduce_a.to_core(0)
    reduce_a.to_line(1)
    reduce_f.to_across(0)
    reduce_f.to_across(1)
    reduce_e.to_across(0)
    reduce_e.to_across(1)
    back_heads((0,), 1)
    back_weights(0)
    reduce_a.to_side(0)
    reduce_a.to_across(1)
    spread_grad.append(back_rows(1))
    reduce_a.to_line(0)
    grad_e = reduce_e.result()
    grad_f = reduce_f.result()
    spread_grad[0].forward()
    reduce_a.to_across(0)
    grad_a = jnp.concatenate([reduce_a.result(), grad_e], axis=1)

    total = jnp.zeros((8, LANES), F32)
    lane = lax.broadcasted_iota(jnp.int32, (rows, LANES), 1)
    for k in range(4):
        block = grad_a[:, k * LANES : (k + 1) * LANES]
        share = jnp.where(lane < USED, 1.0, jnp.where(lane == HIDDEN_AT, 0.0 if k else 1.0, 0.0))
        total = total + fold(block * block * share)
    for k in range(2 * depth // LANES):
        block = grad_f[:, k * LANES : (k + 1) * LANES]
        total = total + fold(block * block)
    near_ref[t, 0:8, :] = line_ref[...]
    near_ref[t, 8:16, :] = jnp.concatenate([total] + [jnp.zeros_like(total)] * 2, axis=1)
    near = [send(near_ref.at[t], near_ref.at[t], (dp, flip(t, k))) for k in (1, 2, 3)]
    arrived(near)
    far_ref[dp] = (near_ref[0] + near_ref[1]) + (near_ref[2] + near_ref[3])
    wide_sends = [send(far_ref.at[dp], far_ref.at[dp], (flip(dp, k), t)) for k in range(1, 8)]
    own_a[...] = grad_a
    own_f[...] = grad_f
    spread_grad[1].forward()
    arrived(wide_sends)
    total = far_ref[0]
    for k in range(1, 8):
        total = total + far_ref[k]
    lines = total[0:8]
    squares = fold(total[8:16, 0:LANES])
    for k in range(depth // LANES):
        block = lines[:, k * LANES : (k + 1) * LANES]
        squares = squares + block * block
    squares = jnp.sum(jnp.sum(squares, axis=0, keepdims=True), axis=1, keepdims=True)
    norm_ref[...] = jnp.broadcast_to(jnp.sqrt(squares), norm_ref.shape)
    turn_ref[...] = jnp.concatenate([lines, jnp.zeros((LANES - 8, depth), F32)], axis=0).T
    own_s[...] = turn_ref[pl.ds(pl.multiple_of(dp * rows, 16), rows), :]
    for item in spread_key + spread_block + spread_grad:
        item.finish()
    mail.close()


def lay(entry, leave, up, down, small, hidden):
    return [entry.transpose(1, 0, 2), leave.T, up, down.T, small, hidden.reshape(1, -1)]


def run_block(masters, keys, tokens, cotangent, key_tokens, ids, dp, tensor):
    key_entry, key_leave, key_up, key_down, key_small, key_hidden = keys
    rows, depth = masters[2].shape
    all_rows = tokens.shape[0]
    count = all_rows // tensor
    args = lay(*masters)
    args += [key_entry.transpose(1, 2, 0), key_leave, key_up, key_down, key_small]
    args.append(key_hidden)

    def all_of(shape):
        return pl.BlockSpec(shape, lambda i: (0,) * len(shape))

    anywhere = pl.BlockSpec(memory_space=pl.ANY)
    hidden = tensor * depth
    scratch = [
        ((count, depth), BF),
        ((count, depth), BF),
        ((count, depth), BF),
        ((count,), jnp.int32),
        ((rows, ATT), BF),
        ((rows, 2 * depth), BF),
        ((tensor, depth, ATT + 2 * depth), BF),
        ((tensor, depth, ATT), BF),
        ((tensor, depth, 2 * depth), BF),
        ((count, tensor * 3 * LANES), BF),
        ((count, tensor * 3 * LANES), BF),
        ((count, tensor * LANES), BF),
        ((count, tensor * LANES), BF),
        ((16, count), F32),
        ((count, depth), BF),
        ((count, depth), BF),
        ((count, depth), F32),
        ((count, depth), F32),
        ((count, hidden), BF),
        ((count, hidden), BF),
        ((count, depth), BF),
        ((depth + 16, count), BF),
        ((count, depth), BF),
        ((depth, count), BF),
        ((1, hidden), F32),
        ((8, depth), F32),
        ((8, depth), F32),
        ((count, depth), F32),
        ((count, LANES), F32),
        ((depth, count), BF),
        ((count, depth), BF),
        ((depth, count), BF),
        ((count, tensor * 3 * LANES), BF),
        ((tensor, depth, 3 * LANES), BF),
        ((tensor, depth, LANES), BF),
        ((tensor, depth, 2 * depth), BF),
        ((count, depth), BF),
        ((count, depth), BF),
        ((count, depth), BF),
        ((tensor, 16, depth), F32),
        ((dp, 16, depth), F32),
        ((depth, LANES), F32),
    ]
    for wide in (3 * LANES, LANES, 2 * depth):
        scratch += [
            ((2, depth, wide), BF),
            ((2, 8, rows, wide), BF),
            ((2, 4, rows, wide), BF),
            ((2, 4, rows, wide), BF),
            ((2, 3, rows, wide), BF),
            ((2, rows, wide), BF),
            ((rows, wide), BF),
        ]
    outs = [
        ((all_rows, depth), BF),
        ((all_rows, depth), BF),
        ((all_rows, depth), BF),
        ((8, LANES), F32),
        ((rows, ATT), F32),
        ((rows, 2 * depth), F32),
        ((rows, LANES), F32),
    ]
    return pl.pallas_call(
        block_kernel,
        grid=(1,),
        in_specs=[all_of(item.shape) for item in args] + [anywhere] * 4,
        out_specs=[anywhere] * 3 + [all_of(shape) for shape, _ in outs[3:]],
        scratch_shapes=[VMEM(shape, kind) for shape, kind in scratch]
        + [
            pltpu.SemaphoreType.DMA((SENDS,)),
            pltpu.SemaphoreType.DMA((SENDS,)),
            pltpu.SemaphoreType.DMA((12,)),
        ],
        out_shape=[jax.ShapeDtypeStruct(shape, kind) for shape, kind in outs],
        compiler_params=pltpu.CompilerParams(
            collective_id=1, has_side_effects=True, vmem_limit_bytes=63 * 2**20
        ),
        name="block_forward_and_backward",
    )(*args, tokens, cotangent, key_tokens, ids)


def step_kernel(*refs):
    held, load_sem, store_sem, state_sem = refs[47:51]
    states = refs[51:]
    chunks, rows = held.shape[0] // 3, held.shape[1]
    loads, stores = [], []
    for k in range(3):
        for c in range(chunks):
            n, part = k * chunks + c, pl.ds(c * rows, rows)
            loads.append(pltpu.make_async_copy(refs[k].at[part], held.at[n], load_sem.at[n]))
            stores.append(pltpu.make_async_copy(held.at[n], refs[25 + k].at[part], store_sem.at[n]))
    inputs = [
        pltpu.make_async_copy(src, dst, state_sem.at[k])
        for k, (src, dst) in enumerate(zip(refs[3:25], states))
    ]
    first = loads[:chunks]
    for copy in first + inputs + loads[chunks:]:
        copy.start()
    for load, store in zip(first, stores):
        load.wait()
        store.start()
    for copy in inputs:
        copy.wait()
    step_states(*states, *refs[28:47])
    for load, store in zip(loads[chunks:], stores[chunks:]):
        load.wait()
        store.start()
    for copy in stores:
        copy.wait()


def step_states(norm_ref, ga_ref, gb_ref, gs_ref, *refs):
    masters, firsts, seconds = refs[0:6], refs[6:12], refs[12:18]
    value_ref, outs = refs[18], refs[19:]
    norm_value = norm_ref[0:1, 0:1]
    value_ref[...] = norm_value
    factor = CLIP / jnp.maximum(norm_value, CLIP)
    grad_a = ga_ref[...] * factor
    grad_b = gb_ref[...] * factor
    depth = grad_b.shape[1] // 2

    def update(k, at, grad):
        new = adamw(grad, firsts[k][at], seconds[k][at], masters[k][at], DECAYS[k], RATES[k])
        for j in range(3):
            outs[3 * k + j][at] = new[j]

    for j in range(3):
        update(0, j, grad_a[:, j * LANES : j * LANES + USED])
    update(1, slice(None), grad_a[:, 3 * LANES : 3 * LANES + USED])
    update(2, slice(None), grad_b[:, :depth])
    update(3, slice(None), grad_b[:, depth:])
    update(4, slice(None), (gs_ref[...] * factor).T[0:6])
    update(5, slice(None), grad_a[:, :LANES].T[HIDDEN_AT : HIDDEN_AT + 1])


def run_step(large, norm_tile, grad_a, grad_b, grad_s, masters, firsts, seconds):
    state = lay(*masters) + lay(*firsts) + lay(*seconds)
    shapes = [jax.ShapeDtypeStruct((1, 1), F32)]
    for item in state[:6]:
        shapes.extend([jax.ShapeDtypeStruct(item.shape, F32)] * 3)
    args = [norm_tile, grad_a, grad_b, grad_s] + state

    def all_of(shape):
        return pl.BlockSpec(shape, lambda i: (0,) * len(shape))

    rows, depth = large[0].shape
    anywhere = pl.BlockSpec(memory_space=pl.ANY)
    result = pl.pallas_call(
        step_kernel,
        grid=(1,),
        in_specs=[anywhere] * (3 + len(args)),
        out_specs=[anywhere] * 3 + [all_of(item.shape) for item in shapes],
        out_shape=[jax.ShapeDtypeStruct(item.shape, item.dtype) for item in large] + shapes,
        scratch_shapes=[
            VMEM((12, rows // 4, depth), BF),
            pltpu.SemaphoreType.DMA((12,)),
            pltpu.SemaphoreType.DMA((12,)),
            pltpu.SemaphoreType.DMA((len(args),)),
        ]
        + [VMEM(item.shape, item.dtype) for item in args],
        compiler_params=pltpu.CompilerParams(vmem_limit_bytes=63 * 2**20),
        name="optimizer_step",
    )(*large, *args)
    large, result = result[:3], result[3:]
    outs = list(result[1:])
    for k in range(3):
        outs[k] = outs[k].transpose(1, 0, 2)
        outs[3 + k] = outs[3 + k].T
        outs[9 + k] = outs[9 + k].T
        outs[15 + k] = outs[15 + k].reshape(-1)
    return (large, result[0].reshape(()), outs)


def on_device(*args):
    tokens, crop_ids, cotangent, key_tokens = args[:4]
    masters, firsts, seconds, keys = args[4:10], args[10:16], args[16:22], args[22:28]
    count, groups = lax.axis_size("dp"), lax.axis_size("tensor")
    if count == 8 and groups == 4:
        result = run_block(masters, keys, tokens, cotangent, key_tokens, crop_ids, count, groups)
        large, norm_value, outs = run_step(result[:3], *result[3:], masters, firsts, seconds)
        return (*large, norm_value, *outs)
    ids = crop_ids.reshape(-1, 1, PACK)
    rows = tokens.shape[0] // groups
    place = lax.axis_index("tensor").astype(jnp.int32)[None]
    key_weights = lax.all_gather(pack_piece(*keys), "tensor", axis=0)
    weights = lax.all_gather(pack_piece(*masters), "dp", axis=0, tiled=True)
    weights = lax.all_gather(weights, "tensor", axis=0)

    def spread(own):
        return lax.all_gather(own, "tensor", axis=0, tiled=True)

    key_out = spread(run_key(place, key_tokens, ids, key_weights, rows))
    forward = run_query(place, tokens, cotangent, ids, weights, rows)
    block_out = spread(forward[0])
    qkv, a, lse, h1, dx1, grad_ffn, lines, hidden = forward[1:]
    grad_rows, grad_att = run_back(
        place, tokens, ids, weights, (qkv, a, lse, h1, dx1, lines, hidden), rows
    )
    input_grad = spread(grad_rows)
    norm_value, outs = finish_plain(grad_att, grad_ffn, masters, firsts, seconds)
    return (block_out, key_out, input_grad, norm_value, *outs)


def solution(mesh):
    rows, line = P("dp", None), P("dp")
    entry, leave, up, down = P("dp", None, "tensor"), P("tensor", "dp"), P("dp", "tensor"), P("tensor", "dp")
    state = (entry, leave, up, down, P(None, "dp"), P(("tensor", "dp")))
    keys = (P(None, None, "tensor"), P("tensor", None), P(None, "tensor"), P("tensor", None), P(), P("tensor"))
    outs = tuple(spec for spec in state for _ in range(3))
    return jax.shard_map(
        on_device,
        mesh=mesh,
        in_specs=(rows, line, rows, rows) + state * 3 + keys,
        out_specs=(rows, rows, rows, P()) + outs,
        check_vma=False,
    )
```
